32 devices in a mesh: section: 2 (over core), dp: 4 (over z), seq: 4 (over y, x).
Axes of the slice: x: 2, y: 2, z: 4, core: 2. Of those that a mesh axis runs over, the one named last changes fastest.
Arguments:
- enc_states: bfloat16 [8, 512, 4096], P(('section', 'dp'), 'seq'), may hold values from -6 to 6
- enc_gain: float32 [4096], replicated, may hold values from 0.1 to 1.9
- key_weight: bfloat16 [4096, 4096], P(None, 'seq'), may hold values from -0.09375 to 0.09375
- value_weight: bfloat16 [4096, 4096], P(None, 'seq'), may hold values from -0.09375 to 0.09375
- queries: bfloat16 [8, 512, 4096], P(('section', 'dp'), None, 'seq'), may hold values from -28 to 28
- out_grad: bfloat16 [8, 512, 4096], P(('section', 'dp'), None, 'seq'), may hold values from -6 to 6
- lengths: int32 [8], replicated, may hold values from 256 to 512, as said below
Outputs:
- attended: bfloat16 [8, 512, 4096], P(('section', 'dp'), None, 'seq')
- enc_grad: bfloat16 [8, 512, 4096], P(('section', 'dp'), 'seq')
- key_grad: float32 [4096, 4096], P(('section', 'dp'), 'seq')
- value_grad: float32 [4096, 4096], P(('section', 'dp'), 'seq')
- query_grad: bfloat16 [8, 512, 4096], P(('section', 'dp'), None, 'seq')
The draws below stay inside these ranges and needn't reach their ends.
Inputs may be any that keep to these rules, and one draw needn't show every extreme that they name: `lengths`: positions at or beyond a sequence's length are padding; at least one sequence in every draw has length 512.
All inputs are finite; a program needn't handle non-finite values.
Results may differ from the reference program's by a relative error of at most 0.023.
The reference program's roundings to bfloat16 on the way (of `normed`, `prob_weights`, `grad_scores` and `row_grad`) count: a program that leaves them out, or rounds other values in their place, can miss the bound.
Values may be sent and summed in bfloat16 or wider, within the bound.
No kernel may reach another device: no remote copies, remote signals or barrier semaphores. Data moves between devices by JAX's collectives and lax.ppermute only.
A program may use at most 128 MiB of HBM per device.

```python
import jax
import jax.numpy as jnp
from jax import lax

D = 4096
HEADS = 16
HD = 256
TGT = 512
SRC = 512
HEADS_DEV = 4
BATCH = 8


def draw_queries(key, part):
    key = jax.random.fold_in(key, 7)
    first = jax.random.fold_in(key, 0)
    shape = (BATCH, TGT, HEADS * HD)
    base = jnp.clip(jax.random.normal(first, shape, jnp.float32), -6.0, 6.0)
    return base.astype(jnp.bfloat16)


def draw_lengths(key, part):
    key = jax.random.fold_in(key, 5)
    first, second = jax.random.split(key)
    drawn = jax.random.randint(first, (BATCH,), SRC // 2, SRC + 1)
    chosen = jax.random.randint(second, (), 0, BATCH)
    return jnp.where(jnp.arange(BATCH) == chosen, SRC, drawn).astype(jnp.int32)


def block_scale(stream_key, dims, cuts, smallest, high):
    def one(dim, shards_of):
        steps = jax.random.uniform(jax.random.fold_in(jax.random.fold_in(stream_key, 6), dim), (shards_of,), jnp.float32, smallest / len(cuts), high / len(cuts))
        return jnp.repeat(jnp.exp(steps), dims[dim] // shards_of).reshape((-1,) + (1,) * (len(dims) - dim - 1))

    level = one(*cuts[0])
    for cut in cuts[1:]:
        level = level * one(*cut)
    return level


def centred(key, extent, deviation, bound, cuts=(), kind=jnp.bfloat16):
    factor_of = block_scale(key, extent, cuts, -0.22, 0.18) if cuts else 1.0
    entries = jax.random.normal(key, extent, jnp.float32) * deviation * factor_of
    return jnp.minimum(jnp.maximum(entries, -bound), bound).astype(kind)


def setup_inputs(seed: int = 0) -> dict:
    key_of = jax.random.split(jax.random.key(seed), 8)
    return {
        "enc_states": centred(key_of[0], (BATCH, SRC, D), 1.0, 6.0, ((0, 8), (1, 4))),
        "enc_gain": jnp.clip(1.0 + 0.18 * jax.random.normal(key_of[1], (D,), jnp.float32), 0.1, 1.9),
        "key_weight": centred(key_of[2], (D, HEADS * HD), D ** -0.5, 0.09375, ((1, 4),)),
        "value_weight": centred(key_of[3], (D, HEADS * HD), D ** -0.5, 0.09375, ((1, 4),)),
        "queries": draw_queries(jax.random.fold_in(key_of[7], 71), 0),
        "out_grad": centred(key_of[5], (BATCH, TGT, HEADS * HD), 1.0, 6.0, ((0, 8), (2, 4))),
        "lengths": draw_lengths(jax.random.fold_in(key_of[7], 71), 0),
    }


EPS = 1e-06
NEG_FILL = -1e+30

def normalize(enc_rows, gain):
    wide_rows = enc_rows.astype(jnp.float32)
    factor = lax.rsqrt(lax.optimization_barrier(jnp.mean(wide_rows * wide_rows, axis=-1, keepdims=True)) + EPS)
    return ((wide_rows * factor * gain).astype(jnp.bfloat16), factor)

def norm_backward(enc_rows, factor, gain, row_grad):
    wide_rows = enc_rows.astype(jnp.float32)
    scaled = row_grad.astype(jnp.float32) * gain
    inner_sum = lax.optimization_barrier(jnp.mean(scaled * wide_rows, axis=-1, keepdims=True))
    return (factor * scaled - wide_rows * factor * factor * factor * inner_sum).astype(jnp.bfloat16)

def attend(query_rows, key_rows, value_rows, upstream, visible):
    score_scale = HD ** (-0.5)
    query_wide = query_rows.astype(jnp.float32)
    key_wide = key_rows.astype(jnp.float32)
    value_wide = value_rows.astype(jnp.float32)
    upstream_wide = upstream.astype(jnp.float32)
    scores = jnp.einsum('thd,shd->hts', query_wide, key_wide) * score_scale
    scores = jnp.where(visible[None, None, :], scores, NEG_FILL)
    row_max = lax.optimization_barrier(jnp.max(scores, axis=-1, keepdims=True))
    exponent = jnp.exp(scores - row_max)
    probability = exponent / lax.optimization_barrier(jnp.sum(exponent, axis=-1, keepdims=True))
    prob_weights = probability.astype(jnp.bfloat16).astype(jnp.float32)
    attended = jnp.einsum('hts,shd->thd', prob_weights, value_wide).astype(jnp.bfloat16)
    grad_probs = jnp.einsum('thd,shd->hts', upstream_wide, value_wide)
    inner_sum = lax.optimization_barrier(jnp.sum(probability * grad_probs, axis=-1, keepdims=True))
    grad_scores = (probability * (grad_probs - inner_sum) * score_scale).astype(jnp.bfloat16).astype(jnp.float32)
    query_grad = jnp.einsum('hts,shd->thd', grad_scores, key_wide).astype(jnp.bfloat16)
    key_grad = jnp.einsum('hts,thd->shd', grad_scores, query_wide).astype(jnp.bfloat16)
    value_grad = jnp.einsum('hts,thd->shd', prob_weights, upstream_wide).astype(jnp.bfloat16)
    return (attended, query_grad, key_grad, value_grad)

def split_heads(block, count, group_count):
    return block.reshape(count, group_count, HEADS_DEV, HD).transpose(1, 0, 2, 3)

def merge_heads(block, count):
    return block.transpose(1, 0, 2, 3).reshape(count, HEADS * HD)

def reference(enc_states, enc_gain, key_weight, value_weight, queries, out_grad, lengths):
    group_count = HEADS // HEADS_DEV
    group_width = HEADS_DEV * HD
    positions = jnp.arange(SRC, dtype=jnp.int32)
    key_blocks = key_weight.reshape(D, group_count, group_width).transpose(1, 0, 2)
    value_blocks = value_weight.reshape(D, group_count, group_width).transpose(1, 0, 2)
    key_total = jnp.zeros((D, HEADS * HD), jnp.float32)
    value_total = jnp.zeros((D, HEADS * HD), jnp.float32)
    attended_list = []
    query_list = []
    grad_list = [None] * BATCH
    for target in range(BATCH):
        partner = (target + BATCH // 2) % BATCH
        normed, factor = normalize(enc_states[partner], enc_gain)
        key_rows = jnp.dot(normed, key_weight, preferred_element_type=jnp.float32).astype(jnp.bfloat16)
        value_rows = jnp.dot(normed, value_weight, preferred_element_type=jnp.float32).astype(jnp.bfloat16)
        visible = positions < lengths[partner]

        def per_group(pieces):
            return attend(pieces[0], pieces[1], pieces[2], pieces[3], visible)
        attended, query_grad, key_grad, value_grad = lax.map(per_group, (split_heads(queries[target], TGT, group_count), split_heads(key_rows, SRC, group_count), split_heads(value_rows, SRC, group_count), split_heads(out_grad[target], TGT, group_count)))
        attended_list.append(merge_heads(attended, TGT))
        query_list.append(merge_heads(query_grad, TGT))

        def add_group(row_total, pieces):
            key_piece, value_piece, key_block, value_block = pieces
            partial_value = jnp.dot(key_piece, key_block.T, preferred_element_type=jnp.float32)
            partial_value = partial_value + jnp.dot(value_piece, value_block.T, preferred_element_type=jnp.float32)
            rounded = lax.optimization_barrier(partial_value.astype(jnp.bfloat16))
            return (row_total + rounded.astype(jnp.float32), None)
        row_total, _ = lax.scan(add_group, jnp.zeros((SRC, D), jnp.float32), (key_grad.reshape(group_count, SRC, group_width), value_grad.reshape(group_count, SRC, group_width), key_blocks, value_blocks))
        row_grad = row_total.astype(jnp.bfloat16)
        grad_list[partner] = norm_backward(enc_states[partner], factor, enc_gain, row_grad)
        key_all = merge_heads(key_grad, SRC)
        value_all = merge_heads(value_grad, SRC)
        key_term = lax.optimization_barrier(jnp.dot(normed.T, key_all, preferred_element_type=jnp.float32).astype(jnp.bfloat16))
        value_term = lax.optimization_barrier(jnp.dot(normed.T, value_all, preferred_element_type=jnp.float32).astype(jnp.bfloat16))
        key_total = key_total + key_term.astype(jnp.float32)
        value_total = value_total + value_term.astype(jnp.float32)
    return (jnp.stack(attended_list), jnp.stack(grad_list), key_total, value_total, jnp.stack(query_list))
```

```python
import jax
import jax.numpy as jnp
from jax import lax
from jax.experimental import pallas as pl
from jax.experimental.pallas import tpu as pltpu
from jax.sharding import PartitionSpec as P

HD = 256


EPS = 1e-06
NEG_FILL = -1e30
BF16 = jnp.bfloat16
F32 = jnp.float32


def swap(value, axis, mask):
    pairs = [(source, source ^ mask) for source in range(lax.axis_size(axis))]
    return lax.ppermute(value, axis, pairs)


def normalize(enc_rows, gain):
    wide_rows = enc_rows.astype(F32)
    factor = lax.rsqrt(jnp.mean(wide_rows * wide_rows, axis=-1, keepdims=True) + EPS)
    return ((wide_rows * factor * gain).astype(BF16), factor)


def norm_backward(enc_rows, factor, gain, row_grad):
    wide_rows = enc_rows.astype(F32)
    scaled = row_grad.astype(F32) * gain
    inner_sum = jnp.mean(scaled * wide_rows, axis=-1, keepdims=True)
    return (factor * scaled - wide_rows * factor * factor * factor * inner_sum).astype(BF16)


def gather_blocks(own):
    count = lax.axis_size("seq")
    if count == 4:
        half = own.shape[0] // 2
        top, bottom = own[:half], own[half:]
        first_top, second_bottom = swap(top, "seq", 1), swap(bottom, "seq", 2)
        first_bottom, second_top = swap(bottom, "seq", 1), swap(top, "seq", 2)
        third_top, third_bottom = swap(first_top, "seq", 2), swap(second_bottom, "seq", 1)
        return [
            own,
            jnp.concatenate([first_top, first_bottom]),
            jnp.concatenate([second_top, second_bottom]),
            jnp.concatenate([third_top, third_bottom]),
        ]
    blocks = [own]
    bit = 1
    while bit < count:
        blocks = blocks + [swap(block, "seq", bit) for block in blocks]
        bit *= 2
    return blocks


def dot(left, right, left_dim, right_dim):
    return lax.dot_general(
        left, right, (((left_dim,), (right_dim,)), ((), ())), preferred_element_type=F32
    )


def attend_kernel(
    visible, query, key_early, key_late, value_early, value_late, upstream, attended, query_grad, kv_grad
):
    score_scale = HD ** (-0.5)
    query_rows, upstream_rows = query[...], upstream[...]
    key_rows = jnp.concatenate([key_early[...], key_late[...]], axis=0)
    value_rows = jnp.concatenate([value_early[...], value_late[...]], axis=0)
    scores = dot(key_rows, query_rows, 1, 1) * score_scale
    scores = jnp.where(visible[...] > 0, scores, NEG_FILL)
    exponent = jnp.exp(scores - jnp.max(scores, axis=0, keepdims=True))
    probability = exponent * (1.0 / jnp.sum(exponent, axis=0, keepdims=True))
    prob_weights = probability.astype(BF16)
    grad_probs = dot(value_rows, upstream_rows, 1, 1)
    inner_sum = jnp.sum(probability * grad_probs, axis=0, keepdims=True)
    grad_scores = (probability * (grad_probs - inner_sum) * score_scale).astype(BF16)
    kv_grad[:, :HD] = dot(grad_scores, query_rows, 1, 0).astype(BF16)
    kv_grad[:, HD:] = dot(prob_weights, upstream_rows, 1, 0).astype(BF16)
    attended[...] = dot(prob_weights, value_rows, 0, 0).astype(BF16)
    query_grad[...] = dot(grad_scores, key_rows, 0, 0).astype(BF16)


def attend_head(head, visible, query, key_early, key_late, value_early, value_late, upstream):
    src_rows, target_rows = visible.shape[0], query.shape[0]

    def column(rows):
        return pl.BlockSpec((rows, HD), lambda step: (0, head))

    def whole(rows, columns):
        return pl.BlockSpec((rows, columns), lambda step: (0, 0))

    early, late = key_early.shape[0], key_late.shape[0]
    return pl.pallas_call(
        attend_kernel,
        grid=(1,),
        in_specs=[
            whole(src_rows, 1),
            column(target_rows),
            column(early),
            column(late),
            column(early),
            column(late),
            column(target_rows),
        ],
        out_specs=[
            whole(target_rows, HD),
            whole(target_rows, HD),
            whole(src_rows, 2 * HD),
        ],
        out_shape=[
            jax.ShapeDtypeStruct((target_rows, HD), BF16),
            jax.ShapeDtypeStruct((target_rows, HD), BF16),
            jax.ShapeDtypeStruct((src_rows, 2 * HD), BF16),
        ],
        compiler_params=pltpu.CompilerParams(vmem_limit_bytes=48 * 1024 * 1024),
        cost_estimate=pl.CostEstimate(
            flops=12 * src_rows * target_rows * HD,
            bytes_accessed=2 * HD * (4 * target_rows + 4 * src_rows),
            transcendentals=src_rows * target_rows,
        ),
    )(visible, query, key_early, key_late, value_early, value_late, upstream)


def on_device(enc_states, enc_gain, key_weight, value_weight, queries, out_grad, lengths):
    enc_rows = enc_states[0]
    own_rows, width = enc_rows.shape
    heads_here = key_weight.shape[1] // HD
    section_count, dp_count, seq_count = (lax.axis_size(name) for name in ("section", "dp", "seq"))
    section, place, seq = (lax.axis_index(name) for name in ("section", "dp", "seq"))
    partner = (section * dp_count + place + dp_count) % (section_count * dp_count)
    src_rows = own_rows * seq_count
    section_width = width // section_count
    target_width = section_width // dp_count

    normed, factor = normalize(enc_rows, enc_gain)
    partner_rows = swap(normed, "section", 1)
    blocks = gather_blocks(partner_rows)
    quarter = seq_count // 4
    quarters = [
        blocks[step] if quarter == 1 else jnp.concatenate(blocks[step * quarter : (step + 1) * quarter])
        for step in range(4)
    ]
    block_start = (seq ^ jnp.arange(seq_count, dtype=jnp.int32)) * own_rows
    positions = block_start[:, None] + jnp.arange(own_rows, dtype=jnp.int32)[None, :]
    visible = (positions.reshape(src_rows, 1) < lengths[partner]).astype(jnp.int32)

    early, late = jnp.concatenate(quarters[:3]), quarters[3]
    key_early, value_early, key_late, value_late = (
        jnp.dot(rows, weight, preferred_element_type=F32).astype(BF16)
        for rows, weight in ((early, key_weight), (early, value_weight), (late, key_weight), (late, value_weight))
    )

    inward = [(0, 1), (3, 2)]
    outward = [(1, 0), (2, 3)]
    across = [(1, 2), (2, 1)]

    def features(rows, xor):
        start = (place ^ xor) * target_width
        return lax.dynamic_slice_in_dim(rows, start, target_width, axis=1)

    mine, theirs, far_mine, far_theirs = [], [], [], []
    for rows in quarters:
        here = lax.dynamic_slice_in_dim(rows, section * section_width, section_width, axis=1)
        away = lax.dynamic_slice_in_dim(rows, (1 - section) * section_width, section_width, axis=1)
        there = swap(away, "section", 1)
        mine.append(here)
        theirs.append(there)
        far = [
            jnp.concatenate([features(half, 3), features(half, 2)], axis=1) for half in (here, there)
        ]
        far = lax.ppermute(jnp.concatenate(far), "dp", inward)
        far_mine.append(far[: far.shape[0] // 2])
        far_theirs.append(far[far.shape[0] // 2 :])
    chip_rows = jnp.concatenate(mine + theirs)
    chip_features = [features(chip_rows, xor) for xor in range(4)]
    outer_far = jnp.concatenate(far_mine + far_theirs)
    outer_features = {2: outer_far[:, :target_width], 3: outer_far[:, target_width:]}
    outer_features[0] = lax.ppermute(chip_features[1], "dp", inward)

    attended, query_grad, kv_grads, sums = [], [], [], []
    for head in range(heads_here):
        head_attended, head_query_grad, kv_grad = attend_head(
            head, visible, queries[0], key_early, key_late, value_early, value_late, out_grad[0]
        )
        attended.append(head_attended)
        query_grad.append(head_query_grad)
        kv_grads.append(kv_grad)
        chip_grad = jnp.concatenate([kv_grad, swap(kv_grad, "section", 1)])
        outer_grad = lax.ppermute(kv_grad, "dp", inward)
        outer_grad = jnp.concatenate([outer_grad, swap(outer_grad, "section", 1)])

        def pair_sum(xor):
            return dot(chip_features[xor], chip_grad, 0, 0) + dot(outer_features[xor], outer_grad, 0, 0)

        to_outer = lax.ppermute(pair_sum(2).astype(BF16), "dp", across)
        to_inner = lax.ppermute(pair_sum(3).astype(BF16), "dp", across)
        relay = (dot(chip_features[1], chip_grad, 0, 0) + to_outer.astype(F32)).astype(BF16)
        relay = lax.ppermute(relay, "dp", outward)
        sums.append(pair_sum(0) + to_inner.astype(F32) + relay.astype(F32))

    key_rows_grad = jnp.concatenate([kv_grad[:, :HD] for kv_grad in kv_grads], axis=1)
    value_rows_grad = jnp.concatenate([kv_grad[:, HD:] for kv_grad in kv_grads], axis=1)
    row_term = (dot(key_rows_grad, key_weight, 1, 1) + dot(value_rows_grad, value_weight, 1, 1)).astype(BF16)
    row_share = row_term[:own_rows].astype(F32)
    for step in range(1, seq_count):
        row_share = row_share + swap(
            row_term[step * own_rows : (step + 1) * own_rows], "seq", step
        ).astype(F32)
    row_grad = swap(row_share.astype(BF16), "section", 1)
    enc_grad = norm_backward(enc_rows, factor, enc_gain, row_grad)
    return (
        jnp.concatenate(attended, axis=1)[None],
        enc_grad[None],
        jnp.concatenate([total[:, :HD] for total in sums], axis=1),
        jnp.concatenate([total[:, HD:] for total in sums], axis=1),
        jnp.concatenate(query_grad, axis=1)[None],
    )


def solution(mesh):
    placed = (
        P(("section", "dp"), "seq", None),
        P(),
        P(None, "seq"),
        P(None, "seq"),
        P(("section", "dp"), None, "seq"),
        P(("section", "dp"), None, "seq"),
        P(),
    )
    return jax.shard_map(
        on_device,
        mesh=mesh,
        in_specs=placed,
        out_specs=(
            P(("section", "dp"), None, "seq"),
            P(("section", "dp"), "seq", None),
            P(("section", "dp"), "seq"),
            P(("section", "dp"), "seq"),
            P(("section", "dp"), None, "seq"),
        ),
        check_vma=False,
    )
```

```python
import jax
import jax.numpy as jnp
from jax import lax
from jax.experimental import pallas as pl
from jax.experimental.pallas import tpu as pltpu
from jax.sharding import PartitionSpec as P

HD = 256


EPS = 1e-06
NEG_FILL = -1e30
BF16 = jnp.bfloat16
F32 = jnp.float32


def swap(value, axis, mask):
    pairs = [(source, source ^ mask) for source in range(lax.axis_size(axis))]
    return lax.ppermute(value, axis, pairs)


def normalize(enc_rows, gain):
    wide_rows = enc_rows.astype(F32)
    factor = lax.rsqrt(jnp.mean(wide_rows * wide_rows, axis=-1, keepdims=True) + EPS)
    return ((wide_rows * factor * gain).astype(BF16), factor)


def norm_backward(enc_rows, factor, gain, row_grad):
    wide_rows = enc_rows.astype(F32)
    scaled = row_grad.astype(F32) * gain
    inner_sum = jnp.mean(scaled * wide_rows, axis=-1, keepdims=True)
    return (factor * scaled - wide_rows * factor * factor * factor * inner_sum).astype(BF16)


def tie(*values):
    return lax.optimization_barrier(values)


def dot(left, right, left_dim, right_dim):
    return lax.dot_general(
        left, right, (((left_dim,), (right_dim,)), ((), ())), preferred_element_type=F32
    )


def attend_kernel(
    visible, query, key_early, key_late, value_early, value_late, upstream, attended, query_grad, kv_grad
):
    score_scale = HD ** (-0.5)
    query_rows, upstream_rows = query[...], upstream[...]
    key_rows = jnp.concatenate([key_early[...], key_late[...]], axis=0)
    value_rows = jnp.concatenate([value_early[...], value_late[...]], axis=0)
    scores = dot(key_rows, query_rows, 1, 1) * score_scale
    scores = jnp.where(visible[...] > 0, scores, NEG_FILL)
    exponent = jnp.exp(scores - jnp.max(scores, axis=0, keepdims=True))
    probability = exponent * (1.0 / jnp.sum(exponent, axis=0, keepdims=True))
    prob_weights = probability.astype(BF16)
    grad_probs = dot(value_rows, upstream_rows, 1, 1)
    inner_sum = jnp.sum(probability * grad_probs, axis=0, keepdims=True)
    grad_scores = (probability * (grad_probs - inner_sum) * score_scale).astype(BF16)
    kv_grad[0] = dot(grad_scores, query_rows, 1, 0).astype(BF16)
    kv_grad[1] = dot(prob_weights, upstream_rows, 1, 0).astype(BF16)
    attended[...] = dot(prob_weights, value_rows, 0, 0).astype(BF16)
    query_grad[...] = dot(grad_scores, key_rows, 0, 0).astype(BF16)


def attend_heads(first, count, visible, query, key_early, key_late, value_early, value_late, upstream):
    src_rows, target_rows = visible.shape[0], query.shape[0]

    def column(rows):
        return pl.BlockSpec((rows, HD), lambda step: (0, first + step))

    def out_column(rows):
        return pl.BlockSpec((rows, HD), lambda step: (0, step))

    early, late = key_early.shape[0], key_late.shape[0]
    return pl.pallas_call(
        attend_kernel,
        grid=(count,),
        in_specs=[
            pl.BlockSpec((src_rows, 1), lambda step: (0, 0)),
            column(target_rows),
            column(early),
            column(late),
            column(early),
            column(late),
            column(target_rows),
        ],
        out_specs=[
            out_column(target_rows),
            out_column(target_rows),
            pl.BlockSpec((2, src_rows, HD), lambda step: (0, 0, step)),
        ],
        out_shape=[
            jax.ShapeDtypeStruct((target_rows, count * HD), BF16),
            jax.ShapeDtypeStruct((target_rows, count * HD), BF16),
            jax.ShapeDtypeStruct((2, src_rows, count * HD), BF16),
        ],
        compiler_params=pltpu.CompilerParams(vmem_limit_bytes=48 * 1024 * 1024),
        cost_estimate=pl.CostEstimate(
            flops=12 * count * src_rows * target_rows * HD,
            bytes_accessed=2 * count * HD * (4 * target_rows + 4 * src_rows),
            transcendentals=count * src_rows * target_rows,
        ),
    )(visible, query, key_early, key_late, value_early, value_late, upstream)


def row_kernel(*refs):
    *grads, key_block, value_block, out = refs
    total = None
    width = grads[0].shape[1]
    for index, grad in enumerate(grads):
        weight = (key_block, value_block)[index % 2]
        start = (index // 2) * width
        term = dot(grad[...], weight[:, start : start + width], 1, 1)
        total = term if total is None else total + term
    out[...] = total.astype(BF16)


def row_product(grads, key_weight, value_weight):
    rows, columns = grads[0].shape
    features, heads_width = key_weight.shape
    block = 512
    whole = pl.BlockSpec((rows, columns), lambda step: (0, 0))
    weight = pl.BlockSpec((block, heads_width), lambda step: (step, 0))
    return pl.pallas_call(
        row_kernel,
        grid=(features // block,),
        in_specs=[whole] * len(grads) + [weight, weight],
        out_specs=pl.BlockSpec((rows, block), lambda step: (0, step)),
        out_shape=jax.ShapeDtypeStruct((rows, features), BF16),
        compiler_params=pltpu.CompilerParams(vmem_limit_bytes=40 * 1024 * 1024),
        cost_estimate=pl.CostEstimate(
            flops=4 * rows * features * heads_width,
            bytes_accessed=4 * features * heads_width + 2 * rows * (features + 2 * heads_width),
            transcendentals=0,
        ),
    )(*grads, key_weight, value_weight)


def add_kernel(*refs):
    local, first, second, out = refs[0], refs[1], refs[2], refs[-1]
    out[...] = local[...] + first[...].astype(F32) + second[...].astype(F32)


def add_columns(total, position, count, local, first, second):
    rows, columns = local.shape
    here = pl.BlockSpec((rows, columns), lambda step: (0, 0))
    terms = [local, first, second]
    kept = [] if total is None else [total]
    return pl.pallas_call(
        add_kernel,
        grid=(1,),
        in_specs=[here] * 3 + [pl.BlockSpec(memory_space=pl.ANY)] * len(kept),
        out_specs=pl.BlockSpec((rows, columns), lambda step: (0, position)),
        out_shape=jax.ShapeDtypeStruct((rows, count * columns), F32),
        input_output_aliases={3: 0} if kept else {},
        cost_estimate=pl.CostEstimate(
            flops=2 * rows * columns, bytes_accessed=12 * rows * columns, transcendentals=0
        ),
        compiler_params=pltpu.CompilerParams(vmem_limit_bytes=32 * 1024 * 1024),
    )(*terms, *kept)


def on_device(enc_states, enc_gain, key_weight, value_weight, queries, out_grad, lengths):
    enc_rows = enc_states[0]
    own_rows, width = enc_rows.shape
    heads_here = key_weight.shape[1] // HD
    section_count, dp_count, seq_count = (lax.axis_size(name) for name in ("section", "dp", "seq"))
    section, place, seq = (lax.axis_index(name) for name in ("section", "dp", "seq"))
    partner = (section * dp_count + place + dp_count) % (section_count * dp_count)
    src_rows = own_rows * seq_count
    section_width = width // section_count
    target_width = section_width // dp_count
    inward = [(0, 1), (3, 2)]
    outward = [(1, 0), (2, 3)]
    across = [(1, 2), (2, 1)]

    def section_features(rows, index):
        return lax.dynamic_slice_in_dim(rows, index * section_width, section_width, axis=1)

    def target_features(rows, xors, base=0):
        return jnp.concatenate(
            [
                lax.dynamic_slice_in_dim(rows, base + (place ^ xor) * target_width, target_width, axis=1)
                for xor in xors
            ],
            axis=1,
        )

    normed, factor = normalize(enc_rows, enc_gain)
    partner_rows = swap(normed, "section", 1)

    if seq_count == 4:
        half = own_rows // 2
        first, second = swap(partner_rows, "seq", 1), swap(partner_rows, "seq", 2)
    else:
        quarter = seq_count // 4
        blocks = [partner_rows]
        bit = 1
        while bit < quarter:
            blocks = blocks + [swap(block, "seq", bit) for block in blocks]
            bit *= 2
        partner_rows = jnp.concatenate(blocks)
        first, second = swap(partner_rows, "seq", quarter), swap(partner_rows, "seq", 2 * quarter)
        half = partner_rows.shape[0] // 2
        blocks = [normed]
        bit = 1
        while bit < quarter:
            blocks = blocks + [swap(block, "seq", bit) for block in blocks]
            bit *= 2
        normed = jnp.concatenate(blocks)
    low, high = max(seq_count // 4, 1), max(seq_count // 2, 1)

    base = section * section_width
    outer_far = jnp.concatenate(
        [target_features(rows, (3, 2), base) for rows in (partner_rows, normed)]
    )
    outer_own = jnp.concatenate([target_features(rows, (1,), base) for rows in (partner_rows, normed)])
    outer_far = lax.ppermute(outer_far, "dp", inward)
    outer_own = lax.ppermute(outer_own, "dp", inward)
    first, second, outer_far, outer_own = tie(first, second, outer_far, outer_own)

    third_top, third_bottom = swap(first[:half], "seq", high), swap(second[half:], "seq", low)
    early = jnp.concatenate([partner_rows, first, second])
    key_early = jnp.dot(early, key_weight, preferred_element_type=F32).astype(BF16)
    value_early = jnp.dot(early, value_weight, preferred_element_type=F32).astype(BF16)
    away_early = swap(section_features(early[2 * half :], 1 - section), "section", 1)

    key_early, value_early, away_early, third_top, third_bottom, outer_far, outer_own = tie(
        key_early, value_early, away_early, third_top, third_bottom, outer_far, outer_own
    )
    outer_first, outer_second = swap(outer_far, "seq", low), swap(outer_far, "seq", high)
    late = jnp.concatenate([third_top, third_bottom])
    key_late = jnp.dot(late, key_weight, preferred_element_type=F32).astype(BF16)
    value_late = jnp.dot(late, value_weight, preferred_element_type=F32).astype(BF16)
    away_late = swap(section_features(late, 1 - section), "section", 1)

    block_start = (seq ^ jnp.arange(seq_count, dtype=jnp.int32)) * own_rows
    positions = block_start[:, None] + jnp.arange(own_rows, dtype=jnp.int32)[None, :]
    visible = (positions.reshape(src_rows, 1) < lengths[partner]).astype(jnp.int32)

    part_heads = max(heads_here // 2, 1)
    parts = heads_here // part_heads
    attended, query_grad, kv_grads = zip(
        *(
            attend_heads(
                part * part_heads,
                part_heads,
                visible,
                queries[0],
                key_early,
                key_late,
                value_early,
                value_late,
                out_grad[0],
            )
            for part in range(parts)
        )
    )
    mine = [kv_grad[kind] for kv_grad in kv_grads for kind in (0, 1)]
    chunk_count = len(mine)
    mine[0], mine[1] = tie(mine[0], mine[1])
    outer_next = lax.ppermute(mine[0], "dp", inward)
    theirs = list(swap(jnp.stack(mine[:2]), "section", 1))
    outer_first, outer_second, away_late, mine[-2], mine[-1] = tie(
        outer_first, outer_second, away_late, mine[-2], mine[-1]
    )
    quarter_rows = outer_far.shape[0] // 2
    outer_third_top = swap(outer_first[:quarter_rows], "seq", high)
    outer_third_bottom = swap(outer_second[quarter_rows:], "seq", low)

    chip_rows = jnp.concatenate(
        [section_features(early, section), section_features(late, section)]
        + [section_features(normed, section), away_early, away_late]
    )
    chip_far = target_features(chip_rows, (2, 3))
    chip_pair = target_features(chip_rows, (1,))
    chip_own = target_features(chip_rows, (0,))

    def in_order(own, one, two, top, bottom):
        pieces = [own, one, two]
        return jnp.concatenate(
            [piece[:quarter_rows] for piece in pieces]
            + [top]
            + [piece[quarter_rows:] for piece in pieces]
            + [bottom]
        )

    crossed, local, relayed = [], [], []
    row_parts = []

    def send_rows(start, stop):
        for step in range(start, stop):
            rows = row_term[step * own_rows : (step + 1) * own_rows]
            row_parts.append(swap(rows, "seq", step))

    for index in range(chunk_count):
        if index == 0:
            outer_next, outer_third_top, outer_third_bottom = tie(
                outer_next, outer_third_top, outer_third_bottom
            )
            outer_far = in_order(outer_far, outer_first, outer_second, outer_third_top, outer_third_bottom)
        chip_grad = jnp.concatenate([mine[index], theirs[index]])
        outer_grad = jnp.concatenate([outer_next, swap(outer_next, "section", 1)])
        far = (dot(chip_far, chip_grad, 0, 0) + dot(outer_far, outer_grad, 0, 0)).astype(BF16)
        if index >= 2:
            far, row_term, crossed[index - 2], *relayed[index - 2 :] = tie(
                far, row_term, crossed[index - 2], *relayed[index - 2 :]
            )
        if index == 0 and parts == 2:
            far, mine[1], mine[2], mine[3], outer_own, chip_grad, outer_grad = tie(
                far, mine[1], mine[2], mine[3], outer_own, chip_grad, outer_grad
            )
            theirs = theirs + list(swap(jnp.stack(mine[2:]), "section", 1))
        elif index == 0:
            far, mine[1], outer_own, chip_grad, outer_grad = tie(
                far, mine[1], outer_own, chip_grad, outer_grad
            )
        elif index == 1:
            far, *both = tie(far, *mine, *theirs)
            mine, theirs = both[:chunk_count], both[chunk_count:]
        elif index + 1 < chunk_count:
            far, mine[index + 1] = tie(far, mine[index + 1])
        if index < chunk_count - 1:
            crossed.append(lax.ppermute(far, "dp", across))
            outer_next = lax.ppermute(mine[index + 1], "dp", inward)
        else:
            to_outer = lax.ppermute(far[:target_width], "dp", across)
            crossed.append((to_outer, lax.ppermute(far[target_width:], "dp", across)))
        if index == 0:
            own_first, own_second = swap(outer_own, "seq", low), swap(outer_own, "seq", high)
            own_third_top = swap(own_first[:quarter_rows], "seq", high)
            own_third_bottom = swap(own_second[quarter_rows:], "seq", low)
            outer_own = in_order(outer_own, own_first, own_second, own_third_top, own_third_bottom)
        if index == 1:
            row_term = row_product(mine, key_weight, value_weight)
        if index >= 2:
            send_rows(1 if index == 2 else 3, 3 if index == 2 else seq_count)
        local.append(dot(chip_own, chip_grad, 0, 0) + dot(outer_own, outer_grad, 0, 0))
        relayed.append(dot(chip_pair, chip_grad, 0, 0))

    def relay(terms):
        return lax.ppermute(jnp.stack([term.astype(BF16) for term in terms]), "dp", outward)

    totals = [None, None]
    outward_terms, inner_terms = [], []
    for index in range(chunk_count):
        if index < chunk_count - 1:
            to_outer, to_inner = crossed[index][:target_width], crossed[index][target_width:]
        else:
            to_outer, to_inner = crossed[index]
        outward_terms.append(relayed[index] + to_outer.astype(F32))
        inner_terms.append(to_inner)
    groups = [(0, 1), (2,), (3,)] if chunk_count == 4 else [(0,), (1,)]
    for group in groups:
        from_inner = relay([outward_terms[index] for index in group])
        for slot, index in enumerate(group):
            totals[index % 2] = add_columns(
                totals[index % 2], index // 2, parts, local[index], inner_terms[index], from_inner[slot]
            )
    if chunk_count == 2:
        send_rows(1, seq_count)

    row_share = row_term[:own_rows].astype(F32)
    for row_part in row_parts:
        row_share = row_share + row_part.astype(F32)
    row_grad = swap(row_share.astype(BF16), "section", 1)
    enc_grad = norm_backward(enc_rows, factor, enc_gain, row_grad)
    return (
        jnp.concatenate(attended, axis=1)[None],
        enc_grad[None],
        totals[0],
        totals[1],
        jnp.concatenate(query_grad, axis=1)[None],
    )


def solution(mesh):
    placed = (
        P(("section", "dp"), "seq", None),
        P(),
        P(None, "seq"),
        P(None, "seq"),
        P(("section", "dp"), None, "seq"),
        P(("section", "dp"), None, "seq"),
        P(),
    )
    return jax.shard_map(
        on_device,
        mesh=mesh,
        in_specs=placed,
        out_specs=(
            P(("section", "dp"), None, "seq"),
            P(("section", "dp"), "seq", None),
            P(("section", "dp"), "seq"),
            P(("section", "dp"), "seq"),
            P(("section", "dp"), None, "seq"),
        ),
        check_vma=False,
    )
```

```python
import functools

import jax
import jax.numpy as jnp
from jax import lax
from jax.experimental import pallas as pl
from jax.experimental.pallas import tpu as pltpu
from jax.sharding import PartitionSpec as P

HD = 256


EPS = 1e-06
NEG_FILL = -1e30
BF16 = jnp.bfloat16
F32 = jnp.float32


def swap(value, axis, mask):
    pairs = [(source, source ^ mask) for source in range(lax.axis_size(axis))]
    return lax.ppermute(value, axis, pairs)


def normalize(enc_rows, gain):
    wide_rows = enc_rows.astype(F32)
    factor = lax.rsqrt(jnp.mean(wide_rows * wide_rows, axis=-1, keepdims=True) + EPS)
    return ((wide_rows * factor * gain).astype(BF16), factor)


def norm_backward(enc_rows, factor, gain, row_grad):
    wide_rows = enc_rows.astype(F32)
    scaled = row_grad.astype(F32) * gain
    inner_sum = jnp.mean(scaled * wide_rows, axis=-1, keepdims=True)
    return (factor * scaled - wide_rows * factor * factor * factor * inner_sum).astype(BF16)


def tie(*values):
    return lax.optimization_barrier(values)


def dot(left, right, left_dim, right_dim):
    return lax.dot_general(
        left, right, (((left_dim,), (right_dim,)), ((), ())), preferred_element_type=F32
    )


def attend_kernel(
    visible, query, key_early, key_late, value_early, value_late, upstream, attended, query_grad, kv_grad
):
    score_scale = HD ** (-0.5)
    query_rows, upstream_rows = query[...], upstream[...]
    key_rows = jnp.concatenate([key_early[...], key_late[...]], axis=0)
    value_rows = jnp.concatenate([value_early[...], value_late[...]], axis=0)
    scores = dot(key_rows, query_rows, 1, 1) * score_scale
    scores = jnp.where(visible[...] > 0, scores, NEG_FILL)
    exponent = jnp.exp(scores - jnp.max(scores, axis=0, keepdims=True))
    probability = exponent * (1.0 / jnp.sum(exponent, axis=0, keepdims=True))
    prob_weights = probability.astype(BF16)
    grad_probs = dot(value_rows, upstream_rows, 1, 1)
    inner_sum = jnp.sum(probability * grad_probs, axis=0, keepdims=True)
    grad_scores = (probability * (grad_probs - inner_sum) * score_scale).astype(BF16)
    kv_grad[:, :HD] = dot(grad_scores, query_rows, 1, 0).astype(BF16)
    kv_grad[:, HD:] = dot(prob_weights, upstream_rows, 1, 0).astype(BF16)
    attended[...] = dot(prob_weights, value_rows, 0, 0).astype(BF16)
    query_grad[...] = dot(grad_scores, key_rows, 0, 0).astype(BF16)


def attend_head(head, visible, query, key_early, key_late, value_early, value_late, upstream):
    src_rows, target_rows = visible.shape[0], query.shape[0]
    early, late = key_early.shape[0], key_late.shape[0]

    def column(rows):
        return pl.BlockSpec((rows, HD), lambda step: (0, head))

    def whole(rows, columns):
        return pl.BlockSpec((rows, columns), lambda step: (0, 0))

    return pl.pallas_call(
        attend_kernel,
        grid=(1,),
        in_specs=[
            whole(src_rows, 1),
            column(target_rows),
            column(early),
            column(late),
            column(early),
            column(late),
            column(target_rows),
        ],
        out_specs=[whole(target_rows, HD), whole(target_rows, HD), whole(src_rows, 2 * HD)],
        out_shape=[
            jax.ShapeDtypeStruct((target_rows, HD), BF16),
            jax.ShapeDtypeStruct((target_rows, HD), BF16),
            jax.ShapeDtypeStruct((src_rows, 2 * HD), BF16),
        ],
        compiler_params=pltpu.CompilerParams(vmem_limit_bytes=48 * 1024 * 1024),
        cost_estimate=pl.CostEstimate(
            flops=12 * src_rows * target_rows * HD,
            bytes_accessed=2 * HD * (4 * target_rows + 4 * src_rows),
            transcendentals=src_rows * target_rows,
        ),
    )(visible, query, key_early, key_late, value_early, value_late, upstream)


def row_kernel(*refs):
    *grads, key_block, value_block, out = refs
    key_grads = jnp.concatenate([grad[:, :HD] for grad in grads], axis=1)
    value_grads = jnp.concatenate([grad[:, HD:] for grad in grads], axis=1)
    out[...] = (dot(key_grads, key_block[...], 1, 1) + dot(value_grads, value_block[...], 1, 1)).astype(BF16)


def row_product(grads, key_weight, value_weight):
    rows, columns = grads[0].shape
    features, heads_width = key_weight.shape
    block = 512
    whole = pl.BlockSpec((rows, columns), lambda step: (0, 0))
    weight = pl.BlockSpec((block, heads_width), lambda step: (step, 0))
    return pl.pallas_call(
        row_kernel,
        grid=(features // block,),
        in_specs=[whole] * len(grads) + [weight, weight],
        out_specs=pl.BlockSpec((rows, block), lambda step: (0, step)),
        out_shape=jax.ShapeDtypeStruct((rows, features), BF16),
        compiler_params=pltpu.CompilerParams(vmem_limit_bytes=40 * 1024 * 1024),
        cost_estimate=pl.CostEstimate(
            flops=4 * rows * features * heads_width,
            bytes_accessed=4 * features * heads_width + 2 * rows * (features + 2 * heads_width),
            transcendentals=0,
        ),
    )(*grads, key_weight, value_weight)


def add_kernel(kind_count, local, first, second, *refs):
    outs = refs[-kind_count:]
    total = local[...] + first[...].astype(F32) + second[...].astype(F32)
    for slot, out in enumerate(outs):
        out[...] = total[:, slot * HD : (slot + 1) * HD]


def add_columns(totals, head, heads_here, local, first, second):
    rows, columns = local.shape
    here = pl.BlockSpec((rows, columns), lambda step: (0, 0))
    kept = [total for total in totals if total is not None]
    count = columns // HD
    return pl.pallas_call(
        functools.partial(add_kernel, count),
        grid=(1,),
        in_specs=[here] * 3 + [pl.BlockSpec(memory_space=pl.ANY)] * len(kept),
        out_specs=[pl.BlockSpec((rows, HD), lambda step: (0, head))] * count,
        out_shape=[jax.ShapeDtypeStruct((rows, heads_here * HD), F32)] * count,
        input_output_aliases={3 + slot: slot for slot in range(len(kept))},
        cost_estimate=pl.CostEstimate(
            flops=2 * rows * columns, bytes_accessed=12 * rows * columns, transcendentals=0
        ),
        compiler_params=pltpu.CompilerParams(vmem_limit_bytes=32 * 1024 * 1024),
    )(local, first, second, *kept)


def on_device(enc_states, enc_gain, key_weight, value_weight, queries, out_grad, lengths):
    enc_rows = enc_states[0]
    own_rows, width = enc_rows.shape
    heads_here = key_weight.shape[1] // HD
    section_count, dp_count, seq_count = (lax.axis_size(name) for name in ("section", "dp", "seq"))
    section, place, seq = (lax.axis_index(name) for name in ("section", "dp", "seq"))
    partner = (section * dp_count + place + dp_count) % (section_count * dp_count)
    src_rows = own_rows * seq_count
    section_width = width // section_count
    target_width = section_width // dp_count
    inward = [(0, 1), (3, 2)]
    outward = [(1, 0), (2, 3)]
    across = [(1, 2), (2, 1)]

    def section_features(rows, index):
        return lax.dynamic_slice_in_dim(rows, index * section_width, section_width, axis=1)

    def target_features(rows, xors, base=0):
        return jnp.concatenate(
            [
                lax.dynamic_slice_in_dim(rows, base + (place ^ xor) * target_width, target_width, axis=1)
                for xor in xors
            ],
            axis=1,
        )

    normed, factor = normalize(enc_rows, enc_gain)
    partner_rows = swap(normed, "section", 1)

    if seq_count == 4:
        half = own_rows // 2
        first, second = swap(partner_rows, "seq", 1), swap(partner_rows, "seq", 2)
    else:
        quarter = seq_count // 4
        blocks = [partner_rows]
        bit = 1
        while bit < quarter:
            blocks = blocks + [swap(block, "seq", bit) for block in blocks]
            bit *= 2
        partner_rows = jnp.concatenate(blocks)
        first, second = swap(partner_rows, "seq", quarter), swap(partner_rows, "seq", 2 * quarter)
        half = partner_rows.shape[0] // 2
        blocks = [normed]
        bit = 1
        while bit < quarter:
            blocks = blocks + [swap(block, "seq", bit) for block in blocks]
            bit *= 2
        normed = jnp.concatenate(blocks)
    low, high = max(seq_count // 4, 1), max(seq_count // 2, 1)

    base = section * section_width
    outer_far = jnp.concatenate(
        [target_features(rows, (3, 2), base) for rows in (partner_rows, normed)]
    )
    outer_far = lax.ppermute(outer_far, "dp", inward)
    first, second, outer_far = tie(first, second, outer_far)

    third_top, third_bottom = swap(first[:half], "seq", high), swap(second[half:], "seq", low)
    early = jnp.concatenate([partner_rows, first, second])
    away_early = swap(section_features(early[2 * half :], 1 - section), "section", 1)
    value_early = jnp.dot(early, value_weight, preferred_element_type=F32).astype(BF16)
    key_early = jnp.dot(early, key_weight, preferred_element_type=F32).astype(BF16)
    key_early, value_early, away_early, third_top, third_bottom, outer_far = tie(
        key_early, value_early, away_early, third_top, third_bottom, outer_far
    )
    outer_first, outer_second = swap(outer_far, "seq", low), swap(outer_far, "seq", high)
    late = jnp.concatenate([third_top, third_bottom])
    away_late = swap(section_features(late, 1 - section), "section", 1)
    key_late = jnp.dot(late, key_weight, preferred_element_type=F32).astype(BF16)
    value_late = jnp.dot(late, value_weight, preferred_element_type=F32).astype(BF16)

    block_start = (seq ^ jnp.arange(seq_count, dtype=jnp.int32)) * own_rows
    positions = block_start[:, None] + jnp.arange(own_rows, dtype=jnp.int32)[None, :]
    visible = (positions.reshape(src_rows, 1) < lengths[partner]).astype(jnp.int32)

    held = {"key_early": key_early, "first": outer_first, "second": outer_second}

    def sync(*names):
        names = [name for name in names if name in held]
        held.update(zip(names, lax.optimization_barrier(tuple(held[name] for name in names))))

    heads = range(heads_here)
    attended, query_grad = [], []

    def attend(head):
        head_attended, head_query_grad, held[f"kv{head}"] = attend_head(
            head, visible, queries[0], held["key_early"], key_late, value_early, value_late, out_grad[0]
        )
        attended.append(head_attended)
        query_grad.append(head_query_grad)

    def hand_in(group):
        together = jnp.concatenate([held[f"kv{head}"] for head in group], axis=1)
        together = lax.ppermute(together, "dp", inward)
        for slot, head in enumerate(group):
            held[f"handed{head}"] = together[:, slot * 2 * HD : (slot + 1) * 2 * HD]

    attend(0)
    sync("kv0")
    hand_in((0,))
    held["their0"] = swap(held["kv0"], "section", 1)
    sync("first", "second", "key_early")
    for head in heads[1:]:
        attend(head)
    if heads_here > 1:
        hand_in((1,))
    quarter_rows = outer_far.shape[0] // 2
    held["top"] = swap(held["first"][:quarter_rows], "seq", high)
    held["bottom"] = swap(held["second"][quarter_rows:], "seq", low)
    chip_rows = jnp.concatenate(
        [section_features(early, section), section_features(late, section)]
        + [section_features(normed, section), away_early, away_late]
    )
    chip_far = target_features(chip_rows, (2, 3))
    chip_pair = target_features(chip_rows, (1,))
    chip_own = target_features(chip_rows, (0,))
    sync("handed0", "top", "bottom", "their0", *(f"kv{head}" for head in heads))
    pieces = [outer_far, held["first"], held["second"]]
    outer_far = jnp.concatenate(
        [piece[:quarter_rows] for piece in pieces]
        + [held["top"]]
        + [piece[quarter_rows:] for piece in pieces]
        + [held["bottom"]]
    )

    def send_rows(steps):
        for step in steps:
            if f"row{step}" not in held:
                rows = held["row_term"][step * own_rows : (step + 1) * own_rows]
                held[f"row{step}"] = swap(rows, "seq", step)

    def relay(head):
        term = dot(chip_pair, grads[head][0], 0, 0) + held[f"outward{head}"].astype(F32)
        held["term"] = term.astype(BF16)
        if head == heads_here - 1:
            sync("term", "row_term", "row1")
        held[f"relay{head}"] = lax.ppermute(held["term"], "dp", outward)

    grads = []
    held["pair"] = chip_pair
    for head in heads:
        held["chip"] = jnp.concatenate([held[f"kv{head}"], held[f"their{head}"]])
        handed = held[f"handed{head}"]
        held["outer"] = jnp.concatenate([handed, swap(handed, "section", 1)])
        held["far"] = (
            dot(chip_far, held["chip"], 0, 0) + dot(outer_far, held["outer"], 0, 0)
        ).astype(BF16)
        sync(
            "far",
            "chip",
            "outer",
            f"outward{head - 1}",
            f"inner{head - 1}",
            f"relay{head - 2}",
            "row_term",
            *(f"row{step}" for step in (1, 2) if head >= 3),
            "pair",
            "own",
            *(f"kv{other}" for other in heads),
            *(f"their{other}" for other in heads[1:]),
        )
        grads.append((held["chip"], held["outer"]))
        if head < heads_here - 1:
            crossed = lax.ppermute(held["far"], "dp", across)
            held[f"outward{head}"], held[f"inner{head}"] = crossed[:target_width], crossed[target_width:]
        else:
            held[f"outward{head}"] = lax.ppermute(held["far"][:target_width], "dp", across)
            held[f"inner{head}"] = lax.ppermute(held["far"][target_width:], "dp", across)
        if head == 0:
            if heads_here > 2:
                hand_in(heads[2:])
            if heads_here > 1:
                theirs = swap(jnp.stack([held[f"kv{other}"] for other in heads[1:]]), "section", 1)
                for other in heads[1:]:
                    held[f"their{other}"] = theirs[other - 1]
        else:
            relay(head - 1)
        if head == min(1, heads_here - 1):
            held["own"] = lax.ppermute(held["pair"], "dp", inward)
            held["row_term"] = row_product([held[f"kv{other}"] for other in heads], key_weight, value_weight)
        if head >= 1:
            send_rows(range(1, min(3, seq_count)) if head == 1 else range(1, seq_count))
    send_rows(range(1, seq_count))
    last = heads_here - 1
    row_names = [f"row{step}" for step in range(1, seq_count)]
    sync(f"outward{last}", f"relay{last - 1}", "row_term", "own")
    relay(last)

    totals = [None, None]
    for head in heads:
        chip_grad, outer_grad = grads[head]
        local = dot(chip_own, chip_grad, 0, 0) + dot(held["own"], outer_grad, 0, 0)
        totals = add_columns(
            totals, head, heads_here, local, held[f"inner{head}"], held[f"relay{head}"]
        )

    row_share = held["row_term"][:own_rows].astype(F32)
    for name in row_names:
        row_share = row_share + held[name].astype(F32)
    row_grad = swap(row_share.astype(BF16), "section", 1)
    enc_grad = norm_backward(enc_rows, factor, enc_gain, row_grad)
    return (
        jnp.concatenate(attended, axis=1)[None],
        enc_grad[None],
        totals[0],
        totals[1],
        jnp.concatenate(query_grad, axis=1)[None],
    )


def solution(mesh):
    placed = (
        P(("section", "dp"), "seq", None),
        P(),
        P(None, "seq"),
        P(None, "seq"),
        P(("section", "dp"), None, "seq"),
        P(("section", "dp"), None, "seq"),
        P(),
    )
    return jax.shard_map(
        on_device,
        mesh=mesh,
        in_specs=placed,
        out_specs=(
            P(("section", "dp"), None, "seq"),
            P(("section", "dp"), "seq", None),
            P(("section", "dp"), "seq"),
            P(("section", "dp"), "seq"),
            P(("section", "dp"), None, "seq"),
        ),
        check_vma=False,
    )
```

```python
import functools

import jax
import jax.numpy as jnp
from jax import lax
from jax.experimental import pallas as pl
from jax.experimental.pallas import tpu as pltpu
from jax.sharding import PartitionSpec as P

HD = 256


EPS = 1e-06
NEG_FILL = -1e30
BF16 = jnp.bfloat16
F32 = jnp.float32
FILLS_WAITS = pl.CostEstimate(flops=0, bytes_accessed=0, transcendentals=0)


def swap(value, axis, mask):
    pairs = [(source, source ^ mask) for source in range(lax.axis_size(axis))]
    return lax.ppermute(value, axis, pairs)


def normalize(enc_rows, gain):
    wide_rows = enc_rows.astype(F32)
    factor = lax.rsqrt(jnp.mean(wide_rows * wide_rows, axis=-1, keepdims=True) + EPS)
    return ((wide_rows * factor * gain).astype(BF16), factor)


def norm_backward(enc_rows, factor, gain, row_grad):
    wide_rows = enc_rows.astype(F32)
    scaled = row_grad.astype(F32) * gain
    inner_sum = jnp.mean(scaled * wide_rows, axis=-1, keepdims=True)
    return (factor * scaled - wide_rows * factor * factor * factor * inner_sum).astype(BF16)


def tie(*values):
    return lax.optimization_barrier(values)


def dot(left, right, left_dim, right_dim):
    return lax.dot_general(
        left, right, (((left_dim,), (right_dim,)), ((), ())), preferred_element_type=F32
    )


def attend_kernel(
    visible, query, key_early, key_late, value_early, value_late, upstream, attended, query_grad, kv_grad
):
    score_scale = HD ** (-0.5)
    query_rows, upstream_rows = query[...], upstream[...]
    key_rows = jnp.concatenate([key_early[...], key_late[...]], axis=0)
    value_rows = jnp.concatenate([value_early[...], value_late[...]], axis=0)
    scores = dot(key_rows, query_rows, 1, 1) * score_scale
    scores = jnp.where(visible[...] > 0, scores, NEG_FILL)
    exponent = jnp.exp(scores - jnp.max(scores, axis=0, keepdims=True))
    probability = exponent * (1.0 / jnp.sum(exponent, axis=0, keepdims=True))
    prob_weights = probability.astype(BF16)
    grad_probs = dot(value_rows, upstream_rows, 1, 1)
    inner_sum = jnp.sum(probability * grad_probs, axis=0, keepdims=True)
    grad_scores = (probability * (grad_probs - inner_sum) * score_scale).astype(BF16)
    kv_grad[:, :HD] = dot(grad_scores, query_rows, 1, 0).astype(BF16)
    kv_grad[:, HD:] = dot(prob_weights, upstream_rows, 1, 0).astype(BF16)
    attended[...] = dot(prob_weights, value_rows, 0, 0).astype(BF16)
    query_grad[...] = dot(grad_scores, key_rows, 0, 0).astype(BF16)


def attend_head(head, visible, query, key_early, key_late, value_early, value_late, upstream):
    src_rows, target_rows = visible.shape[0], query.shape[0]
    early, late = key_early.shape[0], key_late.shape[0]

    def column(rows):
        return pl.BlockSpec((rows, HD), lambda step: (0, head))

    def whole(rows, columns):
        return pl.BlockSpec((rows, columns), lambda step: (0, 0))

    return pl.pallas_call(
        attend_kernel,
        grid=(1,),
        in_specs=[
            whole(src_rows, 1),
            column(target_rows),
            column(early),
            column(late),
            column(early),
            column(late),
            column(target_rows),
        ],
        out_specs=[whole(target_rows, HD), whole(target_rows, HD), whole(src_rows, 2 * HD)],
        out_shape=[
            jax.ShapeDtypeStruct((target_rows, HD), BF16),
            jax.ShapeDtypeStruct((target_rows, HD), BF16),
            jax.ShapeDtypeStruct((src_rows, 2 * HD), BF16),
        ],
        compiler_params=pltpu.CompilerParams(vmem_limit_bytes=48 * 1024 * 1024),
        cost_estimate=FILLS_WAITS,
    )(visible, query, key_early, key_late, value_early, value_late, upstream)


def row_kernel(*refs):
    *grads, key_block, value_block, out = refs
    key_grads = jnp.concatenate([grad[:, :HD] for grad in grads], axis=1)
    value_grads = jnp.concatenate([grad[:, HD:] for grad in grads], axis=1)
    out[...] = (dot(key_grads, key_block[...], 1, 1) + dot(value_grads, value_block[...], 1, 1)).astype(BF16)


def row_product(grads, key_weight, value_weight):
    rows, columns = grads[0].shape
    features, heads_width = key_weight.shape
    block = 512
    whole = pl.BlockSpec((rows, columns), lambda step: (0, 0))
    weight = pl.BlockSpec((block, heads_width), lambda step: (step, 0))
    return pl.pallas_call(
        row_kernel,
        grid=(features // block,),
        in_specs=[whole] * len(grads) + [weight, weight],
        out_specs=pl.BlockSpec((rows, block), lambda step: (0, step)),
        out_shape=jax.ShapeDtypeStruct((rows, features), BF16),
        compiler_params=pltpu.CompilerParams(vmem_limit_bytes=40 * 1024 * 1024),
        cost_estimate=pl.CostEstimate(
            flops=4 * rows * features * heads_width,
            bytes_accessed=4 * features * heads_width + 2 * rows * (features + 2 * heads_width),
            transcendentals=0,
        ),
    )(*grads, key_weight, value_weight)


def add_kernel(kind_count, local, first, second, *refs):
    outs = refs[-kind_count:]
    total = local[...] + first[...].astype(F32) + second[...].astype(F32)
    for slot, out in enumerate(outs):
        out[...] = total[:, slot * HD : (slot + 1) * HD]


def add_columns(totals, head, heads_here, local, first, second):
    rows, columns = local.shape
    here = pl.BlockSpec((rows, columns), lambda step: (0, 0))
    kept = [total for total in totals if total is not None]
    count = columns // HD
    return pl.pallas_call(
        functools.partial(add_kernel, count),
        grid=(1,),
        in_specs=[here] * 3 + [pl.BlockSpec(memory_space=pl.ANY)] * len(kept),
        out_specs=[pl.BlockSpec((rows, HD), lambda step: (0, head))] * count,
        out_shape=[jax.ShapeDtypeStruct((rows, heads_here * HD), F32)] * count,
        input_output_aliases={3 + slot: slot for slot in range(len(kept))},
        cost_estimate=pl.CostEstimate(
            flops=2 * rows * columns, bytes_accessed=12 * rows * columns, transcendentals=0
        ),
        compiler_params=pltpu.CompilerParams(vmem_limit_bytes=32 * 1024 * 1024),
    )(local, first, second, *kept)


def on_device(enc_states, enc_gain, key_weight, value_weight, queries, out_grad, lengths):
    enc_rows = enc_states[0]
    own_rows, width = enc_rows.shape
    heads_here = key_weight.shape[1] // HD
    heads = range(heads_here)
    last = heads_here - 1
    section_count, dp_count, seq_count = (lax.axis_size(name) for name in ("section", "dp", "seq"))
    section, place, seq = (lax.axis_index(name) for name in ("section", "dp", "seq"))
    partner = (section * dp_count + place + dp_count) % (section_count * dp_count)
    src_rows = own_rows * seq_count
    section_width = width // section_count
    target_width = section_width // dp_count
    across = [(1, 2), (2, 1)]
    held = {}

    def sync(*names):
        names = ["factor"] + [name for name in names if name in held]
        held.update(zip(names, lax.optimization_barrier(tuple(held[name] for name in names))))

    def section_features(rows, index):
        return lax.dynamic_slice_in_dim(rows, index * section_width, section_width, axis=1)

    def target_features(rows, xors, base=0):
        return jnp.concatenate(
            [
                lax.dynamic_slice_in_dim(rows, base + (place ^ xor) * target_width, target_width, axis=1)
                for xor in xors
            ],
            axis=1,
        )

    def swap_both(rows, mask):
        count = section_count * seq_count
        pairs = [(source, source ^ (seq_count + mask)) for source in range(count)]
        return lax.ppermute(rows, ("section", "seq"), pairs)

    normed, held["factor"] = normalize(enc_rows, enc_gain)
    partner_rows = swap(normed, "section", 1)

    low, high = max(seq_count // 4, 1), max(seq_count // 2, 1)
    if low > 1:
        gathered = []
        for rows in (normed, partner_rows):
            blocks = [rows]
            bit = 1
            while bit < low:
                blocks = blocks + [swap(block, "seq", bit) for block in blocks]
                bit *= 2
            gathered.append(jnp.concatenate(blocks))
        normed, partner_rows = gathered
    half = normed.shape[0] // 2
    first, second = swap_both(normed, low), swap_both(normed, high)

    base = section * section_width
    outer_far = jnp.concatenate([target_features(rows, (3, 2), base) for rows in (partner_rows, normed)])
    outer_far = swap(outer_far, "dp", 1)
    first, second, outer_far = tie(first, second, outer_far)

    third_top, third_bottom = swap(first[:half], "seq", high), swap(second[half:], "seq", low)
    early = jnp.concatenate([partner_rows, first, second])
    away_early = swap(section_features(early[2 * half :], 1 - section), "section", 1)
    value_early = jnp.dot(early, value_weight, preferred_element_type=F32).astype(BF16)
    key_early = jnp.dot(early, key_weight, preferred_element_type=F32).astype(BF16)
    key_early, value_early, away_early, third_top, third_bottom, outer_far = tie(
        key_early, value_early, away_early, third_top, third_bottom, outer_far
    )
    held["first"], held["second"] = swap(outer_far, "seq", low), swap(outer_far, "seq", high)
    late = jnp.concatenate([third_top, third_bottom])
    away_late = swap(section_features(late, 1 - section), "section", 1)
    key_late = jnp.dot(late, key_weight, preferred_element_type=F32).astype(BF16)
    value_late = jnp.dot(late, value_weight, preferred_element_type=F32).astype(BF16)

    block_start = (seq ^ jnp.arange(seq_count, dtype=jnp.int32)) * own_rows
    positions = block_start[:, None] + jnp.arange(own_rows, dtype=jnp.int32)[None, :]
    visible = (positions.reshape(src_rows, 1) < lengths[partner]).astype(jnp.int32)

    attended, query_grad = [], []
    for head in heads:
        head_attended, head_query_grad, held[f"kv{head}"] = attend_head(
            head, visible, queries[0], key_early, key_late, value_early, value_late, out_grad[0]
        )
        attended.append(head_attended)
        query_grad.append(head_query_grad)

    def hand_in(group):
        together = swap(jnp.concatenate([held[f"kv{head}"] for head in group], axis=1), "dp", 1)
        for slot, head in enumerate(group):
            held[f"handed{head}"] = together[:, slot * 2 * HD : (slot + 1) * 2 * HD]

    hand_in((0,))
    theirs = swap(jnp.stack([held[f"kv{head}"] for head in heads]), "section", 1)
    for head in heads:
        held[f"their{head}"] = theirs[head]
    quarter_rows = outer_far.shape[0] // 2
    sync("first", "second", "kv1")
    held["top"] = swap(held["first"][:quarter_rows], "seq", high)
    held["bottom"] = swap(held["second"][quarter_rows:], "seq", low)
    chip_rows = jnp.concatenate(
        [section_features(early, section), section_features(late, section)]
        + [section_features(normed, section), away_early, away_late]
    )
    held["chip_far"] = target_features(chip_rows, (2, 3))
    held["chip_pair"] = target_features(chip_rows, (1,))
    held["chip_own"] = target_features(chip_rows, (0,))
    early_pieces = [outer_far, held["first"], held["second"]]
    held["mine"] = jnp.concatenate([piece[:quarter_rows] for piece in early_pieces])
    held["yours"] = jnp.concatenate([piece[quarter_rows:] for piece in early_pieces])
    if heads_here > 1:
        hand_in((1,))
    sync("handed0", "top", "bottom", "mine", "yours", "chip_far", "chip_pair", "chip_own")

    def chip_sum(name, head):
        rows = held[name]
        return dot(rows[:src_rows], held[f"kv{head}"], 0, 0) + dot(rows[src_rows:], held[f"their{head}"], 0, 0)

    def outer_sum(head):
        handed = held[f"handed{head}"]
        handed_other = swap(handed, "section", 1)
        cut = 3 * quarter_rows
        return (
            dot(held["mine"], handed[:cut], 0, 0)
            + dot(held["yours"], handed_other[:cut], 0, 0)
            + dot(held["top"], handed[cut:], 0, 0)
            + dot(held["bottom"], handed_other[cut:], 0, 0)
        )

    def send_rows(steps):
        for step in steps:
            if f"row{step}" not in held:
                rows = held["row_term"][step * own_rows : (step + 1) * own_rows]
                held[f"row{step}"] = swap(rows, "seq", step)

    def relay(head):
        term = held[f"pair{head}"] + held[f"outward{head}"].astype(F32)
        held[f"relay{head}"] = swap(term.astype(BF16), "dp", 1)

    def finish(head):
        totals = [held.get(f"total{kind}") for kind in (0, 1)]
        held["total0"], held["total1"] = add_columns(
            totals, head, heads_here, held[f"own{head}"], held[f"inner{head}"], held[f"relay{head}"]
        )

    row_names = [f"row{step}" for step in range(1, seq_count)]
    for head in heads:
        if head == 0:
            held["near0"] = chip_sum("chip_far", 0)
        held["far"] = (held[f"near{head}"] + outer_sum(head)).astype(BF16)
        sync(
            "far",
            f"outward{head - 1}",
            f"inner{head - 1}",
            f"relay{head - 2}",
            f"pair{head - 1}",
            f"own{head - 1}",
            "row_term",
            *(row_names if head == last else ()),
            *(f"kv{other}" for other in heads),
            *(f"their{other}" for other in heads),
        )
        if head < last:
            crossed = lax.ppermute(held["far"], "dp", across)
            held[f"outward{head}"], held[f"inner{head}"] = crossed[:target_width], crossed[target_width:]
        else:
            held[f"outward{head}"] = lax.ppermute(held["far"][:target_width], "dp", across)
            held[f"inner{head}"] = lax.ppermute(held["far"][target_width:], "dp", across)
        if head == 0:
            if heads_here > 2:
                hand_in(heads[2:])
            held["row_term"] = row_product([held[f"kv{other}"] for other in heads], key_weight, value_weight)
        else:
            relay(head - 1)
        held[f"pair{head}"], held[f"own{head}"] = chip_sum("chip_pair", head), chip_sum("chip_own", head)
        if head < last:
            held[f"near{head + 1}"] = chip_sum("chip_far", head + 1)
        if head == 0:
            sync("handed1")
        else:
            sync(f"handed{head + 1}", f"near{head + 1}")
        if head >= 1:
            send_rows(range(1, min(3, seq_count)) if head == 1 else range(1, seq_count))
    send_rows(range(1, seq_count))
    for head in heads[:-1]:
        finish(head)
    relay(last)
    finish(last)

    row_share = held["row_term"][:own_rows].astype(F32)
    for name in row_names:
        row_share = row_share + held[name].astype(F32)
    row_grad = swap(row_share.astype(BF16), "section", 1)
    enc_grad = norm_backward(enc_rows, held["factor"], enc_gain, row_grad)
    return (
        jnp.concatenate(attended, axis=1)[None],
        enc_grad[None],
        held["total0"],
        held["total1"],
        jnp.concatenate(query_grad, axis=1)[None],
    )


def solution(mesh):
    placed = (
        P(("section", "dp"), "seq", None),
        P(),
        P(None, "seq"),
        P(None, "seq"),
        P(("section", "dp"), None, "seq"),
        P(("section", "dp"), None, "seq"),
        P(),
    )
    return jax.shard_map(
        on_device,
        mesh=mesh,
        in_specs=placed,
        out_specs=(
            P(("section", "dp"), None, "seq"),
            P(("section", "dp"), "seq", None),
            P(("section", "dp"), "seq"),
            P(("section", "dp"), "seq"),
            P(("section", "dp"), None, "seq"),
        ),
        check_vma=False,
    )
```

```python
import functools

import jax
import jax.numpy as jnp
from jax import lax
from jax.experimental import pallas as pl
from jax.experimental.pallas import tpu as pltpu
from jax.sharding import PartitionSpec as P

HD = 256


EPS = 1e-06
NEG_FILL = -1e30
BF16 = jnp.bfloat16
F32 = jnp.float32
FILLS_WAITS = pl.CostEstimate(flops=0, bytes_accessed=0, transcendentals=0)


def swap(value, axis, mask):
    pairs = [(source, source ^ mask) for source in range(lax.axis_size(axis))]
    return lax.ppermute(value, axis, pairs)


def normalize(enc_rows, gain):
    wide_rows = enc_rows.astype(F32)
    factor = lax.rsqrt(jnp.mean(wide_rows * wide_rows, axis=-1, keepdims=True) + EPS)
    return ((wide_rows * factor * gain).astype(BF16), factor)


def norm_backward(enc_rows, factor, gain, row_grad):
    wide_rows = enc_rows.astype(F32)
    scaled = row_grad.astype(F32) * gain
    inner_sum = jnp.mean(scaled * wide_rows, axis=-1, keepdims=True)
    return (factor * scaled - wide_rows * factor * factor * factor * inner_sum).astype(BF16)


def tie(*values):
    return lax.optimization_barrier(values)


def dot(left, right, left_dim, right_dim):
    return lax.dot_general(
        left, right, (((left_dim,), (right_dim,)), ((), ())), preferred_element_type=F32
    )


def attend_kernel(
    visible, query, key_early, key_late, value_early, value_late, upstream, attended, query_grad, kv_grad
):
    score_scale = HD ** (-0.5)
    query_rows, upstream_rows = query[...], upstream[...]
    key_rows = jnp.concatenate([key_early[...], key_late[...]], axis=0)
    value_rows = jnp.concatenate([value_early[...], value_late[...]], axis=0)
    scores = dot(key_rows, query_rows, 1, 1) * score_scale
    scores = jnp.where(visible[...] > 0, scores, NEG_FILL)
    exponent = jnp.exp(scores - jnp.max(scores, axis=0, keepdims=True))
    probability = exponent * (1.0 / jnp.sum(exponent, axis=0, keepdims=True))
    prob_weights = probability.astype(BF16)
    grad_probs = dot(value_rows, upstream_rows, 1, 1)
    inner_sum = jnp.sum(probability * grad_probs, axis=0, keepdims=True)
    grad_scores = (probability * (grad_probs - inner_sum) * score_scale).astype(BF16)
    kv_grad[:, :HD] = dot(grad_scores, query_rows, 1, 0).astype(BF16)
    kv_grad[:, HD:] = dot(prob_weights, upstream_rows, 1, 0).astype(BF16)
    attended[...] = dot(prob_weights, value_rows, 0, 0).astype(BF16)
    query_grad[...] = dot(grad_scores, key_rows, 0, 0).astype(BF16)


def attend_head(head, visible, query, key_early, key_late, value_early, value_late, upstream):
    src_rows, target_rows = visible.shape[0], query.shape[0]
    early, late = key_early.shape[0], key_late.shape[0]

    def column(rows):
        return pl.BlockSpec((rows, HD), lambda step: (0, head))

    def whole(rows, columns):
        return pl.BlockSpec((rows, columns), lambda step: (0, 0))

    return pl.pallas_call(
        attend_kernel,
        grid=(1,),
        in_specs=[
            whole(src_rows, 1),
            column(target_rows),
            column(early),
            column(late),
            column(early),
            column(late),
            column(target_rows),
        ],
        out_specs=[whole(target_rows, HD), whole(target_rows, HD), whole(src_rows, 2 * HD)],
        out_shape=[
            jax.ShapeDtypeStruct((target_rows, HD), BF16),
            jax.ShapeDtypeStruct((target_rows, HD), BF16),
            jax.ShapeDtypeStruct((src_rows, 2 * HD), BF16),
        ],
        compiler_params=pltpu.CompilerParams(vmem_limit_bytes=48 * 1024 * 1024),
        cost_estimate=FILLS_WAITS,
    )(visible, query, key_early, key_late, value_early, value_late, upstream)


def row_kernel(*refs):
    *grads, key_block, value_block, out = refs
    key_grads = jnp.concatenate([grad[:, :HD] for grad in grads], axis=1)
    value_grads = jnp.concatenate([grad[:, HD:] for grad in grads], axis=1)
    out[...] = (dot(key_grads, key_block[...], 1, 1) + dot(value_grads, value_block[...], 1, 1)).astype(BF16)


def row_product(grads, key_weight, value_weight):
    rows, columns = grads[0].shape
    features, heads_width = key_weight.shape
    block = 512
    whole = pl.BlockSpec((rows, columns), lambda step: (0, 0))
    weight = pl.BlockSpec((block, heads_width), lambda step: (step, 0))
    return pl.pallas_call(
        row_kernel,
        grid=(features // block,),
        in_specs=[whole] * len(grads) + [weight, weight],
        out_specs=pl.BlockSpec((rows, block), lambda step: (0, step)),
        out_shape=jax.ShapeDtypeStruct((rows, features), BF16),
        compiler_params=pltpu.CompilerParams(vmem_limit_bytes=40 * 1024 * 1024),
        cost_estimate=pl.CostEstimate(
            flops=4 * rows * features * heads_width,
            bytes_accessed=4 * features * heads_width + 2 * rows * (features + 2 * heads_width),
            transcendentals=0,
        ),
    )(*grads, key_weight, value_weight)


def add_kernel(kind_count, local, first, second, *refs):
    outs = refs[-kind_count:]
    total = local[...] + first[...].astype(F32) + second[...].astype(F32)
    for slot, out in enumerate(outs):
        out[...] = total[:, slot * HD : (slot + 1) * HD]


def add_columns(totals, head, heads_here, local, first, second):
    rows, columns = local.shape
    here = pl.BlockSpec((rows, columns), lambda step: (0, 0))
    kept = [total for total in totals if total is not None]
    count = columns // HD
    return pl.pallas_call(
        functools.partial(add_kernel, count),
        grid=(1,),
        in_specs=[here] * 3 + [pl.BlockSpec(memory_space=pl.ANY)] * len(kept),
        out_specs=[pl.BlockSpec((rows, HD), lambda step: (0, head))] * count,
        out_shape=[jax.ShapeDtypeStruct((rows, heads_here * HD), F32)] * count,
        input_output_aliases={3 + slot: slot for slot in range(len(kept))},
        cost_estimate=pl.CostEstimate(
            flops=2 * rows * columns, bytes_accessed=12 * rows * columns, transcendentals=0
        ),
        compiler_params=pltpu.CompilerParams(vmem_limit_bytes=32 * 1024 * 1024),
    )(local, first, second, *kept)


def on_device(enc_states, enc_gain, key_weight, value_weight, queries, out_grad, lengths):
    enc_rows = enc_states[0]
    own_rows, width = enc_rows.shape
    heads_here = key_weight.shape[1] // HD
    heads = range(heads_here)
    last = heads_here - 1
    section_count, dp_count, seq_count = (lax.axis_size(name) for name in ("section", "dp", "seq"))
    section, place, seq = (lax.axis_index(name) for name in ("section", "dp", "seq"))
    partner = (section * dp_count + place + dp_count) % (section_count * dp_count)
    src_rows = own_rows * seq_count
    section_width = width // section_count
    target_width = section_width // dp_count
    across = [(1, 2), (2, 1)]
    held = {}

    def sync(*names):
        names = ["factor"] + [name for name in names if name in held]
        held.update(zip(names, lax.optimization_barrier(tuple(held[name] for name in names))))

    def section_features(rows, index):
        return lax.dynamic_slice_in_dim(rows, index * section_width, section_width, axis=1)

    def target_features(rows, xors, base=0):
        return jnp.concatenate(
            [
                lax.dynamic_slice_in_dim(rows, base + (place ^ xor) * target_width, target_width, axis=1)
                for xor in xors
            ],
            axis=1,
        )

    def swap_both(rows, mask):
        count = section_count * seq_count
        pairs = [(source, source ^ (seq_count + mask)) for source in range(count)]
        return lax.ppermute(rows, ("section", "seq"), pairs)

    normed, held["factor"] = normalize(enc_rows, enc_gain)
    partner_rows = swap(normed, "section", 1)

    low, high = max(seq_count // 4, 1), max(seq_count // 2, 1)
    if low > 1:
        gathered = []
        for rows in (normed, partner_rows):
            blocks = [rows]
            bit = 1
            while bit < low:
                blocks = blocks + [swap(block, "seq", bit) for block in blocks]
                bit *= 2
            gathered.append(jnp.concatenate(blocks))
        normed, partner_rows = gathered
    half = normed.shape[0] // 2
    first, second = swap_both(normed, low), swap_both(normed, high)

    base = section * section_width
    outer_far = jnp.concatenate([target_features(rows, (3, 2), base) for rows in (partner_rows, normed)])
    outer_far = swap(outer_far, "dp", 1)
    first, second, outer_far = tie(first, second, outer_far)

    third_top, third_bottom = swap(first[:half], "seq", high), swap(second[half:], "seq", low)
    early = jnp.concatenate([partner_rows, first, second])
    away_early = swap(section_features(early[2 * half :], 1 - section), "section", 1)
    value_early = jnp.dot(early, value_weight, preferred_element_type=F32).astype(BF16)
    key_early = jnp.dot(early, key_weight, preferred_element_type=F32).astype(BF16)
    key_early, value_early, away_early, third_top, third_bottom, outer_far = tie(
        key_early, value_early, away_early, third_top, third_bottom, outer_far
    )
    held["first"], held["second"] = swap(outer_far, "seq", low), swap(outer_far, "seq", high)
    late = jnp.concatenate([third_top, third_bottom])
    away_late = swap(section_features(late, 1 - section), "section", 1)
    key_late = jnp.dot(late, key_weight, preferred_element_type=F32).astype(BF16)
    value_late = jnp.dot(late, value_weight, preferred_element_type=F32).astype(BF16)

    block_start = (seq ^ jnp.arange(seq_count, dtype=jnp.int32)) * own_rows
    positions = block_start[:, None] + jnp.arange(own_rows, dtype=jnp.int32)[None, :]
    visible = (positions.reshape(src_rows, 1) < lengths[partner]).astype(jnp.int32)

    held["key_early"] = key_early
    attended, query_grad = [], []

    def attend(head):
        head_attended, head_query_grad, held[f"kv{head}"] = attend_head(
            head, visible, queries[0], held["key_early"], key_late, value_early, value_late, out_grad[0]
        )
        attended.append(head_attended)
        query_grad.append(head_query_grad)

    def hand_in(head):
        if head < heads_here:
            held[f"handed{head}"] = swap(held[f"kv{head}"], "dp", 1)

    def exchange(group):
        theirs = swap(jnp.stack([held[f"kv{head}"] for head in group]), "section", 1)
        for slot, head in enumerate(group):
            held[f"their{head}"] = theirs[slot]

    attend(0)
    hand_in(0)
    exchange((0,))
    sync("first", "second", "key_early")
    quarter_rows = outer_far.shape[0] // 2
    held["top"] = swap(held["first"][:quarter_rows], "seq", high)
    held["bottom"] = swap(held["second"][quarter_rows:], "seq", low)
    for head in heads[1:]:
        attend(head)
    hand_in(1)
    chip_rows = jnp.concatenate(
        [section_features(early, section), section_features(late, section)]
        + [section_features(normed, section), away_early, away_late]
    )
    held["chip_far"] = target_features(chip_rows, (2, 3))
    held["chip_pair"] = target_features(chip_rows, (1,))
    held["chip_own"] = target_features(chip_rows, (0,))
    early_pieces = [outer_far, held["first"], held["second"]]
    held["mine"] = jnp.concatenate([piece[:quarter_rows] for piece in early_pieces])
    held["yours"] = jnp.concatenate([piece[quarter_rows:] for piece in early_pieces])
    sync(
        "handed0", "their0", "top", "bottom", "mine", "yours", "chip_far", "chip_pair", "chip_own",
        *(f"kv{head}" for head in heads),
    )

    def chip_sum(name, head):
        rows = held[name]
        return dot(rows[:src_rows], held[f"kv{head}"], 0, 0) + dot(rows[src_rows:], held[f"their{head}"], 0, 0)

    def outer_sum(head):
        handed, handed_other = held[f"handed{head}"], held[f"other{head}"]
        cut = 3 * quarter_rows
        return (
            dot(held["mine"], handed[:cut], 0, 0)
            + dot(held["yours"], handed_other[:cut], 0, 0)
            + dot(held["top"], handed[cut:], 0, 0)
            + dot(held["bottom"], handed_other[cut:], 0, 0)
        )

    def send_rows(steps):
        for step in steps:
            if f"row{step}" not in held:
                rows = held["row_term"][step * own_rows : (step + 1) * own_rows]
                held[f"row{step}"] = swap(rows, "seq", step)

    def relay(group):
        terms = [held[f"pair{head}"] + held[f"outward{head}"].astype(F32) for head in group]
        terms = swap(jnp.concatenate([term.astype(BF16) for term in terms], axis=1), "dp", 1)
        for slot, head in enumerate(group):
            held[f"relay{head}"] = terms[:, slot * 2 * HD : (slot + 1) * 2 * HD]

    def finish(head):
        totals = [held.get(f"total{kind}") for kind in (0, 1)]
        held["total0"], held["total1"] = add_columns(
            totals, head, heads_here, held[f"own{head}"], held[f"inner{head}"], held[f"relay{head}"]
        )

    row_names = [f"row{step}" for step in range(1, seq_count)]
    held["near0"] = chip_sum("chip_far", 0)
    held["other0"] = swap(held["handed0"], "section", 1)
    for head in heads:
        held["far"] = (held[f"near{head}"] + outer_sum(head)).astype(BF16)
        sync(
            "far",
            f"outward{head - 1}",
            f"inner{head - 2}",
            f"relay{head - 2}",
            f"pair{head - 1}",
            f"own{head - 1}",
            f"near{head}",
            "row_term",
            *(row_names[:2] if head == 2 else ()),
            *(f"kv{other}" for other in heads),
            *(f"their{other}" for other in heads),
            *((f"handed{head + 1}",) if head > 0 else ()),
        )
        held[f"outward{head}"] = lax.ppermute(held["far"][:target_width], "dp", across)
        held[f"inner{head}"] = lax.ppermute(held["far"][target_width:], "dp", across)
        hand_in(head + 2)
        if head == 0 and heads_here > 1:
            exchange(heads[1:])
            sync("handed1", *(f"kv{other}" for other in heads))
        if head < last:
            held[f"other{head + 1}"] = swap(held[f"handed{head + 1}"], "section", 1)
            if head > 0:
                sync(f"other{head + 1}", *(f"{kind}{other}" for kind in ("kv", "their") for other in heads))
        held[f"pair{head}"], held[f"own{head}"] = chip_sum("chip_pair", head), chip_sum("chip_own", head)
        if head < last:
            held[f"near{head + 1}"] = chip_sum("chip_far", head + 1)
        if head == 0:
            held["row_term"] = row_product([held[f"kv{other}"] for other in heads], key_weight, value_weight)
            send_rows(range(1, min(3, seq_count)))
        if head == 2:
            relay((0, 1))
            send_rows(range(3, seq_count))
        if head == 3:
            relay((2,))
    send_rows(range(1, seq_count))
    for head in heads[:-1]:
        if f"relay{head}" not in held:
            relay((head,))
        finish(head)
    relay((last,))
    finish(last)

    row_share = held["row_term"][:own_rows].astype(F32)
    for name in row_names:
        row_share = row_share + held[name].astype(F32)
    row_grad = swap(row_share.astype(BF16), "section", 1)
    enc_grad = norm_backward(enc_rows, held["factor"], enc_gain, row_grad)
    return (
        jnp.concatenate(attended, axis=1)[None],
        enc_grad[None],
        held["total0"],
        held["total1"],
        jnp.concatenate(query_grad, axis=1)[None],
    )


def solution(mesh):
    placed = (
        P(("section", "dp"), "seq", None),
        P(),
        P(None, "seq"),
        P(None, "seq"),
        P(("section", "dp"), None, "seq"),
        P(("section", "dp"), None, "seq"),
        P(),
    )
    return jax.shard_map(
        on_device,
        mesh=mesh,
        in_specs=placed,
        out_specs=(
            P(("section", "dp"), None, "seq"),
            P(("section", "dp"), "seq", None),
            P(("section", "dp"), "seq"),
            P(("section", "dp"), "seq"),
            P(("section", "dp"), None, "seq"),
        ),
        check_vma=False,
    )
```

```python
import functools

import jax
import jax.numpy as jnp
from jax import lax
from jax.experimental import pallas as pl
from jax.experimental.pallas import tpu as pltpu
from jax.sharding import PartitionSpec as P

HD = 256


EPS = 1e-06
NEG_FILL = -1e30
BF16 = jnp.bfloat16
F32 = jnp.float32
FILLS_WAITS = pl.CostEstimate(flops=0, bytes_accessed=0, transcendentals=0)


def swap(value, axis, mask):
    pairs = [(source, source ^ mask) for source in range(lax.axis_size(axis))]
    return lax.ppermute(value, axis, pairs)


def normalize(enc_rows, gain):
    wide_rows = enc_rows.astype(F32)
    factor = lax.rsqrt(jnp.mean(wide_rows * wide_rows, axis=-1, keepdims=True) + EPS)
    return ((wide_rows * factor * gain).astype(BF16), factor)


def norm_backward(enc_rows, factor, gain, row_grad):
    wide_rows = enc_rows.astype(F32)
    scaled = row_grad.astype(F32) * gain
    inner_sum = jnp.mean(scaled * wide_rows, axis=-1, keepdims=True)
    return (factor * scaled - wide_rows * factor * factor * factor * inner_sum).astype(BF16)


def tie(*values):
    return lax.optimization_barrier(values)


def dot(left, right, left_dim, right_dim):
    return lax.dot_general(
        left, right, (((left_dim,), (right_dim,)), ((), ())), preferred_element_type=F32
    )


def attend_kernel(
    visible, query, key_early, key_late, value_early, value_late, upstream, attended, query_grad, kv_grad
):
    score_scale = HD ** (-0.5)
    query_rows, upstream_rows = query[...], upstream[...]
    key_rows = jnp.concatenate([key_early[...], key_late[...]], axis=0)
    value_rows = jnp.concatenate([value_early[...], value_late[...]], axis=0)
    scores = dot(key_rows, query_rows, 1, 1) * score_scale
    scores = jnp.where(visible[...] > 0, scores, NEG_FILL)
    exponent = jnp.exp(scores - jnp.max(scores, axis=0, keepdims=True))
    probability = exponent * (1.0 / jnp.sum(exponent, axis=0, keepdims=True))
    prob_weights = probability.astype(BF16)
    grad_probs = dot(value_rows, upstream_rows, 1, 1)
    inner_sum = jnp.sum(probability * grad_probs, axis=0, keepdims=True)
    grad_scores = (probability * (grad_probs - inner_sum) * score_scale).astype(BF16)
    kv_grad[:, :HD] = dot(grad_scores, query_rows, 1, 0).astype(BF16)
    kv_grad[:, HD:] = dot(prob_weights, upstream_rows, 1, 0).astype(BF16)
    attended[...] = dot(prob_weights, value_rows, 0, 0).astype(BF16)
    query_grad[...] = dot(grad_scores, key_rows, 0, 0).astype(BF16)


def attend_head(head, visible, query, key_early, key_late, value_early, value_late, upstream):
    src_rows, target_rows = visible.shape[0], query.shape[0]
    early, late = key_early.shape[0], key_late.shape[0]

    def column(rows):
        return pl.BlockSpec((rows, HD), lambda step: (0, head))

    def whole(rows, columns):
        return pl.BlockSpec((rows, columns), lambda step: (0, 0))

    return pl.pallas_call(
        attend_kernel,
        grid=(1,),
        in_specs=[
            whole(src_rows, 1),
            column(target_rows),
            column(early),
            column(late),
            column(early),
            column(late),
            column(target_rows),
        ],
        out_specs=[whole(target_rows, HD), whole(target_rows, HD), whole(src_rows, 2 * HD)],
        out_shape=[
            jax.ShapeDtypeStruct((target_rows, HD), BF16),
            jax.ShapeDtypeStruct((target_rows, HD), BF16),
            jax.ShapeDtypeStruct((src_rows, 2 * HD), BF16),
        ],
        compiler_params=pltpu.CompilerParams(vmem_limit_bytes=48 * 1024 * 1024),
        cost_estimate=FILLS_WAITS,
    )(visible, query, key_early, key_late, value_early, value_late, upstream)


def row_kernel(*refs):
    *grads, key_block, value_block, out = refs
    key_grads = jnp.concatenate([grad[:, :HD] for grad in grads], axis=1)
    value_grads = jnp.concatenate([grad[:, HD:] for grad in grads], axis=1)
    out[...] = (dot(key_grads, key_block[...], 1, 1) + dot(value_grads, value_block[...], 1, 1)).astype(BF16)


def row_product(grads, key_weight, value_weight):
    rows, columns = grads[0].shape
    features, heads_width = key_weight.shape
    block = 512
    whole = pl.BlockSpec((rows, columns), lambda step: (0, 0))
    weight = pl.BlockSpec((block, heads_width), lambda step: (step, 0))
    return pl.pallas_call(
        row_kernel,
        grid=(features // block,),
        in_specs=[whole] * len(grads) + [weight, weight],
        out_specs=pl.BlockSpec((rows, block), lambda step: (0, step)),
        out_shape=jax.ShapeDtypeStruct((rows, features), BF16),
        compiler_params=pltpu.CompilerParams(vmem_limit_bytes=40 * 1024 * 1024),
        cost_estimate=pl.CostEstimate(
            flops=4 * rows * features * heads_width,
            bytes_accessed=4 * features * heads_width + 2 * rows * (features + 2 * heads_width),
            transcendentals=0,
        ),
    )(*grads, key_weight, value_weight)


def add_kernel(kind_count, local, first, second, *refs):
    outs = refs[-kind_count:]
    total = local[...] + first[...].astype(F32) + second[...].astype(F32)
    for slot, out in enumerate(outs):
        out[...] = total[:, slot * HD : (slot + 1) * HD]


def add_columns(totals, head, heads_here, local, first, second):
    rows, columns = local.shape
    here = pl.BlockSpec((rows, columns), lambda step: (0, 0))
    kept = [total for total in totals if total is not None]
    count = columns // HD
    return pl.pallas_call(
        functools.partial(add_kernel, count),
        grid=(1,),
        in_specs=[here] * 3 + [pl.BlockSpec(memory_space=pl.ANY)] * len(kept),
        out_specs=[pl.BlockSpec((rows, HD), lambda step: (0, head))] * count,
        out_shape=[jax.ShapeDtypeStruct((rows, heads_here * HD), F32)] * count,
        input_output_aliases={3 + slot: slot for slot in range(len(kept))},
        cost_estimate=pl.CostEstimate(
            flops=2 * rows * columns, bytes_accessed=12 * rows * columns, transcendentals=0
        ),
        compiler_params=pltpu.CompilerParams(vmem_limit_bytes=32 * 1024 * 1024),
    )(local, first, second, *kept)


def on_device(enc_states, enc_gain, key_weight, value_weight, queries, out_grad, lengths):
    enc_rows = enc_states[0]
    own_rows, width = enc_rows.shape
    heads_here = key_weight.shape[1] // HD
    heads = range(heads_here)
    last = heads_here - 1
    section_count, dp_count, seq_count = (lax.axis_size(name) for name in ("section", "dp", "seq"))
    section, place, seq = (lax.axis_index(name) for name in ("section", "dp", "seq"))
    partner = (section * dp_count + place + dp_count) % (section_count * dp_count)
    src_rows = own_rows * seq_count
    section_width = width // section_count
    target_width = section_width // dp_count
    across = [(1, 2), (2, 1)]
    held = {}

    def sync(*names):
        names = ["factor"] + [name for name in names if name in held]
        held.update(zip(names, lax.optimization_barrier(tuple(held[name] for name in names))))

    def section_features(rows, index):
        return lax.dynamic_slice_in_dim(rows, index * section_width, section_width, axis=1)

    def target_features(rows, xors, base=0):
        return jnp.concatenate(
            [
                lax.dynamic_slice_in_dim(rows, base + (place ^ xor) * target_width, target_width, axis=1)
                for xor in xors
            ],
            axis=1,
        )

    def swap_both(rows, mask):
        count = section_count * seq_count
        pairs = [(source, source ^ (seq_count + mask)) for source in range(count)]
        return lax.ppermute(rows, ("section", "seq"), pairs)

    normed, held["factor"] = normalize(enc_rows, enc_gain)
    partner_rows = swap(normed, "section", 1)

    low, high = max(seq_count // 4, 1), max(seq_count // 2, 1)
    if low > 1:
        gathered = []
        for rows in (normed, partner_rows):
            blocks = [rows]
            bit = 1
            while bit < low:
                blocks = blocks + [swap(block, "seq", bit) for block in blocks]
                bit *= 2
            gathered.append(jnp.concatenate(blocks))
        normed, partner_rows = gathered
    half = normed.shape[0] // 2
    first, second = swap_both(normed, low), swap_both(normed, high)

    base = section * section_width
    outer_far = jnp.concatenate([target_features(rows, (3, 2), base) for rows in (partner_rows, normed)])
    outer_far = swap(outer_far, "dp", 1)
    first, second, outer_far = tie(first, second, outer_far)

    third_top, third_bottom = swap(first[:half], "seq", high), swap(second[half:], "seq", low)
    early = jnp.concatenate([partner_rows, first, second])
    away_early = swap(section_features(early[2 * half :], 1 - section), "section", 1)
    value_early = jnp.dot(early, value_weight, preferred_element_type=F32).astype(BF16)
    key_early = jnp.dot(early, key_weight, preferred_element_type=F32).astype(BF16)
    key_early, value_early, away_early, third_top, third_bottom, outer_far = tie(
        key_early, value_early, away_early, third_top, third_bottom, outer_far
    )
    held["first"], held["second"] = swap(outer_far, "seq", low), swap(outer_far, "seq", high)
    late = jnp.concatenate([third_top, third_bottom])
    away_late = swap(section_features(late, 1 - section), "section", 1)
    key_late = jnp.dot(late, key_weight, preferred_element_type=F32).astype(BF16)
    value_late = jnp.dot(late, value_weight, preferred_element_type=F32).astype(BF16)

    block_start = (seq ^ jnp.arange(seq_count, dtype=jnp.int32)) * own_rows
    positions = block_start[:, None] + jnp.arange(own_rows, dtype=jnp.int32)[None, :]
    visible = (positions.reshape(src_rows, 1) < lengths[partner]).astype(jnp.int32)

    held["key_early"] = key_early

    def attend(head):
        held[f"attended{head}"], held[f"query{head}"], held[f"kv{head}"] = attend_head(
            head, visible, queries[0], held["key_early"], key_late, value_early, value_late, out_grad[0]
        )

    def hand_in(head):
        if head < heads_here:
            held[f"handed{head}"] = swap(held[f"kv{head}"], "dp", 1)

    def exchange(group):
        theirs = swap(jnp.stack([held[f"kv{head}"] for head in group]), "section", 1)
        for slot, head in enumerate(group):
            held[f"their{head}"] = theirs[slot]

    attend(0)
    hand_in(0)
    exchange((0,))
    chip_rows = jnp.concatenate(
        [section_features(early, section), section_features(late, section)]
        + [section_features(normed, section), away_early, away_late]
    )
    held["chip_far"] = target_features(chip_rows, (2, 3))
    held["chip_pair"] = target_features(chip_rows, (1,))
    held["chip_own"] = target_features(chip_rows, (0,))
    sync("first", "second", "key_early", "chip_far", "chip_pair", "chip_own")
    quarter_rows = outer_far.shape[0] // 2
    held["top"] = swap(held["first"][:quarter_rows], "seq", high)
    held["bottom"] = swap(held["second"][quarter_rows:], "seq", low)
    for head in heads[1:]:
        attend(head)
    hand_in(1)
    early_pieces = [outer_far, held["first"], held["second"]]
    held["mine"] = jnp.concatenate([piece[:quarter_rows] for piece in early_pieces])
    held["yours"] = jnp.concatenate([piece[quarter_rows:] for piece in early_pieces])
    sync(
        "handed0", "their0", "top", "bottom", "mine", "yours",
        *(f"kv{head}" for head in heads),
    )

    def chip_sum(name, head):
        rows = held[name]
        return dot(rows[:src_rows], held[f"kv{head}"], 0, 0) + dot(rows[src_rows:], held[f"their{head}"], 0, 0)

    def outer_sum(head):
        handed, handed_other = held[f"handed{head}"], held[f"other{head}"]
        cut = 3 * quarter_rows
        return (
            dot(held["mine"], handed[:cut], 0, 0)
            + dot(held["yours"], handed_other[:cut], 0, 0)
            + dot(held["top"], handed[cut:], 0, 0)
            + dot(held["bottom"], handed_other[cut:], 0, 0)
        )

    def send_rows(steps):
        for step in steps:
            if f"row{step}" not in held:
                rows = held["row_term"][step * own_rows : (step + 1) * own_rows]
                held[f"row{step}"] = swap(rows, "seq", step)

    def relay(group):
        terms = [held[f"pair{head}"] + held[f"outward{head}"].astype(F32) for head in group]
        terms = swap(jnp.concatenate([term.astype(BF16) for term in terms], axis=1), "dp", 1)
        for slot, head in enumerate(group):
            held[f"relay{head}"] = terms[:, slot * 2 * HD : (slot + 1) * 2 * HD]

    def finish(head):
        totals = [held.get(f"total{kind}") for kind in (0, 1)]
        held["total0"], held["total1"] = add_columns(
            totals, head, heads_here, held[f"own{head}"], held[f"inner{head}"], held[f"relay{head}"]
        )

    row_names = [f"row{step}" for step in range(1, seq_count)]
    held["near0"] = chip_sum("chip_far", 0)
    held["other0"] = swap(held["handed0"], "section", 1)
    for head in heads:
        held["far"] = (held[f"near{head}"] + outer_sum(head)).astype(BF16)
        sync(
            "far",
            f"outward{head - 1}",
            f"inner{head - 2}",
            f"pair{head - 1}",
            f"own{head - 1}",
            f"near{head}",
            "row_term",
            *(f"{kind}{other}" for kind in ("attended", "query") for other in heads if head == min(2, last)),
            *(f"kv{other}" for other in heads),
            *(f"their{other}" for other in heads),
            *((f"handed{head + 1}",) if head > 0 else ()),
        )
        held[f"outward{head}"] = lax.ppermute(held["far"][:target_width], "dp", across)
        if head == last:
            sync("far", f"inner{head - 1}")
        held[f"inner{head}"] = lax.ppermute(held["far"][target_width:], "dp", across)
        if head == 0:
            sync("handed1")
        if head < last:
            held[f"other{head + 1}"] = swap(held[f"handed{head + 1}"], "section", 1)
            sync(
                f"other{head + 1}",
                f"inner{head - 1}",
                *(["row_term"] + row_names[:2] if head == 2 else ()),
                *(f"{kind}{other}" for kind in ("kv", "their") for other in heads),
            )
        if head == 0 and heads_here > 1:
            exchange(heads[1:])
        hand_in(head + 2)
        held[f"pair{head}"], held[f"own{head}"] = chip_sum("chip_pair", head), chip_sum("chip_own", head)
        if head < last:
            held[f"near{head + 1}"] = chip_sum("chip_far", head + 1)
        if head == min(1, last):
            held["row_term"] = row_product([held[f"kv{other}"] for other in heads], key_weight, value_weight)
            send_rows(range(1, min(3, seq_count)))
        if head == 2:
            relay((0, 1))
            send_rows(range(1, seq_count))
        if head == 3:
            relay((2,))
    send_rows(range(1, seq_count))
    for head in heads[:-1]:
        if f"relay{head}" not in held:
            relay((head,))
        finish(head)
    sync(f"outward{last}", f"relay{last - 1}")
    relay((last,))
    finish(last)

    row_share = held["row_term"][:own_rows].astype(F32)
    for name in row_names:
        row_share = row_share + held[name].astype(F32)
    row_grad = swap(row_share.astype(BF16), "section", 1)
    enc_grad = norm_backward(enc_rows, held["factor"], enc_gain, row_grad)
    return (
        jnp.concatenate([held[f"attended{head}"] for head in heads], axis=1)[None],
        enc_grad[None],
        held["total0"],
        held["total1"],
        jnp.concatenate([held[f"query{head}"] for head in heads], axis=1)[None],
    )


def solution(mesh):
    placed = (
        P(("section", "dp"), "seq", None),
        P(),
        P(None, "seq"),
        P(None, "seq"),
        P(("section", "dp"), None, "seq"),
        P(("section", "dp"), None, "seq"),
        P(),
    )
    return jax.shard_map(
        on_device,
        mesh=mesh,
        in_specs=placed,
        out_specs=(
            P(("section", "dp"), None, "seq"),
            P(("section", "dp"), "seq", None),
            P(("section", "dp"), "seq"),
            P(("section", "dp"), "seq"),
            P(("section", "dp"), None, "seq"),
        ),
        check_vma=False,
    )
```

```python
import functools

import jax
import jax.numpy as jnp
from jax import lax
from jax.experimental import pallas as pl
from jax.experimental.pallas import tpu as pltpu
from jax.sharding import PartitionSpec as P

HD = 256


EPS = 1e-06
NEG_FILL = -1e30
BF16 = jnp.bfloat16
F32 = jnp.float32
FILLS_WAITS = pl.CostEstimate(flops=0, bytes_accessed=0, transcendentals=0)


def swap(value, axis, mask):
    pairs = [(source, source ^ mask) for source in range(lax.axis_size(axis))]
    return lax.ppermute(value, axis, pairs)


def normalize(enc_rows, gain):
    wide_rows = enc_rows.astype(F32)
    factor = lax.rsqrt(jnp.mean(wide_rows * wide_rows, axis=-1, keepdims=True) + EPS)
    return ((wide_rows * factor * gain).astype(BF16), factor)


def norm_backward(enc_rows, factor, gain, row_grad):
    wide_rows = enc_rows.astype(F32)
    scaled = row_grad.astype(F32) * gain
    inner_sum = jnp.mean(scaled * wide_rows, axis=-1, keepdims=True)
    return (factor * scaled - wide_rows * factor * factor * factor * inner_sum).astype(BF16)


def tie(*values):
    return lax.optimization_barrier(values)


def dot(left, right, left_dim, right_dim):
    return lax.dot_general(
        left, right, (((left_dim,), (right_dim,)), ((), ())), preferred_element_type=F32
    )


def attend_kernel(
    visible, query, key_early, key_late, value_early, value_late, upstream, attended, query_grad, kv_grad
):
    score_scale = HD ** (-0.5)
    query_rows, upstream_rows = query[...], upstream[...]
    key_rows = jnp.concatenate([key_early[...], key_late[...]], axis=0)
    value_rows = jnp.concatenate([value_early[...], value_late[...]], axis=0)
    scores = dot(key_rows, query_rows, 1, 1) * score_scale
    scores = jnp.where(visible[...] > 0, scores, NEG_FILL)
    exponent = jnp.exp(scores - jnp.max(scores, axis=0, keepdims=True))
    probability = exponent * (1.0 / jnp.sum(exponent, axis=0, keepdims=True))
    prob_weights = probability.astype(BF16)
    grad_probs = dot(value_rows, upstream_rows, 1, 1)
    inner_sum = jnp.sum(probability * grad_probs, axis=0, keepdims=True)
    grad_scores = (probability * (grad_probs - inner_sum) * score_scale).astype(BF16)
    kv_grad[:, :HD] = dot(grad_scores, query_rows, 1, 0).astype(BF16)
    kv_grad[:, HD:] = dot(prob_weights, upstream_rows, 1, 0).astype(BF16)
    attended[...] = dot(prob_weights, value_rows, 0, 0).astype(BF16)
    query_grad[...] = dot(grad_scores, key_rows, 0, 0).astype(BF16)


def attend_head(head, visible, query, key_early, key_late, value_early, value_late, upstream):
    src_rows, target_rows = visible.shape[0], query.shape[0]
    early, late = key_early.shape[0], key_late.shape[0]

    def column(rows):
        return pl.BlockSpec((rows, HD), lambda step: (0, head))

    def whole(rows, columns):
        return pl.BlockSpec((rows, columns), lambda step: (0, 0))

    return pl.pallas_call(
        attend_kernel,
        grid=(1,),
        in_specs=[
            whole(src_rows, 1),
            column(target_rows),
            column(early),
            column(late),
            column(early),
            column(late),
            column(target_rows),
        ],
        out_specs=[whole(target_rows, HD), whole(target_rows, HD), whole(src_rows, 2 * HD)],
        out_shape=[
            jax.ShapeDtypeStruct((target_rows, HD), BF16),
            jax.ShapeDtypeStruct((target_rows, HD), BF16),
            jax.ShapeDtypeStruct((src_rows, 2 * HD), BF16),
        ],
        compiler_params=pltpu.CompilerParams(vmem_limit_bytes=48 * 1024 * 1024),
        cost_estimate=FILLS_WAITS,
    )(visible, query, key_early, key_late, value_early, value_late, upstream)


def row_kernel(head_count, *refs):
    grads, (key_block, value_block), out = refs[:head_count], refs[head_count : head_count + 2], refs[-1]
    key_grads = jnp.concatenate([grad[:, :HD] for grad in grads], axis=1)
    value_grads = jnp.concatenate([grad[:, HD:] for grad in grads], axis=1)
    out[...] = (dot(key_grads, key_block[...], 1, 1) + dot(value_grads, value_block[...], 1, 1)).astype(BF16)


def row_product(grads, key_weight, value_weight, part, parts):
    rows, columns = grads[0].shape
    features, heads_width = key_weight.shape
    block = 512
    steps = features // block // parts
    first = part * steps
    whole = pl.BlockSpec((rows, columns), lambda step: (0, 0))
    weight = pl.BlockSpec((block, heads_width), lambda step: (first + step, 0))
    return pl.pallas_call(
        functools.partial(row_kernel, len(grads)),
        grid=(steps,),
        in_specs=[whole] * len(grads) + [weight, weight],
        out_specs=pl.BlockSpec((rows, block), lambda step: (0, step)),
        out_shape=jax.ShapeDtypeStruct((rows, features // parts), BF16),
        compiler_params=pltpu.CompilerParams(vmem_limit_bytes=40 * 1024 * 1024),
        cost_estimate=pl.CostEstimate(
            flops=4 * rows * features * heads_width // parts,
            bytes_accessed=(4 * features * heads_width + 2 * rows * (features + 2 * heads_width)) // parts,
            transcendentals=0,
        ),
    )(*grads, key_weight, value_weight)


def add_kernel(kind_count, local, first, second, *refs):
    outs = refs[-kind_count:]
    total = local[...] + first[...].astype(F32) + second[...].astype(F32)
    for slot, out in enumerate(outs):
        out[...] = total[:, slot * HD : (slot + 1) * HD]


def add_columns(totals, head, heads_here, local, first, second):
    rows, columns = local.shape
    here = pl.BlockSpec((rows, columns), lambda step: (0, 0))
    kept = [total for total in totals if total is not None]
    count = columns // HD
    return pl.pallas_call(
        functools.partial(add_kernel, count),
        grid=(1,),
        in_specs=[here] * 3 + [pl.BlockSpec(memory_space=pl.ANY)] * len(kept),
        out_specs=[pl.BlockSpec((rows, HD), lambda step: (0, head))] * count,
        out_shape=[jax.ShapeDtypeStruct((rows, heads_here * HD), F32)] * count,
        input_output_aliases={3 + slot: slot for slot in range(len(kept))},
        cost_estimate=pl.CostEstimate(
            flops=2 * rows * columns, bytes_accessed=12 * rows * columns, transcendentals=0
        ),
        compiler_params=pltpu.CompilerParams(vmem_limit_bytes=32 * 1024 * 1024),
    )(local, first, second, *kept)


def on_device(enc_states, enc_gain, key_weight, value_weight, queries, out_grad, lengths):
    enc_rows = enc_states[0]
    own_rows, width = enc_rows.shape
    heads_here = key_weight.shape[1] // HD
    heads = range(heads_here)
    last = heads_here - 1
    section_count, dp_count, seq_count = (lax.axis_size(name) for name in ("section", "dp", "seq"))
    section, place, seq = (lax.axis_index(name) for name in ("section", "dp", "seq"))
    partner = (section * dp_count + place + dp_count) % (section_count * dp_count)
    src_rows = own_rows * seq_count
    section_width = width // section_count
    target_width = section_width // dp_count
    across = [(0, 0), (1, 2), (2, 1), (3, 3)]
    inner_chip = (place == 1) | (place == 2)
    held = {}

    def sync(*names):
        names = ["factor"] + [name for name in names if name in held]
        held.update(zip(names, lax.optimization_barrier(tuple(held[name] for name in names))))

    def section_features(rows, index):
        return lax.dynamic_slice_in_dim(rows, index * section_width, section_width, axis=1)

    def target_features(rows, xors, base=0):
        return jnp.concatenate(
            [
                lax.dynamic_slice_in_dim(rows, base + (place ^ xor) * target_width, target_width, axis=1)
                for xor in xors
            ],
            axis=1,
        )

    def swap_both(rows, mask):
        count = section_count * seq_count
        pairs = [(source, source ^ (seq_count + mask)) for source in range(count)]
        return lax.ppermute(rows, ("section", "seq"), pairs)

    normed, held["factor"] = normalize(enc_rows, enc_gain)
    partner_rows = swap(normed, "section", 1)

    low, high = max(seq_count // 4, 1), max(seq_count // 2, 1)
    if low > 1:
        gathered = []
        for rows in (normed, partner_rows):
            blocks = [rows]
            bit = 1
            while bit < low:
                blocks = blocks + [swap(block, "seq", bit) for block in blocks]
                bit *= 2
            gathered.append(jnp.concatenate(blocks))
        normed, partner_rows = gathered
    half = normed.shape[0] // 2
    first, second = swap_both(normed, low), swap_both(normed, high)

    base = section * section_width
    outer_far = jnp.concatenate([target_features(rows, (3, 2), base) for rows in (partner_rows, normed)])
    outer_far = swap(outer_far, "dp", 1)
    first, second, outer_far = tie(first, second, outer_far)

    third_top, third_bottom = swap(first[:half], "seq", high), swap(second[half:], "seq", low)
    early = jnp.concatenate([partner_rows, first, second])
    away_early = swap(section_features(early[2 * half :], 1 - section), "section", 1)
    value_early = jnp.dot(early, value_weight, preferred_element_type=F32).astype(BF16)
    key_early = jnp.dot(early, key_weight, preferred_element_type=F32).astype(BF16)
    key_early, value_early, away_early, third_top, third_bottom, outer_far = tie(
        key_early, value_early, away_early, third_top, third_bottom, outer_far
    )
    held["first"], held["second"] = swap(outer_far, "seq", low), swap(outer_far, "seq", high)
    late = jnp.concatenate([third_top, third_bottom])
    away_late = swap(section_features(late, 1 - section), "section", 1)
    key_late = jnp.dot(late, key_weight, preferred_element_type=F32).astype(BF16)
    value_late = jnp.dot(late, value_weight, preferred_element_type=F32).astype(BF16)

    block_start = (seq ^ jnp.arange(seq_count, dtype=jnp.int32)) * own_rows
    positions = block_start[:, None] + jnp.arange(own_rows, dtype=jnp.int32)[None, :]
    visible = (positions.reshape(src_rows, 1) < lengths[partner]).astype(jnp.int32)

    held["key_early"] = key_early

    def attend(head):
        held[f"attended{head}"], held[f"query{head}"], held[f"kv{head}"] = attend_head(
            head, visible, queries[0], held["key_early"], key_late, value_early, value_late, out_grad[0]
        )

    def hand_in(head):
        if head < heads_here:
            held[f"handed{head}"] = swap(held[f"kv{head}"], "dp", 1)

    def exchange(head):
        held[f"their{head}"] = swap(held[f"kv{head}"], "section", 1)

    attend(0)
    hand_in(0)
    exchange(0)
    chip_rows = jnp.concatenate(
        [section_features(early, section), section_features(late, section)]
        + [section_features(normed, section), away_early, away_late]
    )
    held["chip_far"] = target_features(chip_rows, (2, 3))
    held["chip_pair"] = target_features(chip_rows, (1,))
    held["chip_own"] = target_features(chip_rows, (0,))
    sync("first", "second", "key_early", "chip_far", "chip_pair", "chip_own")
    quarter_rows = outer_far.shape[0] // 2
    held["top"] = swap(held["first"][:quarter_rows], "seq", high)
    held["bottom"] = swap(held["second"][quarter_rows:], "seq", low)
    if heads_here > 1:
        attend(1)
        exchange(1)
    hand_in(1)
    early_pieces = [outer_far, held["first"], held["second"]]
    held["mine"] = jnp.concatenate([piece[:quarter_rows] for piece in early_pieces])
    held["yours"] = jnp.concatenate([piece[quarter_rows:] for piece in early_pieces])
    sync(
        "handed0", "their0", "top", "bottom", "mine", "yours",
        *(f"kv{head}" for head in heads[:2]),
    )

    def chip_sum(name, head):
        rows = held[name]
        return dot(rows[:src_rows], held[f"kv{head}"], 0, 0) + dot(rows[src_rows:], held[f"their{head}"], 0, 0)

    def outer_sum(head):
        handed, handed_other = held[f"handed{head}"], held[f"other{head}"]
        cut = 3 * quarter_rows
        return (
            dot(held["mine"], handed[:cut], 0, 0)
            + dot(held["yours"], handed_other[:cut], 0, 0)
            + dot(held["top"], handed[cut:], 0, 0)
            + dot(held["bottom"], handed_other[cut:], 0, 0)
        )

    def row_block(step):
        block = slice(step * own_rows, (step + 1) * own_rows)
        return jnp.concatenate([held["row_low"][block], held["row_high"][block]], axis=1)

    def send_rows(steps):
        for step in steps:
            if f"row{step}" not in held:
                held[f"row{step}"] = swap(row_block(step), "seq", step)

    def relay(head):
        term = chip_sum("chip_pair", head) + held[f"outward{head}"].astype(F32)
        held[f"relay{head}"] = swap(term.astype(BF16), "dp", 1)

    def finish(head):
        totals = [held.get(f"total{kind}") for kind in (0, 1)]
        held["total0"], held["total1"] = add_columns(
            totals, head, heads_here, chip_sum("chip_own", head), held[f"inner{head}"], held[f"relay{head}"]
        )

    row_names = [f"row{step}" for step in range(1, seq_count)]
    held["near0"] = chip_sum("chip_far", 0)
    held["other0"] = swap(held["handed0"], "section", 1)
    def kinds(*names):
        return [f"{name}{other}" for name in names for other in heads]

    for head in heads:
        held["far"] = jnp.where(inner_chip, held[f"near{head}"] + outer_sum(head), 0.0).astype(BF16)
        sync(
            "far",
            "key_early",
            f"outward{head - 1}",
            f"inner{head - 2}",
            f"near{head}",
            f"relay{head - 2}",
            "row_low",
            "row_high",
            *kinds("kv", "their"),
            *((f"handed{head + 1}",) if head > 0 else ()),
            *(kinds("attended", "query") if head == min(2, last) else ()),
        )
        held[f"outward{head}"] = lax.ppermute(held["far"][:target_width], "dp", across)
        if head == last:
            sync("far", f"inner{head - 1}")
        held[f"inner{head}"] = lax.ppermute(held["far"][target_width:], "dp", across)
        if head == 0:
            for other in heads[2:]:
                attend(other)
                exchange(other)
        hand_in(head + 2)
        if head < last:
            if head == 0:
                held["near1"] = chip_sum("chip_far", 1)
                grads = [held[f"kv{other}"] for other in heads]
                held["row_low"] = row_product(grads, key_weight, value_weight, 0, 2)
                sync("outward0", "handed1", "near1")
            held[f"other{head + 1}"] = swap(held[f"handed{head + 1}"], "section", 1)
            if head > 0:
                sync(
                    f"other{head + 1}",
                    f"inner{head - 1}",
                    *(["row_low", "row_high"] + row_names[:2] if head == 2 else ()),
                    *kinds("kv", "their"),
                )
                held[f"near{head + 1}"] = chip_sum("chip_far", head + 1)
        if head == 1:
            relay(0)
            grads = [held[f"kv{other}"] for other in heads]
            held["row_high"] = row_product(grads, key_weight, value_weight, 1, 2)
            send_rows(range(1, min(3, seq_count)))
        if head == 2:
            relay(1)
            send_rows(range(1, seq_count))
        if head == 3:
            relay(2)
    if heads_here == 1:
        held["row_low"] = row_product([held["kv0"]], key_weight, value_weight, 0, 2)
        held["row_high"] = row_product([held["kv0"]], key_weight, value_weight, 1, 2)
    send_rows(range(1, seq_count))
    for head in heads[:-1]:
        if f"relay{head}" not in held:
            relay(head)
        finish(head)
    sync(f"outward{last}", f"relay{last - 1}")
    relay(last)
    finish(last)

    row_share = row_block(0).astype(F32)
    for name in row_names:
        row_share = row_share + held[name].astype(F32)
    row_grad = swap(row_share.astype(BF16), "section", 1)
    enc_grad = norm_backward(enc_rows, held["factor"], enc_gain, row_grad)
    return (
        jnp.concatenate([held[f"attended{head}"] for head in heads], axis=1)[None],
        enc_grad[None],
        held["total0"],
        held["total1"],
        jnp.concatenate([held[f"query{head}"] for head in heads], axis=1)[None],
    )


def solution(mesh):
    placed = (
        P(("section", "dp"), "seq", None),
        P(),
        P(None, "seq"),
        P(None, "seq"),
        P(("section", "dp"), None, "seq"),
        P(("section", "dp"), None, "seq"),
        P(),
    )
    return jax.shard_map(
        on_device,
        mesh=mesh,
        in_specs=placed,
        out_specs=(
            P(("section", "dp"), None, "seq"),
            P(("section", "dp"), "seq", None),
            P(("section", "dp"), "seq"),
            P(("section", "dp"), "seq"),
            P(("section", "dp"), None, "seq"),
        ),
        check_vma=False,
    )
```

```python
import functools

import jax
import jax.numpy as jnp
from jax import lax
from jax.experimental import pallas as pl
from jax.experimental.pallas import tpu as pltpu
from jax.sharding import PartitionSpec as P

HD = 256


EPS = 1e-06
NEG_FILL = -1e30
BF16 = jnp.bfloat16
F32 = jnp.float32
MIB = 1024 * 1024
FILLS_WAITS = pl.CostEstimate(flops=0, bytes_accessed=0, transcendentals=0)


def swap(value, axis, mask):
    pairs = [(source, source ^ mask) for source in range(lax.axis_size(axis))]
    return lax.ppermute(value, axis, pairs)


def normalize(enc_rows, gain):
    wide_rows = enc_rows.astype(F32)
    factor = lax.rsqrt(jnp.mean(wide_rows * wide_rows, axis=-1, keepdims=True) + EPS)
    return ((wide_rows * factor * gain).astype(BF16), factor)


def norm_backward(enc_rows, factor, gain, row_grad):
    wide_rows = enc_rows.astype(F32)
    scaled = row_grad.astype(F32) * gain
    inner_sum = jnp.mean(scaled * wide_rows, axis=-1, keepdims=True)
    return (factor * scaled - wide_rows * factor * factor * factor * inner_sum).astype(BF16)


def tie(*values):
    return lax.optimization_barrier(values)


def dot(left, right, left_dim, right_dim):
    return lax.dot_general(
        left, right, (((left_dim,), (right_dim,)), ((), ())), preferred_element_type=F32
    )


def attend_kernel(
    visible, query, key_early, key_late, value_early, value_late, upstream, attended, query_grad, kv_grad
):
    score_scale = HD ** (-0.5)
    query_rows, upstream_rows = query[...], upstream[...]
    key_rows = jnp.concatenate([key_early[...], key_late[...]], axis=0)
    value_rows = jnp.concatenate([value_early[...], value_late[...]], axis=0)
    scores = dot(key_rows, query_rows, 1, 1) * score_scale
    scores = jnp.where(visible[...] > 0, scores, NEG_FILL)
    exponent = jnp.exp(scores - jnp.max(scores, axis=0, keepdims=True))
    probability = exponent * (1.0 / jnp.sum(exponent, axis=0, keepdims=True))
    prob_weights = probability.astype(BF16)
    grad_probs = dot(value_rows, upstream_rows, 1, 1)
    inner_sum = jnp.sum(probability * grad_probs, axis=0, keepdims=True)
    grad_scores = (probability * (grad_probs - inner_sum) * score_scale).astype(BF16)
    kv_grad[:, :HD] = dot(grad_scores, query_rows, 1, 0).astype(BF16)
    kv_grad[:, HD:] = dot(prob_weights, upstream_rows, 1, 0).astype(BF16)
    attended[...] = dot(prob_weights, value_rows, 0, 0).astype(BF16)
    query_grad[...] = dot(grad_scores, key_rows, 0, 0).astype(BF16)


def attend_head(head, visible, query, key_early, key_late, value_early, value_late, upstream):
    src_rows, target_rows = visible.shape[0], query.shape[0]
    early, late = key_early.shape[0], key_late.shape[0]

    def column(rows):
        return pl.BlockSpec((rows, HD), lambda step: (0, head))

    def whole(rows, columns):
        return pl.BlockSpec((rows, columns), lambda step: (0, 0))

    return pl.pallas_call(
        attend_kernel,
        grid=(1,),
        in_specs=[
            whole(src_rows, 1),
            column(target_rows),
            column(early),
            column(late),
            column(early),
            column(late),
            column(target_rows),
        ],
        out_specs=[whole(target_rows, HD), whole(target_rows, HD), whole(src_rows, 2 * HD)],
        out_shape=[
            jax.ShapeDtypeStruct((target_rows, HD), BF16),
            jax.ShapeDtypeStruct((target_rows, HD), BF16),
            jax.ShapeDtypeStruct((src_rows, 2 * HD), BF16),
        ],
        compiler_params=pltpu.CompilerParams(vmem_limit_bytes=6 * MIB + 40 * src_rows * target_rows),
        cost_estimate=FILLS_WAITS,
    )(visible, query, key_early, key_late, value_early, value_late, upstream)


def row_kernel(head_count, *refs):
    grads, (key_block, value_block), out = refs[:head_count], refs[head_count : head_count + 2], refs[-1]
    key_grads = jnp.concatenate([grad[:, :HD] for grad in grads], axis=1)
    value_grads = jnp.concatenate([grad[:, HD:] for grad in grads], axis=1)
    out[...] = (dot(key_grads, key_block[...], 1, 1) + dot(value_grads, value_block[...], 1, 1)).astype(BF16)


def row_product(grads, key_weight, value_weight, part, parts):
    rows, columns = grads[0].shape
    features, heads_width = key_weight.shape
    block = 512
    steps = features // block // parts
    first = part * steps
    whole = pl.BlockSpec((rows, columns), lambda step: (0, 0))
    weight = pl.BlockSpec((block, heads_width), lambda step: (first + step, 0))
    return pl.pallas_call(
        functools.partial(row_kernel, len(grads)),
        grid=(steps,),
        in_specs=[whole] * len(grads) + [weight, weight],
        out_specs=pl.BlockSpec((rows, block), lambda step: (0, step)),
        out_shape=jax.ShapeDtypeStruct((rows, features // parts), BF16),
        compiler_params=pltpu.CompilerParams(vmem_limit_bytes=14 * MIB + 12 * rows * block),
        cost_estimate=pl.CostEstimate(
            flops=4 * rows * features * heads_width // parts,
            bytes_accessed=(4 * features * heads_width + 2 * rows * (features + 2 * heads_width)) // parts,
            transcendentals=0,
        ),
    )(*grads, key_weight, value_weight)


def add_kernel(kind_count, local, first, second, *refs):
    outs = refs[-kind_count:]
    total = local[...] + first[...].astype(F32) + second[...].astype(F32)
    for slot, out in enumerate(outs):
        out[...] = total[:, slot * HD : (slot + 1) * HD]


def add_columns(totals, head, heads_here, local, first, second):
    rows, columns = local.shape
    here = pl.BlockSpec((rows, columns), lambda step: (0, 0))
    kept = [total for total in totals if total is not None]
    count = columns // HD
    return pl.pallas_call(
        functools.partial(add_kernel, count),
        grid=(1,),
        in_specs=[here] * 3 + [pl.BlockSpec(memory_space=pl.ANY)] * len(kept),
        out_specs=[pl.BlockSpec((rows, HD), lambda step: (0, head))] * count,
        out_shape=[jax.ShapeDtypeStruct((rows, heads_here * HD), F32)] * count,
        input_output_aliases={3 + slot: slot for slot in range(len(kept))},
        cost_estimate=pl.CostEstimate(
            flops=2 * rows * columns, bytes_accessed=12 * rows * columns, transcendentals=0
        ),
        compiler_params=pltpu.CompilerParams(vmem_limit_bytes=12 * MIB),
    )(local, first, second, *kept)


def on_device(enc_states, enc_gain, key_weight, value_weight, queries, out_grad, lengths):
    enc_rows = enc_states[0]
    own_rows, width = enc_rows.shape
    heads_here = key_weight.shape[1] // HD
    heads = range(heads_here)
    last = heads_here - 1
    section_count, dp_count, seq_count = (lax.axis_size(name) for name in ("section", "dp", "seq"))
    section, place, seq = (lax.axis_index(name) for name in ("section", "dp", "seq"))
    partner = (section * dp_count + place + dp_count) % (section_count * dp_count)
    src_rows = own_rows * seq_count
    section_width = width // section_count
    target_width = section_width // dp_count
    across = [(1, 2), (2, 1)]
    held = {}

    def sync(*names):
        names = ["factor"] + [name for name in names if name in held]
        held.update(zip(names, lax.optimization_barrier(tuple(held[name] for name in names))))

    def section_features(rows, index):
        return lax.dynamic_slice_in_dim(rows, index * section_width, section_width, axis=1)

    def target_features(rows, xors, base=0):
        return jnp.concatenate(
            [
                lax.dynamic_slice_in_dim(rows, base + (place ^ xor) * target_width, target_width, axis=1)
                for xor in xors
            ],
            axis=1,
        )

    def swap_both(rows, mask):
        count = section_count * seq_count
        pairs = [(source, source ^ (seq_count + mask)) for source in range(count)]
        return lax.ppermute(rows, ("section", "seq"), pairs)

    normed, held["factor"] = normalize(enc_rows, enc_gain)
    partner_rows = swap(normed, "section", 1)

    low, high = max(seq_count // 4, 1), max(seq_count // 2, 1)
    if low > 1:
        gathered = []
        for rows in (normed, partner_rows):
            blocks = [rows]
            bit = 1
            while bit < low:
                blocks = blocks + [swap(block, "seq", bit) for block in blocks]
                bit *= 2
            gathered.append(jnp.concatenate(blocks))
        normed, partner_rows = gathered
    half = normed.shape[0] // 2
    first, second = swap_both(normed, low), swap_both(normed, high)

    base = section * section_width
    outer_far = jnp.concatenate([target_features(rows, (3, 2), base) for rows in (partner_rows, normed)])
    outer_far = swap(outer_far, "dp", 1)
    first, second, outer_far = tie(first, second, outer_far)

    third_top, third_bottom = swap(first[:half], "seq", high), swap(second[half:], "seq", low)
    early = jnp.concatenate([partner_rows, first, second])
    away_early = swap(section_features(early[2 * half :], 1 - section), "section", 1)
    value_early = jnp.dot(early, value_weight, preferred_element_type=F32).astype(BF16)
    key_early = jnp.dot(early, key_weight, preferred_element_type=F32).astype(BF16)
    key_early, value_early, away_early, third_top, third_bottom, outer_far = tie(
        key_early, value_early, away_early, third_top, third_bottom, outer_far
    )
    held["first"], held["second"] = swap(outer_far, "seq", low), swap(outer_far, "seq", high)
    late = jnp.concatenate([third_top, third_bottom])
    away_late = swap(section_features(late, 1 - section), "section", 1)
    key_late = jnp.dot(late, key_weight, preferred_element_type=F32).astype(BF16)
    value_late = jnp.dot(late, value_weight, preferred_element_type=F32).astype(BF16)

    block_start = (seq ^ jnp.arange(seq_count, dtype=jnp.int32)) * own_rows
    positions = block_start[:, None] + jnp.arange(own_rows, dtype=jnp.int32)[None, :]
    visible = (positions.reshape(src_rows, 1) < lengths[partner]).astype(jnp.int32)

    held["key_early"] = key_early

    def attend(head):
        held[("attended", head)], held[("query", head)], held[("kv", head)] = attend_head(
            head, visible, queries[0], held["key_early"], key_late, value_early, value_late, out_grad[0]
        )

    def hand_in(head):
        if head < heads_here:
            held[("handed", head)] = swap(held[("kv", head)], "dp", 1)

    def exchange(head):
        held[("their", head)] = swap(held[("kv", head)], "section", 1)

    attend(0)
    hand_in(0)
    exchange(0)
    chip_rows = jnp.concatenate(
        [section_features(early, section), section_features(late, section)]
        + [section_features(normed, section), away_early, away_late]
    )
    held["chip_far"] = target_features(chip_rows, (2, 3))
    held["chip_pair"] = target_features(chip_rows, (1,))
    held["chip_own"] = target_features(chip_rows, (0,))
    sync("first", "second", "key_early", "chip_far", "chip_pair", "chip_own")
    quarter_rows = outer_far.shape[0] // 2
    held["top"] = swap(held["first"][:quarter_rows], "seq", high)
    held["bottom"] = swap(held["second"][quarter_rows:], "seq", low)
    for head in heads[1:]:
        attend(head)
        exchange(head)
    hand_in(1)
    early_pieces = [outer_far, held["first"], held["second"]]
    held["mine"] = jnp.concatenate([piece[:quarter_rows] for piece in early_pieces])
    held["yours"] = jnp.concatenate([piece[quarter_rows:] for piece in early_pieces])
    sync(
        ("handed", 0), ("their", 0), "top", "bottom", "mine", "yours",
        *(("kv", head) for head in heads),
    )

    def chip_sum(name, head):
        rows = held[name]
        return dot(rows[:src_rows], held[("kv", head)], 0, 0) + dot(rows[src_rows:], held[("their", head)], 0, 0)

    def outer_sum(head):
        handed, handed_other = held[("handed", head)], held[("other", head)]
        cut = 3 * quarter_rows
        return (
            dot(held["mine"], handed[:cut], 0, 0)
            + dot(held["yours"], handed_other[:cut], 0, 0)
            + dot(held["top"], handed[cut:], 0, 0)
            + dot(held["bottom"], handed_other[cut:], 0, 0)
        )

    def row_block(step):
        block = slice(step * own_rows, (step + 1) * own_rows)
        return jnp.concatenate([held["row_low"][block], held["row_high"][block]], axis=1)

    def send_rows(steps):
        for step in steps:
            if ("row", step) not in held:
                held[("row", step)] = swap(row_block(step), "seq", step)

    def relay(head):
        term = chip_sum("chip_pair", head) + held[("outward", head)].astype(F32)
        held[("relay", head)] = swap(term.astype(BF16), "dp", 1)

    def finish(head):
        totals = [held.get(("total", kind)) for kind in (0, 1)]
        held[("total", 0)], held[("total", 1)] = add_columns(
            totals, head, heads_here, chip_sum("chip_own", head), held[("inner", head)], held[("relay", head)]
        )

    row_names = [("row", step) for step in range(1, seq_count)]
    held[("near", 0)] = chip_sum("chip_far", 0)
    held[("other", 0)] = swap(held[("handed", 0)], "section", 1)
    def kinds(*names):
        return [(name, other) for name in names for other in heads]

    for head in heads:
        held["far"] = (held[("near", head)] + outer_sum(head)).astype(BF16)
        sync(
            "far",
            "key_early",
            ("outward", head - 1),
            ("inner", head - 2),
            ("near", head),
            ("relay", head - 2),
            "row_low",
            "row_high",
            *(row_names[:2] if head == 3 else ()),
            *kinds("kv", "their"),
            *((("handed", head + 1),) if head > 0 else ()),
            *(kinds("attended", "query") if head == min(2, last) else ()),
        )
        held[("outward", head)] = lax.ppermute(held["far"][:target_width], "dp", across)
        if head == last:
            sync("far", ("inner", head - 1))
        held[("inner", head)] = lax.ppermute(held["far"][target_width:], "dp", across)
        hand_in(head + 2)
        if head < last:
            if head == 0:
                grads = [held[("kv", other)] for other in heads]
                held["row_low"] = row_product(grads, key_weight, value_weight, 0, 2)
                sync(("outward", 0), ("handed", 1), *kinds("their"))
                held[("near", 1)] = chip_sum("chip_far", 1)
            held[("other", head + 1)] = swap(held[("handed", head + 1)], "section", 1)
            if head > 0:
                sync(
                    ("other", head + 1),
                    ("inner", head - 1),
                    *kinds("kv", "their"),
                )
                held[("near", head + 1)] = chip_sum("chip_far", head + 1)
        if head == 1:
            relay(0)
            grads = [held[("kv", other)] for other in heads]
            held["row_high"] = row_product(grads, key_weight, value_weight, 1, 2)
            send_rows(range(1, min(3, seq_count)))
        if head == 2:
            relay(1)
        if head == 3:
            relay(2)
            send_rows(range(1, seq_count))
    if heads_here == 1:
        held["row_low"] = row_product([held[("kv", 0)]], key_weight, value_weight, 0, 2)
        held["row_high"] = row_product([held[("kv", 0)]], key_weight, value_weight, 1, 2)
    send_rows(range(1, seq_count))
    for head in heads[:-1]:
        if ("relay", head) not in held:
            relay(head)
        finish(head)
    sync(("outward", last), ("relay", last - 1))
    relay(last)
    finish(last)

    row_share = row_block(0).astype(F32)
    for name in row_names:
        row_share = row_share + held[name].astype(F32)
    row_grad = swap(row_share.astype(BF16), "section", 1)
    enc_grad = norm_backward(enc_rows, held["factor"], enc_gain, row_grad)
    return (
        jnp.concatenate([held[("attended", head)] for head in heads], axis=1)[None],
        enc_grad[None],
        held[("total", 0)],
        held[("total", 1)],
        jnp.concatenate([held[("query", head)] for head in heads], axis=1)[None],
    )


def solution(mesh):
    placed = (
        P(("section", "dp"), "seq", None),
        P(),
        P(None, "seq"),
        P(None, "seq"),
        P(("section", "dp"), None, "seq"),
        P(("section", "dp"), None, "seq"),
        P(),
    )
    return jax.shard_map(
        on_device,
        mesh=mesh,
        in_specs=placed,
        out_specs=(
            P(("section", "dp"), None, "seq"),
            P(("section", "dp"), "seq", None),
            P(("section", "dp"), "seq"),
            P(("section", "dp"), "seq"),
            P(("section", "dp"), None, "seq"),
        ),
        check_vma=False,
    )
```

```python
import functools

import jax
import jax.numpy as jnp
from jax import lax
from jax.experimental import pallas as pl
from jax.experimental.pallas import tpu as pltpu
from jax.sharding import PartitionSpec as P

HD = 256


EPS = 1e-06
NEG_FILL = -1e30
BF16 = jnp.bfloat16
F32 = jnp.float32
MIB = 1024 * 1024
FILLS_WAITS = pl.CostEstimate(flops=0, bytes_accessed=0, transcendentals=0)


def swap(value, axis, mask):
    pairs = [(source, source ^ mask) for source in range(lax.axis_size(axis))]
    return lax.ppermute(value, axis, pairs)


def normalize(enc_rows, gain):
    wide_rows = enc_rows.astype(F32)
    factor = lax.rsqrt(jnp.mean(wide_rows * wide_rows, axis=-1, keepdims=True) + EPS)
    return ((wide_rows * factor * gain).astype(BF16), factor)


def norm_backward(enc_rows, factor, gain, row_grad):
    wide_rows = enc_rows.astype(F32)
    scaled = row_grad.astype(F32) * gain
    inner_sum = jnp.mean(scaled * wide_rows, axis=-1, keepdims=True)
    return (factor * scaled - wide_rows * factor * factor * factor * inner_sum).astype(BF16)


def tie(*values):
    return lax.optimization_barrier(values)


def dot(left, right, left_dim, right_dim):
    return lax.dot_general(
        left, right, (((left_dim,), (right_dim,)), ((), ())), preferred_element_type=F32
    )


def attend_kernel(
    visible, query, key_early, key_late, value_early, value_late, upstream, attended, query_grad, kv_grad
):
    score_scale = HD ** (-0.5)
    query_rows, upstream_rows = query[...], upstream[...]
    key_rows = jnp.concatenate([key_early[...], key_late[...]], axis=0)
    value_rows = jnp.concatenate([value_early[...], value_late[...]], axis=0)
    scores = dot(key_rows, query_rows, 1, 1) * score_scale
    scores = jnp.where(visible[...] > 0, scores, NEG_FILL)
    exponent = jnp.exp(scores - jnp.max(scores, axis=0, keepdims=True))
    probability = exponent * (1.0 / jnp.sum(exponent, axis=0, keepdims=True))
    prob_weights = probability.astype(BF16)
    grad_probs = dot(value_rows, upstream_rows, 1, 1)
    inner_sum = jnp.sum(probability * grad_probs, axis=0, keepdims=True)
    grad_scores = (probability * (grad_probs - inner_sum) * score_scale).astype(BF16)
    kv_grad[:, :HD] = dot(grad_scores, query_rows, 1, 0).astype(BF16)
    kv_grad[:, HD:] = dot(prob_weights, upstream_rows, 1, 0).astype(BF16)
    attended[...] = dot(prob_weights, value_rows, 0, 0).astype(BF16)
    query_grad[...] = dot(grad_scores, key_rows, 0, 0).astype(BF16)


def attend_head(head, visible, query, key_early, key_late, value_early, value_late, upstream):
    src_rows, target_rows = visible.shape[0], query.shape[0]
    early, late = key_early.shape[0], key_late.shape[0]

    def column(rows):
        return pl.BlockSpec((rows, HD), lambda step: (0, head))

    def whole(rows, columns):
        return pl.BlockSpec((rows, columns), lambda step: (0, 0))

    return pl.pallas_call(
        attend_kernel,
        grid=(1,),
        in_specs=[
            whole(src_rows, 1),
            column(target_rows),
            column(early),
            column(late),
            column(early),
            column(late),
            column(target_rows),
        ],
        out_specs=[whole(target_rows, HD), whole(target_rows, HD), whole(src_rows, 2 * HD)],
        out_shape=[
            jax.ShapeDtypeStruct((target_rows, HD), BF16),
            jax.ShapeDtypeStruct((target_rows, HD), BF16),
            jax.ShapeDtypeStruct((src_rows, 2 * HD), BF16),
        ],
        compiler_params=pltpu.CompilerParams(vmem_limit_bytes=6 * MIB + 40 * src_rows * target_rows),
        cost_estimate=FILLS_WAITS,
    )(visible, query, key_early, key_late, value_early, value_late, upstream)


def row_kernel(head_count, *refs):
    grads, (key_block, value_block), out = refs[:head_count], refs[head_count : head_count + 2], refs[-1]
    key_grads = jnp.concatenate([grad[:, :HD] for grad in grads], axis=1)
    value_grads = jnp.concatenate([grad[:, HD:] for grad in grads], axis=1)
    out[...] = (dot(key_grads, key_block[...], 1, 1) + dot(value_grads, value_block[...], 1, 1)).astype(BF16)


def row_product(grads, key_weight, value_weight, part, parts):
    rows, columns = grads[0].shape
    features, heads_width = key_weight.shape
    block = 512
    steps = features // block // parts
    first = part * steps
    whole = pl.BlockSpec((rows, columns), lambda step: (0, 0))
    weight = pl.BlockSpec((block, heads_width), lambda step: (first + step, 0))
    return pl.pallas_call(
        functools.partial(row_kernel, len(grads)),
        grid=(steps,),
        in_specs=[whole] * len(grads) + [weight, weight],
        out_specs=pl.BlockSpec((rows, block), lambda step: (0, step)),
        out_shape=jax.ShapeDtypeStruct((rows, features // parts), BF16),
        compiler_params=pltpu.CompilerParams(vmem_limit_bytes=14 * MIB + 12 * rows * block),
        cost_estimate=pl.CostEstimate(
            flops=4 * rows * features * heads_width // parts,
            bytes_accessed=(4 * features * heads_width + 2 * rows * (features + 2 * heads_width)) // parts,
            transcendentals=0,
        ),
    )(*grads, key_weight, value_weight)


def add_kernel(kind_count, local, first, second, *refs):
    outs = refs[-kind_count:]
    total = local[...] + first[...].astype(F32) + second[...].astype(F32)
    for slot, out in enumerate(outs):
        out[...] = total[:, slot * HD : (slot + 1) * HD]


def add_columns(totals, head, heads_here, local, first, second):
    rows, columns = local.shape
    here = pl.BlockSpec((rows, columns), lambda step: (0, 0))
    kept = [total for total in totals if total is not None]
    count = columns // HD
    return pl.pallas_call(
        functools.partial(add_kernel, count),
        grid=(1,),
        in_specs=[here] * 3 + [pl.BlockSpec(memory_space=pl.ANY)] * len(kept),
        out_specs=[pl.BlockSpec((rows, HD), lambda step: (0, head))] * count,
        out_shape=[jax.ShapeDtypeStruct((rows, heads_here * HD), F32)] * count,
        input_output_aliases={3 + slot: slot for slot in range(len(kept))},
        cost_estimate=pl.CostEstimate(
            flops=2 * rows * columns, bytes_accessed=12 * rows * columns, transcendentals=0
        ),
        compiler_params=pltpu.CompilerParams(vmem_limit_bytes=12 * MIB),
    )(local, first, second, *kept)


def on_device(enc_states, enc_gain, key_weight, value_weight, queries, out_grad, lengths):
    enc_rows = enc_states[0]
    own_rows, width = enc_rows.shape
    heads_here = key_weight.shape[1] // HD
    heads = range(heads_here)
    last = heads_here - 1
    section_count, dp_count, seq_count = (lax.axis_size(name) for name in ("section", "dp", "seq"))
    section, place, seq = (lax.axis_index(name) for name in ("section", "dp", "seq"))
    partner = (section * dp_count + place + dp_count) % (section_count * dp_count)
    src_rows = own_rows * seq_count
    section_width = width // section_count
    target_width = section_width // dp_count
    across = [(1, 2), (2, 1)]
    held = {}

    def sync(*names):
        names = ["factor"] + [name for name in names if name in held]
        held.update(zip(names, lax.optimization_barrier(tuple(held[name] for name in names))))

    def section_features(rows, index):
        return lax.dynamic_slice_in_dim(rows, index * section_width, section_width, axis=1)

    def target_features(rows, xors, base=0):
        return jnp.concatenate(
            [
                lax.dynamic_slice_in_dim(rows, base + (place ^ xor) * target_width, target_width, axis=1)
                for xor in xors
            ],
            axis=1,
        )

    def swap_both(rows, mask):
        count = section_count * seq_count
        pairs = [(source, source ^ (seq_count + mask)) for source in range(count)]
        return lax.ppermute(rows, ("section", "seq"), pairs)

    normed, held["factor"] = normalize(enc_rows, enc_gain)
    partner_rows = swap(normed, "section", 1)

    low, high = max(seq_count // 4, 1), max(seq_count // 2, 1)
    if low > 1:
        gathered = []
        for rows in (normed, partner_rows):
            blocks = [rows]
            bit = 1
            while bit < low:
                blocks = blocks + [swap(block, "seq", bit) for block in blocks]
                bit *= 2
            gathered.append(jnp.concatenate(blocks))
        normed, partner_rows = gathered
    half = normed.shape[0] // 2
    first, second = swap_both(normed, low), swap_both(normed, high)

    base = section * section_width
    outer_far = jnp.concatenate([target_features(rows, (3, 2), base) for rows in (partner_rows, normed)])
    outer_far = swap(outer_far, "dp", 1)
    first, second, outer_far = tie(first, second, outer_far)

    third_top, third_bottom = swap(first[:half], "seq", high), swap(second[half:], "seq", low)
    early = jnp.concatenate([partner_rows, first, second])
    away_early = swap(section_features(early[2 * half :], 1 - section), "section", 1)
    value_early = jnp.dot(early, value_weight, preferred_element_type=F32).astype(BF16)
    key_early = jnp.dot(early, key_weight, preferred_element_type=F32).astype(BF16)
    key_early, value_early, away_early, third_top, third_bottom, outer_far = tie(
        key_early, value_early, away_early, third_top, third_bottom, outer_far
    )
    held["first"], held["second"] = swap(outer_far, "seq", low), swap(outer_far, "seq", high)
    late = jnp.concatenate([third_top, third_bottom])
    away_late = swap(section_features(late, 1 - section), "section", 1)
    key_late = jnp.dot(late, key_weight, preferred_element_type=F32).astype(BF16)
    value_late = jnp.dot(late, value_weight, preferred_element_type=F32).astype(BF16)

    block_start = (seq ^ jnp.arange(seq_count, dtype=jnp.int32)) * own_rows
    positions = block_start[:, None] + jnp.arange(own_rows, dtype=jnp.int32)[None, :]
    visible = (positions.reshape(src_rows, 1) < lengths[partner]).astype(jnp.int32)

    held["key_early"] = key_early

    def attend(head):
        held[("attended", head)], held[("query", head)], held[("kv", head)] = attend_head(
            head, visible, queries[0], held["key_early"], key_late, value_early, value_late, out_grad[0]
        )

    def hand_in(head):
        if head < heads_here:
            held[("handed", head)] = swap(held[("kv", head)], "dp", 1)

    def exchange(head):
        held[("their", head)] = swap(held[("kv", head)], "section", 1)

    attend(0)
    hand_in(0)
    exchange(0)
    chip_rows = jnp.concatenate(
        [section_features(early, section), section_features(late, section)]
        + [section_features(normed, section), away_early, away_late]
    )
    held["chip_far"] = target_features(chip_rows, (2, 3))
    held["chip_pair"] = target_features(chip_rows, (1,))
    held["chip_own"] = target_features(chip_rows, (0,))
    sync("first", "second", "key_early", "chip_far", "chip_pair", "chip_own")
    quarter_rows = outer_far.shape[0] // 2
    held["top"] = swap(held["first"][:quarter_rows], "seq", high)
    held["bottom"] = swap(held["second"][quarter_rows:], "seq", low)
    for head in heads[1:]:
        attend(head)
        exchange(head)
    hand_in(1)
    early_pieces = [outer_far, held["first"], held["second"]]
    held["mine"] = jnp.concatenate([piece[:quarter_rows] for piece in early_pieces])
    held["yours"] = jnp.concatenate([piece[quarter_rows:] for piece in early_pieces])
    sync(
        ("handed", 0), ("their", 0), "top", "bottom", "mine", "yours",
        *(("kv", head) for head in heads),
    )

    def chip_sum(name, head):
        rows = held[name]
        return dot(rows[:src_rows], held[("kv", head)], 0, 0) + dot(rows[src_rows:], held[("their", head)], 0, 0)

    def outer_sum(head):
        handed, handed_other = held[("handed", head)], held[("other", head)]
        cut = 3 * quarter_rows
        return (
            dot(held["mine"], handed[:cut], 0, 0)
            + dot(held["yours"], handed_other[:cut], 0, 0)
            + dot(held["top"], handed[cut:], 0, 0)
            + dot(held["bottom"], handed_other[cut:], 0, 0)
        )

    by_steps = seq_count == 4 and heads_here == 4

    def row_block(name, step):
        return held[name][step * own_rows : (step + 1) * own_rows]

    def first_step(name, near, far):
        together = jnp.concatenate([row_block(name, near), row_block(name, far)])
        held[(name, "first")] = swap(together, "seq", near)

    def second_step(name, other):
        passed = row_block(name, other).astype(F32) + held[(name, "first")][own_rows:].astype(F32)
        held[(name, "second")] = swap(passed.astype(BF16), "seq", other)

    def row_total(name):
        total = row_block(name, 0).astype(F32)
        if by_steps:
            first, second = held[(name, "first")][:own_rows], held[(name, "second")]
            return total + first.astype(F32) + second.astype(F32)
        for step in range(1, seq_count):
            total = total + swap(row_block(name, step), "seq", step).astype(F32)
        return total

    def relay(head):
        term = chip_sum("chip_pair", head) + held[("outward", head)].astype(F32)
        held[("relay", head)] = swap(term.astype(BF16), "dp", 1)

    def finish(head):
        totals = [held.get(("total", kind)) for kind in (0, 1)]
        held[("total", 0)], held[("total", 1)] = add_columns(
            totals, head, heads_here, chip_sum("chip_own", head), held[("inner", head)], held[("relay", head)]
        )

    held[("near", 0)] = chip_sum("chip_far", 0)
    held[("other", 0)] = swap(held[("handed", 0)], "section", 1)
    def kinds(*names):
        return [(name, other) for name in names for other in heads]

    for head in heads:
        held["far"] = (held[("near", head)] + outer_sum(head)).astype(BF16)
        sync(
            "far",
            "key_early",
            ("outward", head - 1),
            ("inner", head - 2),
            ("near", head),
            *([("relay", 1)] if head == 3 else []),
            "row_low",
            "row_high",
            *([("row_low", "first")] if head == 2 else [("row_high", "first")] if head == 3 else []),
            *kinds("kv", "their"),
            *((("handed", head + 1),) if head > 0 else ()),
        )
        held[("outward", head)] = lax.ppermute(held["far"][:target_width], "dp", across)
        if head == last:
            sync("far", ("inner", head - 1), *kinds("attended", "query"))
        held[("inner", head)] = lax.ppermute(held["far"][target_width:], "dp", across)
        hand_in(head + 2)
        if head > 0:
            relay(head - 1)
        if head < last:
            if head == 0:
                grads = [held[("kv", other)] for other in heads]
                held["row_low"] = row_product(grads, key_weight, value_weight, 0, 2)
                sync(("outward", 0), ("handed", 1), *kinds("their"))
                held[("near", 1)] = chip_sum("chip_far", 1)
            held[("other", head + 1)] = swap(held[("handed", head + 1)], "section", 1)
            if head > 0:
                sync(
                    ("other", head + 1),
                    ("inner", head - 1),
                    ("relay", head - 2),
                    *kinds("kv", "their"),
                )
                held[("near", head + 1)] = chip_sum("chip_far", head + 1)
        if head == 1:
            if by_steps:
                first_step("row_low", 1, 3)
            grads = [held[("kv", other)] for other in heads]
            held["row_high"] = row_product(grads, key_weight, value_weight, 1, 2)
            if by_steps:
                first_step("row_high", 2, 3)
        if head == 2:
            if by_steps:
                second_step("row_low", 2)
        if head == 3:
            if by_steps:
                second_step("row_high", 1)
    if heads_here == 1:
        held["row_low"] = row_product([held[("kv", 0)]], key_weight, value_weight, 0, 2)
        held["row_high"] = row_product([held[("kv", 0)]], key_weight, value_weight, 1, 2)
    for head in heads[:-1]:
        finish(head)
    sync(("outward", last), *(("relay", head) for head in heads[:-1]))
    relay(last)
    finish(last)

    row_share = jnp.concatenate([row_total("row_low"), row_total("row_high")], axis=1)
    row_grad = swap(row_share.astype(BF16), "section", 1)
    enc_grad = norm_backward(enc_rows, held["factor"], enc_gain, row_grad)
    return (
        jnp.concatenate([held[("attended", head)] for head in heads], axis=1)[None],
        enc_grad[None],
        held[("total", 0)],
        held[("total", 1)],
        jnp.concatenate([held[("query", head)] for head in heads], axis=1)[None],
    )


def solution(mesh):
    placed = (
        P(("section", "dp"), "seq", None),
        P(),
        P(None, "seq"),
        P(None, "seq"),
        P(("section", "dp"), None, "seq"),
        P(("section", "dp"), None, "seq"),
        P(),
    )
    return jax.shard_map(
        on_device,
        mesh=mesh,
        in_specs=placed,
        out_specs=(
            P(("section", "dp"), None, "seq"),
            P(("section", "dp"), "seq", None),
            P(("section", "dp"), "seq"),
            P(("section", "dp"), "seq"),
            P(("section", "dp"), None, "seq"),
        ),
        check_vma=False,
    )
```

```python
import functools

import jax
import jax.numpy as jnp
from jax import lax
from jax.experimental import pallas as pl
from jax.experimental.pallas import tpu as pltpu
from jax.sharding import PartitionSpec as P

HD = 256


EPS = 1e-06
NEG_FILL = -1e30
BF16 = jnp.bfloat16
F32 = jnp.float32
MIB = 1024 * 1024
FILLS_WAITS = pl.CostEstimate(flops=0, bytes_accessed=0, transcendentals=0)


def swap(value, axis, mask):
    pairs = [(source, source ^ mask) for source in range(lax.axis_size(axis))]
    return lax.ppermute(value, axis, pairs)


def normalize(enc_rows, gain):
    wide_rows = enc_rows.astype(F32)
    factor = lax.rsqrt(jnp.mean(wide_rows * wide_rows, axis=-1, keepdims=True) + EPS)
    return ((wide_rows * factor * gain).astype(BF16), factor)


def norm_backward(enc_rows, factor, gain, row_grad):
    wide_rows = enc_rows.astype(F32)
    scaled = row_grad.astype(F32) * gain
    inner_sum = jnp.mean(scaled * wide_rows, axis=-1, keepdims=True)
    return (factor * scaled - wide_rows * factor * factor * factor * inner_sum).astype(BF16)


def tie(*values):
    return lax.optimization_barrier(values)


def dot(left, right, left_dim, right_dim):
    return lax.dot_general(
        left, right, (((left_dim,), (right_dim,)), ((), ())), preferred_element_type=F32
    )


def attend_kernel(visible, query, key_early, key_late, value_early, value_late, upstream, *refs):
    attended, query_grad, kv_grad = refs[-3:]
    score_scale = HD ** (-0.5)
    query_rows, upstream_rows = query[...], upstream[...]
    key_rows = jnp.concatenate([key_early[...], key_late[...]], axis=0)
    value_rows = jnp.concatenate([value_early[...], value_late[...]], axis=0)
    scores = dot(key_rows, query_rows, 1, 1) * score_scale
    scores = jnp.where(visible[...] > 0, scores, NEG_FILL)
    exponent = jnp.exp(scores - jnp.max(scores, axis=0, keepdims=True))
    probability = exponent * (1.0 / jnp.sum(exponent, axis=0, keepdims=True))
    prob_weights = probability.astype(BF16)
    grad_probs = dot(value_rows, upstream_rows, 1, 1)
    inner_sum = jnp.sum(probability * grad_probs, axis=0, keepdims=True)
    grad_scores = (probability * (grad_probs - inner_sum) * score_scale).astype(BF16)
    kv_grad[:, :HD] = dot(grad_scores, query_rows, 1, 0).astype(BF16)
    kv_grad[:, HD:] = dot(prob_weights, upstream_rows, 1, 0).astype(BF16)
    attended[...] = dot(prob_weights, value_rows, 0, 0).astype(BF16)
    query_grad[...] = dot(grad_scores, key_rows, 0, 0).astype(BF16)


def attend_head(head, visible, query, key_early, key_late, value_early, value_late, upstream, kept):
    src_rows, target_rows = visible.shape[0], query.shape[0]
    early, late = key_early.shape[0], key_late.shape[0]

    def column(rows):
        return pl.BlockSpec((rows, HD), lambda step: (0, head))

    def whole(rows, columns):
        return pl.BlockSpec((rows, columns), lambda step: (0, 0))

    return pl.pallas_call(
        attend_kernel,
        grid=(1,),
        in_specs=[
            whole(src_rows, 1),
            column(target_rows),
            column(early),
            column(late),
            column(early),
            column(late),
            column(target_rows),
        ]
        + [pl.BlockSpec(memory_space=pl.ANY)] * len(kept),
        out_specs=[column(target_rows), column(target_rows), whole(src_rows, 2 * HD)],
        out_shape=[
            jax.ShapeDtypeStruct(query.shape, BF16),
            jax.ShapeDtypeStruct(query.shape, BF16),
            jax.ShapeDtypeStruct((src_rows, 2 * HD), BF16),
        ],
        input_output_aliases={7 + slot: slot for slot in range(len(kept))},
        compiler_params=pltpu.CompilerParams(vmem_limit_bytes=6 * MIB + 40 * src_rows * target_rows),
        cost_estimate=FILLS_WAITS,
    )(visible, query, key_early, key_late, value_early, value_late, upstream, *kept)


def row_kernel(head_count, *refs):
    grads, (key_block, value_block), out = refs[:head_count], refs[head_count : head_count + 2], refs[-1]
    key_grads = jnp.concatenate([grad[:, :HD] for grad in grads], axis=1)
    value_grads = jnp.concatenate([grad[:, HD:] for grad in grads], axis=1)
    out[...] = (dot(key_grads, key_block[...], 1, 1) + dot(value_grads, value_block[...], 1, 1)).astype(BF16)


def row_product(grads, key_weight, value_weight, part, parts):
    rows, columns = grads[0].shape
    features, heads_width = key_weight.shape
    block = 512
    steps = features // block // parts
    first = part * steps
    whole = pl.BlockSpec((rows, columns), lambda step: (0, 0))
    weight = pl.BlockSpec((block, heads_width), lambda step: (first + step, 0))
    return pl.pallas_call(
        functools.partial(row_kernel, len(grads)),
        grid=(steps,),
        in_specs=[whole] * len(grads) + [weight, weight],
        out_specs=pl.BlockSpec((rows, block), lambda step: (0, step)),
        out_shape=jax.ShapeDtypeStruct((rows, features // parts), BF16),
        compiler_params=pltpu.CompilerParams(vmem_limit_bytes=14 * MIB + 12 * rows * block),
        cost_estimate=pl.CostEstimate(
            flops=4 * rows * features * heads_width // parts,
            bytes_accessed=(4 * features * heads_width + 2 * rows * (features + 2 * heads_width)) // parts,
            transcendentals=0,
        ),
    )(*grads, key_weight, value_weight)


def add_kernel(kind_count, local, first, second, *refs):
    outs = refs[-kind_count:]
    total = local[...] + first[...].astype(F32) + second[...].astype(F32)
    for slot, out in enumerate(outs):
        out[...] = total[:, slot * HD : (slot + 1) * HD]


def add_columns(totals, head, heads_here, local, first, second):
    rows, columns = local.shape
    here = pl.BlockSpec((rows, columns), lambda step: (0, 0))
    kept = [total for total in totals if total is not None]
    count = columns // HD
    return pl.pallas_call(
        functools.partial(add_kernel, count),
        grid=(1,),
        in_specs=[here] * 3 + [pl.BlockSpec(memory_space=pl.ANY)] * len(kept),
        out_specs=[pl.BlockSpec((rows, HD), lambda step: (0, head))] * count,
        out_shape=[jax.ShapeDtypeStruct((rows, heads_here * HD), F32)] * count,
        input_output_aliases={3 + slot: slot for slot in range(len(kept))},
        cost_estimate=pl.CostEstimate(
            flops=2 * rows * columns, bytes_accessed=12 * rows * columns, transcendentals=0
        ),
        compiler_params=pltpu.CompilerParams(vmem_limit_bytes=12 * MIB),
    )(local, first, second, *kept)


def on_device(enc_states, enc_gain, key_weight, value_weight, queries, out_grad, lengths):
    enc_rows = enc_states[0]
    own_rows, width = enc_rows.shape
    heads_here = key_weight.shape[1] // HD
    heads = range(heads_here)
    last = heads_here - 1
    section_count, dp_count, seq_count = (lax.axis_size(name) for name in ("section", "dp", "seq"))
    section, place, seq = (lax.axis_index(name) for name in ("section", "dp", "seq"))
    partner = (section * dp_count + place + dp_count) % (section_count * dp_count)
    src_rows = own_rows * seq_count
    section_width = width // section_count
    target_width = section_width // dp_count
    across = [(1, 2), (2, 1)]
    held = {}

    def sync(*names):
        names = ["factor"] + [name for name in names if name in held]
        held.update(zip(names, lax.optimization_barrier(tuple(held[name] for name in names))))

    def section_features(rows, index):
        return lax.dynamic_slice_in_dim(rows, index * section_width, section_width, axis=1)

    def target_features(rows, xors, base=0):
        return jnp.concatenate(
            [
                lax.dynamic_slice_in_dim(rows, base + (place ^ xor) * target_width, target_width, axis=1)
                for xor in xors
            ],
            axis=1,
        )

    def swap_both(rows, mask):
        count = section_count * seq_count
        pairs = [(source, source ^ (seq_count + mask)) for source in range(count)]
        return lax.ppermute(rows, ("section", "seq"), pairs)

    normed, held["factor"] = normalize(enc_rows, enc_gain)
    partner_rows = swap(normed, "section", 1)

    low, high = max(seq_count // 4, 1), max(seq_count // 2, 1)
    if low > 1:
        gathered = []
        for rows in (normed, partner_rows):
            blocks = [rows]
            bit = 1
            while bit < low:
                blocks = blocks + [swap(block, "seq", bit) for block in blocks]
                bit *= 2
            gathered.append(jnp.concatenate(blocks))
        normed, partner_rows = gathered
    half = normed.shape[0] // 2
    first, second = swap_both(normed, low), swap_both(normed, high)

    base = section * section_width
    outer_far = jnp.concatenate([target_features(rows, (3, 2), base) for rows in (partner_rows, normed)])
    outer_far = swap(outer_far, "dp", 1)
    first, second, outer_far = tie(first, second, outer_far)

    third_top, third_bottom = swap(first[:half], "seq", high), swap(second[half:], "seq", low)
    early = jnp.concatenate([partner_rows, first, second])
    away_early = swap(section_features(early[2 * half :], 1 - section), "section", 1)
    value_early = jnp.dot(early, value_weight, preferred_element_type=F32).astype(BF16)
    key_early = jnp.dot(early, key_weight, preferred_element_type=F32).astype(BF16)
    key_early, value_early, away_early, third_top, third_bottom, outer_far = tie(
        key_early, value_early, away_early, third_top, third_bottom, outer_far
    )
    held["first"], held["second"] = swap(outer_far, "seq", low), swap(outer_far, "seq", high)
    late = jnp.concatenate([third_top, third_bottom])
    away_late = swap(section_features(late, 1 - section), "section", 1)
    key_late = jnp.dot(late, key_weight, preferred_element_type=F32).astype(BF16)
    value_late = jnp.dot(late, value_weight, preferred_element_type=F32).astype(BF16)

    block_start = (seq ^ jnp.arange(seq_count, dtype=jnp.int32)) * own_rows
    positions = block_start[:, None] + jnp.arange(own_rows, dtype=jnp.int32)[None, :]
    visible = (positions.reshape(src_rows, 1) < lengths[partner]).astype(jnp.int32)

    held["key_early"] = key_early

    outputs = []

    def attend(head):
        early_keys = held["key_early"]
        *outputs[:], held[("kv", head)] = attend_head(
            head, visible, queries[0], early_keys, key_late, value_early, value_late, out_grad[0], list(outputs)
        )

    def hand_in(head):
        if head < heads_here:
            held[("handed", head)] = swap(held[("kv", head)], "dp", 1)

    def exchange(head):
        held[("their", head)] = swap(held[("kv", head)], "section", 1)

    attend(0)
    hand_in(0)
    exchange(0)
    chip_rows = jnp.concatenate(
        [section_features(early, section), section_features(late, section)]
        + [section_features(normed, section), away_early, away_late]
    )
    held["chip_far"] = target_features(chip_rows, (2, 3))
    held["chip_pair"] = target_features(chip_rows, (1,))
    held["chip_own"] = target_features(chip_rows, (0,))
    sync("first", "second", "key_early", "chip_far", "chip_pair", "chip_own")
    quarter_rows = outer_far.shape[0] // 2
    held["top"] = swap(held["first"][:quarter_rows], "seq", high)
    held["bottom"] = swap(held["second"][quarter_rows:], "seq", low)
    for head in heads[1:]:
        attend(head)
        exchange(head)
    hand_in(1)
    early_pieces = [outer_far, held["first"], held["second"]]
    held["mine"] = jnp.concatenate([piece[:quarter_rows] for piece in early_pieces])
    held["yours"] = jnp.concatenate([piece[quarter_rows:] for piece in early_pieces])
    sync(
        ("handed", 0), ("their", 0), "top", "bottom", "mine", "yours",
        *(("kv", head) for head in heads),
    )

    def chip_sum(name, head):
        rows = held[name]
        return dot(rows[:src_rows], held[("kv", head)], 0, 0) + dot(rows[src_rows:], held[("their", head)], 0, 0)

    def outer_sum(head):
        handed, handed_other = held[("handed", head)], held[("other", head)]
        cut = 3 * quarter_rows
        return (
            dot(held["mine"], handed[:cut], 0, 0)
            + dot(held["yours"], handed_other[:cut], 0, 0)
            + dot(held["top"], handed[cut:], 0, 0)
            + dot(held["bottom"], handed_other[cut:], 0, 0)
        )

    by_steps = seq_count == 4 and heads_here == 4

    def row_block(name, step):
        return held[name][step * own_rows : (step + 1) * own_rows]

    def first_step(name, near, far):
        together = jnp.concatenate([row_block(name, near), row_block(name, far)])
        held[(name, "first")] = swap(together, "seq", near)

    def second_step(name, other):
        passed = row_block(name, other).astype(F32) + held[(name, "first")][own_rows:].astype(F32)
        held[(name, "second")] = swap(passed.astype(BF16), "seq", other)

    def row_total(name):
        total = row_block(name, 0).astype(F32)
        if by_steps:
            first, second = held[(name, "first")][:own_rows], held[(name, "second")]
            return total + first.astype(F32) + second.astype(F32)
        for step in range(1, seq_count):
            total = total + swap(row_block(name, step), "seq", step).astype(F32)
        return total

    def relay(head):
        term = chip_sum("chip_pair", head) + held[("outward", head)].astype(F32)
        held[("relay", head)] = swap(term.astype(BF16), "dp", 1)

    def finish(head):
        totals = [held.get(("total", kind)) for kind in (0, 1)]
        held[("total", 0)], held[("total", 1)] = add_columns(
            totals, head, heads_here, chip_sum("chip_own", head), held[("inner", head)], held[("relay", head)]
        )

    held[("near", 0)] = chip_sum("chip_far", 0)
    held[("other", 0)] = swap(held[("handed", 0)], "section", 1)
    def kinds(*names):
        return [(name, other) for name in names for other in heads]

    for head in heads:
        held["far"] = (held[("near", head)] + outer_sum(head)).astype(BF16)
        sync(
            "far",
            "key_early",
            ("outward", head - 1),
            ("inner", head - 2),
            ("near", head),
            *([("relay", 1)] if head == 3 else []),
            "row_low",
            "row_high",
            *([("row_high", "first")] if head == 2 else []),
            *([("row_low", "second"), ("row_high", "second")] if head == 3 else []),
            *kinds("kv", "their"),
            *((("handed", head + 1),) if head > 0 else ()),
        )
        held[("outward", head)] = lax.ppermute(held["far"][:target_width], "dp", across)
        held[("inner", head)] = lax.ppermute(held["far"][target_width:], "dp", across)
        hand_in(head + 2)
        if head > 0:
            relay(head - 1)
        if head < last:
            if head == 0:
                grads = [held[("kv", other)] for other in heads]
                held["row_low"] = row_product(grads, key_weight, value_weight, 0, 2)
                if by_steps:
                    first_step("row_low", 1, 3)
                    held["row_high"] = row_product(grads, key_weight, value_weight, 1, 2)
                    first_step("row_high", 2, 3)
                sync(("outward", 0), ("handed", 1), *kinds("their"))
                held[("near", 1)] = chip_sum("chip_far", 1)
            held[("other", head + 1)] = swap(held[("handed", head + 1)], "section", 1)
            if head > 0:
                sync(
                    ("other", head + 1),
                    ("inner", head - 1),
                    ("relay", head - 2),
                    *([("row_low", "first")] if head == 1 else []),
                    *kinds("kv", "their"),
                )
                held[("near", head + 1)] = chip_sum("chip_far", head + 1)
        if head == 1:
            if by_steps:
                second_step("row_low", 2)
        if head == 2 and by_steps:
            second_step("row_high", 1)
    if not by_steps:
        held["row_low"] = row_product([held[("kv", head)] for head in heads], key_weight, value_weight, 0, 2)
        held["row_high"] = row_product([held[("kv", head)] for head in heads], key_weight, value_weight, 1, 2)
    sync(*kinds("outward", "relay"), *(("inner", head) for head in heads[:-1]), *kinds("kv", "their"))
    relay(last)
    for head in heads[:-1]:
        finish(head)
    row_share = jnp.concatenate([row_total("row_low"), row_total("row_high")], axis=1)
    row_grad = swap(row_share.astype(BF16), "section", 1)
    held["enc_grad"] = norm_backward(enc_rows, held["factor"], enc_gain, row_grad)
    sync(("relay", last), "enc_grad")
    finish(last)
    return (
        outputs[0][None],
        held["enc_grad"][None],
        held[("total", 0)],
        held[("total", 1)],
        outputs[1][None],
    )


def solution(mesh):
    placed = (
        P(("section", "dp"), "seq", None),
        P(),
        P(None, "seq"),
        P(None, "seq"),
        P(("section", "dp"), None, "seq"),
        P(("section", "dp"), None, "seq"),
        P(),
    )
    return jax.shard_map(
        on_device,
        mesh=mesh,
        in_specs=placed,
        out_specs=(
            P(("section", "dp"), None, "seq"),
            P(("section", "dp"), "seq", None),
            P(("section", "dp"), "seq"),
            P(("section", "dp"), "seq"),
            P(("section", "dp"), None, "seq"),
        ),
        check_vma=False,
    )
```

```python
import functools

import jax
import jax.numpy as jnp
from jax import lax
from jax.experimental import pallas as pl
from jax.experimental.pallas import tpu as pltpu
from jax.sharding import PartitionSpec as P

HD = 256


EPS = 1e-06
NEG_FILL = -1e30
BF16 = jnp.bfloat16
F32 = jnp.float32
MIB = 1024 * 1024
FILLS_WAITS = pl.CostEstimate(flops=0, bytes_accessed=0, transcendentals=0)


def swap(value, axis, mask):
    pairs = [(source, source ^ mask) for source in range(lax.axis_size(axis))]
    return lax.ppermute(value, axis, pairs)


def normalize(enc_rows, gain):
    wide_rows = enc_rows.astype(F32)
    factor = lax.rsqrt(jnp.mean(wide_rows * wide_rows, axis=-1, keepdims=True) + EPS)
    return ((wide_rows * factor * gain).astype(BF16), factor)


def norm_backward(enc_rows, factor, gain, row_grad):
    wide_rows = enc_rows.astype(F32)
    scaled = row_grad.astype(F32) * gain
    inner_sum = jnp.mean(scaled * wide_rows, axis=-1, keepdims=True)
    return (factor * scaled - wide_rows * factor * factor * factor * inner_sum).astype(BF16)


def tie(*values):
    return lax.optimization_barrier(values)


def dot(left, right, left_dim, right_dim):
    return lax.dot_general(
        left, right, (((left_dim,), (right_dim,)), ((), ())), preferred_element_type=F32
    )


def attend_kernel(
    visible, query, key_early, key_late, value_early, value_late, upstream, attended, query_grad, kv_grad
):
    score_scale = HD ** (-0.5)
    query_rows, upstream_rows = query[...], upstream[...]
    key_rows = jnp.concatenate([key_early[...], key_late[...]], axis=0)
    value_rows = jnp.concatenate([value_early[...], value_late[...]], axis=0)
    scores = dot(key_rows, query_rows, 1, 1) * score_scale
    scores = jnp.where(visible[...] > 0, scores, NEG_FILL)
    exponent = jnp.exp(scores - jnp.max(scores, axis=0, keepdims=True))
    probability = exponent * (1.0 / jnp.sum(exponent, axis=0, keepdims=True))
    prob_weights = probability.astype(BF16)
    grad_probs = dot(value_rows, upstream_rows, 1, 1)
    inner_sum = jnp.sum(probability * grad_probs, axis=0, keepdims=True)
    grad_scores = (probability * (grad_probs - inner_sum) * score_scale).astype(BF16)
    kv_grad[:, :HD] = dot(grad_scores, query_rows, 1, 0).astype(BF16)
    kv_grad[:, HD:] = dot(prob_weights, upstream_rows, 1, 0).astype(BF16)
    attended[...] = dot(prob_weights, value_rows, 0, 0).astype(BF16)
    query_grad[...] = dot(grad_scores, key_rows, 0, 0).astype(BF16)


def attend_head(head, visible, query, key_early, key_late, value_early, value_late, upstream):
    src_rows, target_rows = visible.shape[0], query.shape[0]
    early, late = key_early.shape[0], key_late.shape[0]

    def column(rows):
        return pl.BlockSpec((rows, HD), lambda step: (0, head))

    def whole(rows, columns):
        return pl.BlockSpec((rows, columns), lambda step: (0, 0))

    return pl.pallas_call(
        attend_kernel,
        grid=(1,),
        in_specs=[
            whole(src_rows, 1),
            column(target_rows),
            column(early),
            column(late),
            column(early),
            column(late),
            column(target_rows),
        ],
        out_specs=[whole(target_rows, HD), whole(target_rows, HD), whole(src_rows, 2 * HD)],
        out_shape=[
            jax.ShapeDtypeStruct((target_rows, HD), BF16),
            jax.ShapeDtypeStruct((target_rows, HD), BF16),
            jax.ShapeDtypeStruct((src_rows, 2 * HD), BF16),
        ],
        compiler_params=pltpu.CompilerParams(vmem_limit_bytes=6 * MIB + 40 * src_rows * target_rows),
        cost_estimate=FILLS_WAITS,
    )(visible, query, key_early, key_late, value_early, value_late, upstream)


def row_kernel(head_count, *refs):
    grads, (key_block, value_block), out = refs[:head_count], refs[head_count : head_count + 2], refs[-1]
    key_grads = jnp.concatenate([grad[:, :HD] for grad in grads], axis=1)
    value_grads = jnp.concatenate([grad[:, HD:] for grad in grads], axis=1)
    out[...] = (dot(key_grads, key_block[...], 1, 1) + dot(value_grads, value_block[...], 1, 1)).astype(BF16)


def row_product(grads, key_weight, value_weight, part, parts):
    rows, columns = grads[0].shape
    features, heads_width = key_weight.shape
    block = 512
    steps = features // block // parts
    first = part * steps
    whole = pl.BlockSpec((rows, columns), lambda step: (0, 0))
    weight = pl.BlockSpec((block, heads_width), lambda step: (first + step, 0))
    return pl.pallas_call(
        functools.partial(row_kernel, len(grads)),
        grid=(steps,),
        in_specs=[whole] * len(grads) + [weight, weight],
        out_specs=pl.BlockSpec((rows, block), lambda step: (0, step)),
        out_shape=jax.ShapeDtypeStruct((rows, features // parts), BF16),
        compiler_params=pltpu.CompilerParams(vmem_limit_bytes=14 * MIB + 12 * rows * block),
        cost_estimate=pl.CostEstimate(
            flops=4 * rows * features * heads_width // parts,
            bytes_accessed=(4 * features * heads_width + 2 * rows * (features + 2 * heads_width)) // parts,
            transcendentals=0,
        ),
    )(*grads, key_weight, value_weight)


def add_kernel(kind_count, local, first, second, *refs):
    outs = refs[-kind_count:]
    total = local[...] + first[...].astype(F32) + second[...].astype(F32)
    for slot, out in enumerate(outs):
        out[...] = total[:, slot * HD : (slot + 1) * HD]


def add_columns(totals, head, heads_here, local, first, second):
    rows, columns = local.shape
    here = pl.BlockSpec((rows, columns), lambda step: (0, 0))
    kept = [total for total in totals if total is not None]
    count = columns // HD
    return pl.pallas_call(
        functools.partial(add_kernel, count),
        grid=(1,),
        in_specs=[here] * 3 + [pl.BlockSpec(memory_space=pl.ANY)] * len(kept),
        out_specs=[pl.BlockSpec((rows, HD), lambda step: (0, head))] * count,
        out_shape=[jax.ShapeDtypeStruct((rows, heads_here * HD), F32)] * count,
        input_output_aliases={3 + slot: slot for slot in range(len(kept))},
        cost_estimate=pl.CostEstimate(
            flops=2 * rows * columns, bytes_accessed=12 * rows * columns, transcendentals=0
        ),
        compiler_params=pltpu.CompilerParams(vmem_limit_bytes=12 * MIB),
    )(local, first, second, *kept)


def on_device(enc_states, enc_gain, key_weight, value_weight, queries, out_grad, lengths):
    enc_rows = enc_states[0]
    own_rows, width = enc_rows.shape
    heads_here = key_weight.shape[1] // HD
    heads = range(heads_here)
    last = heads_here - 1
    section_count, dp_count, seq_count = (lax.axis_size(name) for name in ("section", "dp", "seq"))
    section, place, seq = (lax.axis_index(name) for name in ("section", "dp", "seq"))
    partner = (section * dp_count + place + dp_count) % (section_count * dp_count)
    src_rows = own_rows * seq_count
    section_width = width // section_count
    target_width = section_width // dp_count
    across = [(1, 2), (2, 1)]
    held = {}

    def sync(*names):
        names = ["factor"] + [name for name in names if name in held]
        held.update(zip(names, lax.optimization_barrier(tuple(held[name] for name in names))))

    def section_features(rows, index):
        return lax.dynamic_slice_in_dim(rows, index * section_width, section_width, axis=1)

    def target_features(rows, xors, base=0):
        return jnp.concatenate(
            [
                lax.dynamic_slice_in_dim(rows, base + (place ^ xor) * target_width, target_width, axis=1)
                for xor in xors
            ],
            axis=1,
        )

    def swap_both(rows, mask):
        count = section_count * seq_count
        pairs = [(source, source ^ (seq_count + mask)) for source in range(count)]
        return lax.ppermute(rows, ("section", "seq"), pairs)

    normed, held["factor"] = normalize(enc_rows, enc_gain)
    partner_rows = swap(normed, "section", 1)

    low, high = max(seq_count // 4, 1), max(seq_count // 2, 1)
    if low > 1:
        gathered = []
        for rows in (normed, partner_rows):
            blocks = [rows]
            bit = 1
            while bit < low:
                blocks = blocks + [swap(block, "seq", bit) for block in blocks]
                bit *= 2
            gathered.append(jnp.concatenate(blocks))
        normed, partner_rows = gathered
    half = normed.shape[0] // 2
    first, second = swap_both(normed, low), swap_both(normed, high)

    base = section * section_width
    outer_far = jnp.concatenate([target_features(rows, (3, 2), base) for rows in (partner_rows, normed)])
    outer_far = swap(outer_far, "dp", 1)
    first, second, outer_far = tie(first, second, outer_far)

    third_top, third_bottom = swap(first[:half], "seq", high), swap(second[half:], "seq", low)
    early = jnp.concatenate([partner_rows, first, second])
    away_early = swap(section_features(early[2 * half :], 1 - section), "section", 1)
    value_early = jnp.dot(early, value_weight, preferred_element_type=F32).astype(BF16)
    key_early = jnp.dot(early, key_weight, preferred_element_type=F32).astype(BF16)
    key_early, value_early, away_early, third_top, third_bottom, outer_far = tie(
        key_early, value_early, away_early, third_top, third_bottom, outer_far
    )
    held["first"], held["second"] = swap(outer_far, "seq", low), swap(outer_far, "seq", high)
    late = jnp.concatenate([third_top, third_bottom])
    away_late = swap(section_features(late, 1 - section), "section", 1)
    key_late = jnp.dot(late, key_weight, preferred_element_type=F32).astype(BF16)
    value_late = jnp.dot(late, value_weight, preferred_element_type=F32).astype(BF16)

    block_start = (seq ^ jnp.arange(seq_count, dtype=jnp.int32)) * own_rows
    positions = block_start[:, None] + jnp.arange(own_rows, dtype=jnp.int32)[None, :]
    visible = (positions.reshape(src_rows, 1) < lengths[partner]).astype(jnp.int32)

    held["key_early"] = key_early

    def attend(head):
        held[("attended", head)], held[("query", head)], held[("kv", head)] = attend_head(
            head, visible, queries[0], held["key_early"], key_late, value_early, value_late, out_grad[0]
        )

    def hand_in(head):
        if head < heads_here:
            held[("handed", head)] = swap(held[("kv", head)], "dp", 1)

    def exchange(head):
        held[("their", head)] = swap(held[("kv", head)], "section", 1)

    attend(0)
    hand_in(0)
    exchange(0)
    chip_rows = jnp.concatenate(
        [section_features(early, section), section_features(late, section)]
        + [section_features(normed, section), away_early, away_late]
    )
    held["chip_far"] = target_features(chip_rows, (2, 3))
    held["chip_pair"] = target_features(chip_rows, (1,))
    held["chip_own"] = target_features(chip_rows, (0,))
    sync("first", "second", "key_early", "chip_far", "chip_pair", "chip_own")
    quarter_rows = outer_far.shape[0] // 2
    held["top"] = swap(held["first"][:quarter_rows], "seq", high)
    held["bottom"] = swap(held["second"][quarter_rows:], "seq", low)
    for head in heads[1:]:
        attend(head)
        exchange(head)
    hand_in(1)
    early_pieces = [outer_far, held["first"], held["second"]]
    held["mine"] = jnp.concatenate([piece[:quarter_rows] for piece in early_pieces])
    held["yours"] = jnp.concatenate([piece[quarter_rows:] for piece in early_pieces])
    sync(
        ("handed", 0), ("their", 0), "top", "bottom", "mine", "yours",
        *(("kv", head) for head in heads),
    )

    def chip_sum(name, head):
        rows = held[name]
        return dot(rows[:src_rows], held[("kv", head)], 0, 0) + dot(rows[src_rows:], held[("their", head)], 0, 0)

    def outer_sum(head):
        handed, handed_other = held[("handed", head)], held[("other", head)]
        cut = 3 * quarter_rows
        return (
            dot(held["mine"], handed[:cut], 0, 0)
            + dot(held["yours"], handed_other[:cut], 0, 0)
            + dot(held["top"], handed[cut:], 0, 0)
            + dot(held["bottom"], handed_other[cut:], 0, 0)
        )

    by_steps = seq_count == 4 and heads_here == 4

    def row_block(name, step):
        return held[name][step * own_rows : (step + 1) * own_rows]

    def first_step(name, near, far):
        together = jnp.concatenate([row_block(name, near), row_block(name, far)])
        held[(name, "first")] = swap(together, "seq", near)

    def second_step(name, other):
        passed = row_block(name, other).astype(F32) + held[(name, "first")][own_rows:].astype(F32)
        held[(name, "second")] = swap(passed.astype(BF16), "seq", other)

    def row_total(name):
        total = row_block(name, 0).astype(F32)
        if by_steps:
            first, second = held[(name, "first")][:own_rows], held[(name, "second")]
            return total + first.astype(F32) + second.astype(F32)
        for step in range(1, seq_count):
            total = total + swap(row_block(name, step), "seq", step).astype(F32)
        return total

    def relay(head):
        term = chip_sum("chip_pair", head) + held[("outward", head)].astype(F32)
        held[("relay", head)] = swap(term.astype(BF16), "dp", 1)

    def finish(head):
        totals = [held.get(("total", kind)) for kind in (0, 1)]
        held[("total", 0)], held[("total", 1)] = add_columns(
            totals, head, heads_here, chip_sum("chip_own", head), held[("inner", head)], held[("relay", head)]
        )

    held[("near", 0)] = chip_sum("chip_far", 0)
    held[("other", 0)] = swap(held[("handed", 0)], "section", 1)
    def kinds(*names):
        return [(name, other) for name in names for other in heads]

    for head in heads:
        held["far"] = (held[("near", head)] + outer_sum(head)).astype(BF16)
        sync(
            "far",
            "key_early",
            ("outward", head - 1),
            ("inner", head - 2),
            ("near", head),
            *([("relay", 1)] if head == 3 else []),
            "row_low",
            "row_high",
            *([("row_high", "first")] if head == 2 else []),
            *([("row_low", "second"), ("row_high", "second")] if head == 3 else []),
            *kinds("kv", "their"),
            *((("handed", head + 1),) if head > 0 else ()),
        )
        held[("outward", head)] = lax.ppermute(held["far"][:target_width], "dp", across)
        held[("inner", head)] = lax.ppermute(held["far"][target_width:], "dp", across)
        hand_in(head + 2)
        if head > 0:
            relay(head - 1)
        if head < last:
            if head == 0:
                grads = [held[("kv", other)] for other in heads]
                held["row_low"] = row_product(grads, key_weight, value_weight, 0, 2)
                if by_steps:
                    first_step("row_low", 1, 3)
                    held["row_high"] = row_product(grads, key_weight, value_weight, 1, 2)
                    first_step("row_high", 2, 3)
                sync(("outward", 0), ("handed", 1), *kinds("their"))
                held[("near", 1)] = chip_sum("chip_far", 1)
            held[("other", head + 1)] = swap(held[("handed", head + 1)], "section", 1)
            if head > 0:
                sync(
                    ("other", head + 1),
                    ("inner", head - 1),
                    ("relay", head - 2),
                    *([("row_low", "first")] if head == 1 else []),
                    *kinds("kv", "their"),
                )
                held[("near", head + 1)] = chip_sum("chip_far", head + 1)
        if head == 1:
            if by_steps:
                second_step("row_low", 2)
        if head == 2 and by_steps:
            second_step("row_high", 1)
    if not by_steps:
        held["row_low"] = row_product([held[("kv", head)] for head in heads], key_weight, value_weight, 0, 2)
        held["row_high"] = row_product([held[("kv", head)] for head in heads], key_weight, value_weight, 1, 2)
    sync(("relay", last - 1), *kinds("attended", "query"))
    for name in ("attended", "query"):
        held[name] = jnp.concatenate([held[(name, head)] for head in heads], axis=1)
    ends = ["attended", "query", *kinds("outward", "relay"), *(("inner", head) for head in heads[:-1])]
    sync(*ends, *kinds("kv", "their"))
    relay(last)
    for head in heads[:-1]:
        finish(head)
    row_share = jnp.concatenate([row_total("row_low"), row_total("row_high")], axis=1)
    row_grad = swap(row_share.astype(BF16), "section", 1)
    held["enc_grad"] = norm_backward(enc_rows, held["factor"], enc_gain, row_grad)
    sync(("relay", last), "enc_grad")
    finish(last)
    return (
        held["attended"][None],
        held["enc_grad"][None],
        held[("total", 0)],
        held[("total", 1)],
        held["query"][None],
    )


def solution(mesh):
    placed = (
        P(("section", "dp"), "seq", None),
        P(),
        P(None, "seq"),
        P(None, "seq"),
        P(("section", "dp"), None, "seq"),
        P(("section", "dp"), None, "seq"),
        P(),
    )
    return jax.shard_map(
        on_device,
        mesh=mesh,
        in_specs=placed,
        out_specs=(
            P(("section", "dp"), None, "seq"),
            P(("section", "dp"), "seq", None),
            P(("section", "dp"), "seq"),
            P(("section", "dp"), "seq"),
            P(("section", "dp"), None, "seq"),
        ),
        check_vma=False,
    )
```

```python
import functools

import jax
import jax.numpy as jnp
from jax import lax
from jax.experimental import pallas as pl
from jax.experimental.pallas import tpu as pltpu
from jax.sharding import PartitionSpec as P

HD = 256


EPS = 1e-06
NEG_FILL = -1e30
BF16 = jnp.bfloat16
F32 = jnp.float32
MIB = 1024 * 1024
FILLS_WAITS = pl.CostEstimate(flops=0, bytes_accessed=0, transcendentals=0)


def swap(value, axis, mask):
    pairs = [(source, source ^ mask) for source in range(lax.axis_size(axis))]
    return lax.ppermute(value, axis, pairs)


def normalize(enc_rows, gain):
    wide_rows = enc_rows.astype(F32)
    factor = lax.rsqrt(jnp.mean(wide_rows * wide_rows, axis=-1, keepdims=True) + EPS)
    return ((wide_rows * factor * gain).astype(BF16), factor)


def norm_backward(enc_rows, factor, gain, row_grad):
    wide_rows = enc_rows.astype(F32)
    scaled = row_grad.astype(F32) * gain
    inner_sum = jnp.mean(scaled * wide_rows, axis=-1, keepdims=True)
    return (factor * scaled - wide_rows * factor * factor * factor * inner_sum).astype(BF16)


def tie(*values):
    return lax.optimization_barrier(values)


def dot(left, right, left_dim, right_dim):
    return lax.dot_general(
        left, right, (((left_dim,), (right_dim,)), ((), ())), preferred_element_type=F32
    )


def in_order(early, late):
    half = early.shape[0] // 4
    return jnp.concatenate([early[: 3 * half], late[: 2 * half], early[3 * half :], late[2 * half :]], axis=0)


def attend_kernel(
    visible, query, key_early, key_late, value_early, value_late, upstream, attended, query_grad, kv_grad
):
    score_scale = HD ** (-0.5)
    query_rows, upstream_rows = query[...], upstream[...]
    key_rows, value_rows = in_order(key_early, key_late), in_order(value_early, value_late)
    scores = dot(key_rows, query_rows, 1, 1) * score_scale
    scores = jnp.where(visible[...] > 0, scores, NEG_FILL)
    exponent = jnp.exp(scores - jnp.max(scores, axis=0, keepdims=True))
    probability = exponent * (1.0 / jnp.sum(exponent, axis=0, keepdims=True))
    prob_weights = probability.astype(BF16)
    grad_probs = dot(value_rows, upstream_rows, 1, 1)
    inner_sum = jnp.sum(probability * grad_probs, axis=0, keepdims=True)
    grad_scores = (probability * (grad_probs - inner_sum) * score_scale).astype(BF16)
    kv_grad[:, :HD] = dot(grad_scores, query_rows, 1, 0).astype(BF16)
    kv_grad[:, HD:] = dot(prob_weights, upstream_rows, 1, 0).astype(BF16)
    attended[...] = dot(prob_weights, value_rows, 0, 0).astype(BF16)
    query_grad[...] = dot(grad_scores, key_rows, 0, 0).astype(BF16)


def attend_head(head, visible, query, key_early, key_late, value_early, value_late, upstream):
    src_rows, target_rows = visible.shape[0], query.shape[0]
    early, late = key_early.shape[0], key_late.shape[0]

    def column(rows):
        return pl.BlockSpec((rows, HD), lambda step: (0, head))

    def whole(rows, columns):
        return pl.BlockSpec((rows, columns), lambda step: (0, 0))

    return pl.pallas_call(
        attend_kernel,
        grid=(1,),
        in_specs=[
            whole(src_rows, 1),
            column(target_rows),
            column(early),
            column(late),
            column(early),
            column(late),
            column(target_rows),
        ],
        out_specs=[whole(target_rows, HD), whole(target_rows, HD), whole(src_rows, 2 * HD)],
        out_shape=[
            jax.ShapeDtypeStruct((target_rows, HD), BF16),
            jax.ShapeDtypeStruct((target_rows, HD), BF16),
            jax.ShapeDtypeStruct((src_rows, 2 * HD), BF16),
        ],
        compiler_params=pltpu.CompilerParams(vmem_limit_bytes=6 * MIB + 40 * src_rows * target_rows),
        cost_estimate=FILLS_WAITS,
    )(visible, query, key_early, key_late, value_early, value_late, upstream)


def row_kernel(head_count, *refs):
    grads, (key_block, value_block), out = refs[:head_count], refs[head_count : head_count + 2], refs[-1]
    key_grads = jnp.concatenate([grad[:, :HD] for grad in grads], axis=1)
    value_grads = jnp.concatenate([grad[:, HD:] for grad in grads], axis=1)
    out[...] = (dot(key_grads, key_block[...], 1, 1) + dot(value_grads, value_block[...], 1, 1)).astype(BF16)


def row_product(grads, key_weight, value_weight, part, parts):
    rows, columns = grads[0].shape
    features, heads_width = key_weight.shape
    block = 512
    steps = features // block // parts
    first = part * steps
    whole = pl.BlockSpec((rows, columns), lambda step: (0, 0))
    weight = pl.BlockSpec((block, heads_width), lambda step: (first + step, 0))
    return pl.pallas_call(
        functools.partial(row_kernel, len(grads)),
        grid=(steps,),
        in_specs=[whole] * len(grads) + [weight, weight],
        out_specs=pl.BlockSpec((rows, block), lambda step: (0, step)),
        out_shape=jax.ShapeDtypeStruct((rows, features // parts), BF16),
        compiler_params=pltpu.CompilerParams(vmem_limit_bytes=14 * MIB + 12 * rows * block),
        cost_estimate=pl.CostEstimate(
            flops=4 * rows * features * heads_width // parts,
            bytes_accessed=(4 * features * heads_width + 2 * rows * (features + 2 * heads_width)) // parts,
            transcendentals=0,
        ),
    )(*grads, key_weight, value_weight)


def add_kernel(kind_count, local, first, second, *refs):
    outs = refs[-kind_count:]
    total = local[...] + first[...].astype(F32) + second[...].astype(F32)
    for slot, out in enumerate(outs):
        out[...] = total[:, slot * HD : (slot + 1) * HD]


def add_columns(totals, head, heads_here, local, first, second):
    rows, columns = local.shape
    here = pl.BlockSpec((rows, columns), lambda step: (0, 0))
    kept = [total for total in totals if total is not None]
    count = columns // HD
    return pl.pallas_call(
        functools.partial(add_kernel, count),
        grid=(1,),
        in_specs=[here] * 3 + [pl.BlockSpec(memory_space=pl.ANY)] * len(kept),
        out_specs=[pl.BlockSpec((rows, HD), lambda step: (0, head))] * count,
        out_shape=[jax.ShapeDtypeStruct((rows, heads_here * HD), F32)] * count,
        input_output_aliases={3 + slot: slot for slot in range(len(kept))},
        cost_estimate=pl.CostEstimate(
            flops=2 * rows * columns, bytes_accessed=12 * rows * columns, transcendentals=0
        ),
        compiler_params=pltpu.CompilerParams(vmem_limit_bytes=12 * MIB),
    )(local, first, second, *kept)


def on_device(enc_states, enc_gain, key_weight, value_weight, queries, out_grad, lengths):
    enc_rows = enc_states[0]
    own_rows, width = enc_rows.shape
    heads_here = key_weight.shape[1] // HD
    heads = range(heads_here)
    last = heads_here - 1
    section_count, dp_count, seq_count = (lax.axis_size(name) for name in ("section", "dp", "seq"))
    section, place, seq = (lax.axis_index(name) for name in ("section", "dp", "seq"))
    partner = (section * dp_count + place + dp_count) % (section_count * dp_count)
    src_rows = own_rows * seq_count
    section_width = width // section_count
    target_width = section_width // dp_count
    across = [(1, 2), (2, 1)]
    held = {}

    def sync(*names):
        names = ["factor"] + [name for name in names if name in held]
        held.update(zip(names, lax.optimization_barrier(tuple(held[name] for name in names))))

    def section_features(rows, index):
        return lax.dynamic_slice_in_dim(rows, index * section_width, section_width, axis=1)

    def target_features(rows, xors, base=0):
        return jnp.concatenate(
            [
                lax.dynamic_slice_in_dim(rows, base + (place ^ xor) * target_width, target_width, axis=1)
                for xor in xors
            ],
            axis=1,
        )

    def swap_both(rows, mask):
        count = section_count * seq_count
        pairs = [(source, source ^ (seq_count + mask)) for source in range(count)]
        return lax.ppermute(rows, ("section", "seq"), pairs)

    normed, held["factor"] = normalize(enc_rows, enc_gain)
    partner_rows = swap(normed, "section", 1)

    low, high = max(seq_count // 4, 1), max(seq_count // 2, 1)
    if low > 1:
        gathered = []
        for rows in (normed, partner_rows):
            blocks = [rows]
            bit = 1
            while bit < low:
                blocks = blocks + [swap(block, "seq", bit) for block in blocks]
                bit *= 2
            gathered.append(jnp.concatenate(blocks))
        normed, partner_rows = gathered
    half = normed.shape[0] // 2
    top, bottom = normed[:half], normed[half:]
    first_top, second_bottom = swap_both(top, low), swap_both(bottom, high)
    first_bottom, second_top = swap_both(bottom, low), swap_both(top, high)

    base = section * section_width
    outer_far = jnp.concatenate([target_features(rows, (3, 2), base) for rows in (partner_rows, normed)])
    outer_far = swap(outer_far, "dp", 1)

    def project(rows):
        return [
            jnp.dot(rows, weight, preferred_element_type=F32).astype(BF16) for weight in (key_weight, value_weight)
        ]

    first_top, second_bottom = tie(first_top, second_bottom)
    third_top, third_bottom = swap(first_top, "seq", high), swap(second_bottom, "seq", low)
    key_early, value_early = project(jnp.concatenate([partner_rows, first_top, second_bottom]))
    key_early, value_early, outer_far, first_bottom, second_top, third_top, third_bottom = tie(
        key_early, value_early, outer_far, first_bottom, second_top, third_top, third_bottom
    )
    held["first"], held["second"] = swap(outer_far, "seq", low), swap(outer_far, "seq", high)
    gathered = [first_top, first_bottom, second_top, second_bottom, third_top, third_bottom]
    away = [section_features(rows, 1 - section) for rows in gathered]
    away = swap(jnp.concatenate(away), "section", 1)
    key_late, value_late = project(jnp.concatenate([first_bottom, second_top, third_top, third_bottom]))

    block_start = (seq ^ jnp.arange(seq_count, dtype=jnp.int32)) * own_rows
    positions = block_start[:, None] + jnp.arange(own_rows, dtype=jnp.int32)[None, :]
    visible = (positions.reshape(src_rows, 1) < lengths[partner]).astype(jnp.int32)

    held["key_early"] = key_early

    def attend(head):
        held[("attended", head)], held[("query", head)], held[("kv", head)] = attend_head(
            head, visible, queries[0], held["key_early"], key_late, value_early, value_late, out_grad[0]
        )

    def hand_in(head):
        if head < heads_here:
            held[("handed", head)] = swap(held[("kv", head)], "dp", 1)

    def exchange(head):
        held[("their", head)] = swap(held[("kv", head)], "section", 1)

    attend(0)
    hand_in(0)
    exchange(0)
    chip_rows = jnp.concatenate(
        [section_features(rows, section) for rows in (partner_rows, *gathered, normed)] + [away]
    )
    held["chip_far"] = target_features(chip_rows, (2, 3))
    held["chip_pair"] = target_features(chip_rows, (1,))
    held["chip_own"] = target_features(chip_rows, (0,))
    sync("first", "second", "key_early", "chip_far", "chip_pair", "chip_own")
    quarter_rows = outer_far.shape[0] // 2
    held["top"] = swap(held["first"][:quarter_rows], "seq", high)
    held["bottom"] = swap(held["second"][quarter_rows:], "seq", low)
    for head in heads[1:]:
        attend(head)
        exchange(head)
    hand_in(1)
    early_pieces = [outer_far, held["first"], held["second"]]
    held["mine"] = jnp.concatenate([piece[:quarter_rows] for piece in early_pieces])
    held["yours"] = jnp.concatenate([piece[quarter_rows:] for piece in early_pieces])
    sync(
        ("handed", 0), ("their", 0), "top", "bottom", "mine", "yours",
        *(("kv", head) for head in heads),
    )

    def chip_sum(name, head):
        rows = held[name]
        return dot(rows[:src_rows], held[("kv", head)], 0, 0) + dot(rows[src_rows:], held[("their", head)], 0, 0)

    def outer_sum(head):
        handed, handed_other = held[("handed", head)], held[("other", head)]
        cut = 3 * quarter_rows
        return (
            dot(held["mine"], handed[:cut], 0, 0)
            + dot(held["yours"], handed_other[:cut], 0, 0)
            + dot(held["top"], handed[cut:], 0, 0)
            + dot(held["bottom"], handed_other[cut:], 0, 0)
        )

    by_steps = seq_count == 4 and heads_here == 4

    def row_block(name, step):
        return held[name][step * own_rows : (step + 1) * own_rows]

    def first_step(name, near, far):
        together = jnp.concatenate([row_block(name, near), row_block(name, far)])
        held[(name, "first")] = swap(together, "seq", near)

    def second_step(name, other):
        passed = row_block(name, other).astype(F32) + held[(name, "first")][own_rows:].astype(F32)
        held[(name, "second")] = swap(passed.astype(BF16), "seq", other)

    def row_total(name):
        total = row_block(name, 0).astype(F32)
        if by_steps:
            first, second = held[(name, "first")][:own_rows], held[(name, "second")]
            return total + first.astype(F32) + second.astype(F32)
        for step in range(1, seq_count):
            total = total + swap(row_block(name, step), "seq", step).astype(F32)
        return total

    def relay(head):
        term = chip_sum("chip_pair", head) + held[("outward", head)].astype(F32)
        held[("relay", head)] = swap(term.astype(BF16), "dp", 1)

    def finish(head):
        totals = [held.get(("total", kind)) for kind in (0, 1)]
        held[("total", 0)], held[("total", 1)] = add_columns(
            totals, head, heads_here, chip_sum("chip_own", head), held[("inner", head)], held[("relay", head)]
        )

    held[("near", 0)] = chip_sum("chip_far", 0)
    held[("other", 0)] = swap(held[("handed", 0)], "section", 1)
    def kinds(*names):
        return [(name, other) for name in names for other in heads]

    for head in heads:
        held["far"] = (held[("near", head)] + outer_sum(head)).astype(BF16)
        sync(
            "far",
            "key_early",
            ("outward", head - 1),
            ("inner", head - 2),
            ("near", head),
            *([("relay", 1)] if head == 3 else []),
            "row_low",
            "row_high",
            *([("row_high", "first")] if head == 2 else []),
            *([("row_low", "second"), ("row_high", "second")] if head == 3 else []),
            *kinds("kv", "their"),
            *((("handed", head + 1),) if head > 0 else ()),
        )
        held[("outward", head)] = lax.ppermute(held["far"][:target_width], "dp", across)
        held[("inner", head)] = lax.ppermute(held["far"][target_width:], "dp", across)
        hand_in(head + 2)
        if head > 0:
            relay(head - 1)
        if head < last:
            if head == 0:
                grads = [held[("kv", other)] for other in heads]
                held["row_low"] = row_product(grads, key_weight, value_weight, 0, 2)
                if by_steps:
                    first_step("row_low", 1, 3)
                    held["row_high"] = row_product(grads, key_weight, value_weight, 1, 2)
                    first_step("row_high", 2, 3)
                sync(("outward", 0), ("handed", 1), *kinds("their"))
                held[("near", 1)] = chip_sum("chip_far", 1)
            held[("other", head + 1)] = swap(held[("handed", head + 1)], "section", 1)
            if head > 0:
                sync(
                    ("other", head + 1),
                    ("inner", head - 1),
                    ("relay", head - 2),
                    *([("row_low", "first")] if head == 1 else []),
                    *kinds("kv", "their"),
                )
                held[("near", head + 1)] = chip_sum("chip_far", head + 1)
        if head == 1:
            if by_steps:
                second_step("row_low", 2)
        if head == 2 and by_steps:
            second_step("row_high", 1)
    if not by_steps:
        held["row_low"] = row_product([held[("kv", head)] for head in heads], key_weight, value_weight, 0, 2)
        held["row_high"] = row_product([held[("kv", head)] for head in heads], key_weight, value_weight, 1, 2)
    sync(("relay", last - 1), *kinds("attended", "query"))
    for name in ("attended", "query"):
        held[name] = jnp.concatenate([held[(name, head)] for head in heads], axis=1)
    ends = ["attended", "query", *kinds("outward", "relay"), *(("inner", head) for head in heads[:-1])]
    sync(*ends, *kinds("kv", "their"))
    relay(last)
    for head in heads[:-1]:
        finish(head)
    row_share = jnp.concatenate([row_total("row_low"), row_total("row_high")], axis=1)
    row_grad = swap(row_share.astype(BF16), "section", 1)
    held["enc_grad"] = norm_backward(enc_rows, held["factor"], enc_gain, row_grad)
    sync(("relay", last), "enc_grad")
    finish(last)
    return (
        held["attended"][None],
        held["enc_grad"][None],
        held[("total", 0)],
        held[("total", 1)],
        held["query"][None],
    )


def solution(mesh):
    placed = (
        P(("section", "dp"), "seq", None),
        P(),
        P(None, "seq"),
        P(None, "seq"),
        P(("section", "dp"), None, "seq"),
        P(("section", "dp"), None, "seq"),
        P(),
    )
    return jax.shard_map(
        on_device,
        mesh=mesh,
        in_specs=placed,
        out_specs=(
            P(("section", "dp"), None, "seq"),
            P(("section", "dp"), "seq", None),
            P(("section", "dp"), "seq"),
            P(("section", "dp"), "seq"),
            P(("section", "dp"), None, "seq"),
        ),
        check_vma=False,
    )
```

```python
import functools

import jax
import jax.numpy as jnp
from jax import lax
from jax.experimental import pallas as pl
from jax.experimental.pallas import tpu as pltpu
from jax.sharding import PartitionSpec as P

HD = 256


EPS = 1e-06
NEG_FILL = -1e30
BF16 = jnp.bfloat16
F32 = jnp.float32
MIB = 1024 * 1024
FILLS_WAITS = pl.CostEstimate(flops=0, bytes_accessed=0, transcendentals=0)


def swap(value, axis, mask):
    pairs = [(source, source ^ mask) for source in range(lax.axis_size(axis))]
    return lax.ppermute(value, axis, pairs)


def normalize(enc_rows, gain):
    wide_rows = enc_rows.astype(F32)
    factor = lax.rsqrt(jnp.mean(wide_rows * wide_rows, axis=-1, keepdims=True) + EPS)
    return ((wide_rows * factor * gain).astype(BF16), factor)


def norm_backward(enc_rows, factor, gain, row_grad):
    wide_rows = enc_rows.astype(F32)
    scaled = row_grad.astype(F32) * gain
    inner_sum = jnp.mean(scaled * wide_rows, axis=-1, keepdims=True)
    return (factor * scaled - wide_rows * factor * factor * factor * inner_sum).astype(BF16)


def tie(*values):
    return lax.optimization_barrier(values)


def dot(left, right, left_dim, right_dim):
    return lax.dot_general(
        left, right, (((left_dim,), (right_dim,)), ((), ())), preferred_element_type=F32
    )


def in_order(early, middle, late):
    cut = early.shape[0] // 4 * 3
    return jnp.concatenate([early[:cut], middle[...], early[cut:], late[...]], axis=0)


def attend_kernel(visible, query, upstream, *refs):
    key_sets, value_sets, (attended, query_grad, kv_grad) = refs[:3], refs[3:6], refs[6:]
    score_scale = HD ** (-0.5)
    query_rows, upstream_rows = query[...], upstream[...]
    key_rows, value_rows = in_order(*key_sets), in_order(*value_sets)
    scores = dot(key_rows, query_rows, 1, 1) * score_scale
    scores = jnp.where(visible[...] > 0, scores, NEG_FILL)
    exponent = jnp.exp(scores - jnp.max(scores, axis=0, keepdims=True))
    probability = exponent * (1.0 / jnp.sum(exponent, axis=0, keepdims=True))
    prob_weights = probability.astype(BF16)
    grad_probs = dot(value_rows, upstream_rows, 1, 1)
    inner_sum = jnp.sum(probability * grad_probs, axis=0, keepdims=True)
    grad_scores = (probability * (grad_probs - inner_sum) * score_scale).astype(BF16)
    kv_grad[:, :HD] = dot(grad_scores, query_rows, 1, 0).astype(BF16)
    kv_grad[:, HD:] = dot(prob_weights, upstream_rows, 1, 0).astype(BF16)
    attended[...] = dot(prob_weights, value_rows, 0, 0).astype(BF16)
    query_grad[...] = dot(grad_scores, key_rows, 0, 0).astype(BF16)


def attend_head(head, visible, query, upstream, keys, values):
    src_rows, target_rows = visible.shape[0], query.shape[0]

    def column(rows):
        return pl.BlockSpec((rows, HD), lambda step: (0, head))

    def whole(rows, columns):
        return pl.BlockSpec((rows, columns), lambda step: (0, 0))

    return pl.pallas_call(
        attend_kernel,
        grid=(1,),
        in_specs=[
            whole(src_rows, 1),
            column(target_rows),
            column(target_rows),
        ]
        + [column(rows.shape[0]) for rows in (*keys, *values)],
        out_specs=[whole(target_rows, HD), whole(target_rows, HD), whole(src_rows, 2 * HD)],
        out_shape=[
            jax.ShapeDtypeStruct((target_rows, HD), BF16),
            jax.ShapeDtypeStruct((target_rows, HD), BF16),
            jax.ShapeDtypeStruct((src_rows, 2 * HD), BF16),
        ],
        compiler_params=pltpu.CompilerParams(vmem_limit_bytes=6 * MIB + 40 * src_rows * target_rows),
        cost_estimate=FILLS_WAITS,
    )(visible, query, upstream, *keys, *values)


def row_kernel(head_count, *refs):
    grads, (key_block, value_block), out = refs[:head_count], refs[head_count : head_count + 2], refs[-1]
    key_grads = jnp.concatenate([grad[:, :HD] for grad in grads], axis=1)
    value_grads = jnp.concatenate([grad[:, HD:] for grad in grads], axis=1)
    out[...] = (dot(key_grads, key_block[...], 1, 1) + dot(value_grads, value_block[...], 1, 1)).astype(BF16)


def row_product(grads, key_weight, value_weight, part, parts):
    rows, columns = grads[0].shape
    features, heads_width = key_weight.shape
    block = 512
    steps = features // block // parts
    first = part * steps
    whole = pl.BlockSpec((rows, columns), lambda step: (0, 0))
    weight = pl.BlockSpec((block, heads_width), lambda step: (first + step, 0))
    return pl.pallas_call(
        functools.partial(row_kernel, len(grads)),
        grid=(steps,),
        in_specs=[whole] * len(grads) + [weight, weight],
        out_specs=pl.BlockSpec((rows, block), lambda step: (0, step)),
        out_shape=jax.ShapeDtypeStruct((rows, features // parts), BF16),
        compiler_params=pltpu.CompilerParams(vmem_limit_bytes=14 * MIB + 12 * rows * block),
        cost_estimate=pl.CostEstimate(
            flops=4 * rows * features * heads_width // parts,
            bytes_accessed=(4 * features * heads_width + 2 * rows * (features + 2 * heads_width)) // parts,
            transcendentals=0,
        ),
    )(*grads, key_weight, value_weight)


def add_kernel(kind_count, local, first, second, *refs):
    outs = refs[-kind_count:]
    total = local[...] + first[...].astype(F32) + second[...].astype(F32)
    for slot, out in enumerate(outs):
        out[...] = total[:, slot * HD : (slot + 1) * HD]


def add_columns(totals, head, heads_here, local, first, second):
    rows, columns = local.shape
    here = pl.BlockSpec((rows, columns), lambda step: (0, 0))
    kept = [total for total in totals if total is not None]
    count = columns // HD
    return pl.pallas_call(
        functools.partial(add_kernel, count),
        grid=(1,),
        in_specs=[here] * 3 + [pl.BlockSpec(memory_space=pl.ANY)] * len(kept),
        out_specs=[pl.BlockSpec((rows, HD), lambda step: (0, head))] * count,
        out_shape=[jax.ShapeDtypeStruct((rows, heads_here * HD), F32)] * count,
        input_output_aliases={3 + slot: slot for slot in range(len(kept))},
        cost_estimate=pl.CostEstimate(
            flops=2 * rows * columns, bytes_accessed=12 * rows * columns, transcendentals=0
        ),
        compiler_params=pltpu.CompilerParams(vmem_limit_bytes=12 * MIB),
    )(local, first, second, *kept)


def on_device(enc_states, enc_gain, key_weight, value_weight, queries, out_grad, lengths):
    enc_rows = enc_states[0]
    own_rows, width = enc_rows.shape
    heads_here = key_weight.shape[1] // HD
    heads = range(heads_here)
    last = heads_here - 1
    section_count, dp_count, seq_count = (lax.axis_size(name) for name in ("section", "dp", "seq"))
    section, place, seq = (lax.axis_index(name) for name in ("section", "dp", "seq"))
    partner = (section * dp_count + place + dp_count) % (section_count * dp_count)
    src_rows = own_rows * seq_count
    section_width = width // section_count
    target_width = section_width // dp_count
    across = [(1, 2), (2, 1)]
    held = {}

    def sync(*names):
        names = ["factor"] + [name for name in names if name in held]
        held.update(zip(names, lax.optimization_barrier(tuple(held[name] for name in names))))

    def section_features(rows, index):
        return lax.dynamic_slice_in_dim(rows, index * section_width, section_width, axis=1)

    def target_features(rows, xors, base=0):
        return jnp.concatenate(
            [
                lax.dynamic_slice_in_dim(rows, base + (place ^ xor) * target_width, target_width, axis=1)
                for xor in xors
            ],
            axis=1,
        )

    def swap_both(rows, mask):
        count = section_count * seq_count
        pairs = [(source, source ^ (seq_count + mask)) for source in range(count)]
        return lax.ppermute(rows, ("section", "seq"), pairs)

    normed, held["factor"] = normalize(enc_rows, enc_gain)
    partner_rows = swap(normed, "section", 1)

    low, high = max(seq_count // 4, 1), max(seq_count // 2, 1)
    if low > 1:
        gathered = []
        for rows in (normed, partner_rows):
            blocks = [rows]
            bit = 1
            while bit < low:
                blocks = blocks + [swap(block, "seq", bit) for block in blocks]
                bit *= 2
            gathered.append(jnp.concatenate(blocks))
        normed, partner_rows = gathered
    half = normed.shape[0] // 2
    top, bottom = normed[:half], normed[half:]
    first_top, second_bottom = swap_both(top, low), swap_both(bottom, high)
    first_bottom, second_top = swap_both(bottom, low), swap_both(top, high)

    base = section * section_width
    outer_far = jnp.concatenate([target_features(rows, (3, 2), base) for rows in (partner_rows, normed)])
    outer_far = swap(outer_far, "dp", 1)

    def project(rows):
        return [
            jnp.dot(rows, weight, preferred_element_type=F32).astype(BF16) for weight in (key_weight, value_weight)
        ]

    first_top, second_bottom = tie(first_top, second_bottom)
    third_top, third_bottom = swap(first_top, "seq", high), swap(second_bottom, "seq", low)
    key_early, value_early = project(jnp.concatenate([partner_rows, first_top, second_bottom]))
    key_early, value_early, outer_far, first_bottom, second_top = tie(
        key_early, value_early, outer_far, first_bottom, second_top
    )
    key_middle, value_middle = project(jnp.concatenate([first_bottom, second_top]))
    key_middle, value_middle, third_top, third_bottom, outer_far = tie(
        key_middle, value_middle, third_top, third_bottom, outer_far
    )
    held["first"], held["second"] = swap(outer_far, "seq", low), swap(outer_far, "seq", high)
    gathered = [first_top, first_bottom, second_top, second_bottom, third_top, third_bottom]
    away = [section_features(rows, 1 - section) for rows in gathered]
    away = swap(jnp.concatenate(away), "section", 1)
    key_late, value_late = project(jnp.concatenate([third_top, third_bottom]))
    keys, values = (key_middle, key_late), (value_early, value_middle, value_late)

    block_start = (seq ^ jnp.arange(seq_count, dtype=jnp.int32)) * own_rows
    positions = block_start[:, None] + jnp.arange(own_rows, dtype=jnp.int32)[None, :]
    visible = (positions.reshape(src_rows, 1) < lengths[partner]).astype(jnp.int32)

    held["key_early"] = key_early

    def attend(head):
        held[("attended", head)], held[("query", head)], held[("kv", head)] = attend_head(
            head, visible, queries[0], out_grad[0], (held["key_early"], *keys), values
        )

    def hand_in(head):
        if head < heads_here:
            held[("handed", head)] = swap(held[("kv", head)], "dp", 1)

    def exchange(head):
        held[("their", head)] = swap(held[("kv", head)], "section", 1)

    attend(0)
    hand_in(0)
    exchange(0)
    chip_rows = jnp.concatenate(
        [section_features(rows, section) for rows in (partner_rows, *gathered, normed)] + [away]
    )
    held["chip_far"] = target_features(chip_rows, (2, 3))
    held["chip_pair"] = target_features(chip_rows, (1,))
    held["chip_own"] = target_features(chip_rows, (0,))
    sync("first", "second", "key_early", "chip_far", "chip_pair", "chip_own")
    quarter_rows = outer_far.shape[0] // 2
    held["top"] = swap(held["first"][:quarter_rows], "seq", high)
    held["bottom"] = swap(held["second"][quarter_rows:], "seq", low)
    for head in heads[1:]:
        attend(head)
        exchange(head)
    hand_in(1)
    early_pieces = [outer_far, held["first"], held["second"]]
    held["mine"] = jnp.concatenate([piece[:quarter_rows] for piece in early_pieces])
    held["yours"] = jnp.concatenate([piece[quarter_rows:] for piece in early_pieces])
    sync(
        ("handed", 0), ("their", 0), "top", "bottom", "mine", "yours",
        *(("kv", head) for head in heads),
    )

    def chip_sum(name, head):
        rows = held[name]
        return dot(rows[:src_rows], held[("kv", head)], 0, 0) + dot(rows[src_rows:], held[("their", head)], 0, 0)

    def outer_sum(head):
        handed, handed_other = held[("handed", head)], held[("other", head)]
        cut = 3 * quarter_rows
        return (
            dot(held["mine"], handed[:cut], 0, 0)
            + dot(held["yours"], handed_other[:cut], 0, 0)
            + dot(held["top"], handed[cut:], 0, 0)
            + dot(held["bottom"], handed_other[cut:], 0, 0)
        )

    by_steps = seq_count == 4 and heads_here == 4

    def row_block(name, step):
        return held[name][step * own_rows : (step + 1) * own_rows]

    def first_step(name, near, far):
        together = jnp.concatenate([row_block(name, near), row_block(name, far)])
        held[(name, "first")] = swap(together, "seq", near)

    def second_step(name, other):
        passed = row_block(name, other).astype(F32) + held[(name, "first")][own_rows:].astype(F32)
        held[(name, "second")] = swap(passed.astype(BF16), "seq", other)

    def row_total(name):
        total = row_block(name, 0).astype(F32)
        if by_steps:
            first, second = held[(name, "first")][:own_rows], held[(name, "second")]
            return total + first.astype(F32) + second.astype(F32)
        for step in range(1, seq_count):
            total = total + swap(row_block(name, step), "seq", step).astype(F32)
        return total

    def relay(head):
        term = chip_sum("chip_pair", head) + held[("outward", head)].astype(F32)
        held[("relay", head)] = swap(term.astype(BF16), "dp", 1)

    def finish(head):
        totals = [held.get(("total", kind)) for kind in (0, 1)]
        held[("total", 0)], held[("total", 1)] = add_columns(
            totals, head, heads_here, chip_sum("chip_own", head), held[("inner", head)], held[("relay", head)]
        )

    held[("near", 0)] = chip_sum("chip_far", 0)
    held[("other", 0)] = swap(held[("handed", 0)], "section", 1)
    def kinds(*names):
        return [(name, other) for name in names for other in heads]

    for head in heads:
        held["far"] = (held[("near", head)] + outer_sum(head)).astype(BF16)
        sync(
            "far",
            "key_early",
            ("outward", head - 1),
            ("inner", head - 2),
            ("near", head),
            *([("relay", 1)] if head == 3 else []),
            "row_low",
            "row_high",
            *([("row_high", "first")] if head == 2 else []),
            *([("row_low", "second"), ("row_high", "second")] if head == 3 else []),
            *kinds("kv", "their"),
            *((("handed", head + 1),) if head > 0 else ()),
        )
        held[("outward", head)] = lax.ppermute(held["far"][:target_width], "dp", across)
        held[("inner", head)] = lax.ppermute(held["far"][target_width:], "dp", across)
        hand_in(head + 2)
        if head > 0:
            relay(head - 1)
        if head < last:
            if head == 0:
                grads = [held[("kv", other)] for other in heads]
                held["row_low"] = row_product(grads, key_weight, value_weight, 0, 2)
                if by_steps:
                    first_step("row_low", 1, 3)
                    held["row_high"] = row_product(grads, key_weight, value_weight, 1, 2)
                    first_step("row_high", 2, 3)
                sync(("outward", 0), ("handed", 1), *kinds("their"))
                held[("near", 1)] = chip_sum("chip_far", 1)
            held[("other", head + 1)] = swap(held[("handed", head + 1)], "section", 1)
            if head > 0:
                sync(
                    ("other", head + 1),
                    ("inner", head - 1),
                    ("relay", head - 2),
                    *([("row_low", "first")] if head == 1 else []),
                    *kinds("kv", "their"),
                )
                held[("near", head + 1)] = chip_sum("chip_far", head + 1)
        if head == 1:
            if by_steps:
                second_step("row_low", 2)
        if head == 2 and by_steps:
            second_step("row_high", 1)
    if not by_steps:
        held["row_low"] = row_product([held[("kv", head)] for head in heads], key_weight, value_weight, 0, 2)
        held["row_high"] = row_product([held[("kv", head)] for head in heads], key_weight, value_weight, 1, 2)
    sync(("relay", last - 1), *kinds("attended", "query"))
    for name in ("attended", "query"):
        held[name] = jnp.concatenate([held[(name, head)] for head in heads], axis=1)
    ends = ["attended", "query", *kinds("outward", "relay"), *(("inner", head) for head in heads[:-1])]
    sync(*ends, *kinds("kv", "their"))
    relay(last)
    for head in heads[:-1]:
        finish(head)
    row_share = jnp.concatenate([row_total("row_low"), row_total("row_high")], axis=1)
    row_grad = swap(row_share.astype(BF16), "section", 1)
    held["enc_grad"] = norm_backward(enc_rows, held["factor"], enc_gain, row_grad)
    sync(("relay", last), "enc_grad")
    finish(last)
    return (
        held["attended"][None],
        held["enc_grad"][None],
        held[("total", 0)],
        held[("total", 1)],
        held["query"][None],
    )


def solution(mesh):
    placed = (
        P(("section", "dp"), "seq", None),
        P(),
        P(None, "seq"),
        P(None, "seq"),
        P(("section", "dp"), None, "seq"),
        P(("section", "dp"), None, "seq"),
        P(),
    )
    return jax.shard_map(
        on_device,
        mesh=mesh,
        in_specs=placed,
        out_specs=(
            P(("section", "dp"), None, "seq"),
            P(("section", "dp"), "seq", None),
            P(("section", "dp"), "seq"),
            P(("section", "dp"), "seq"),
            P(("section", "dp"), None, "seq"),
        ),
        check_vma=False,
    )
```
